32 devices in a mesh: narrow: 1, wide: 32 (over z, y, x, core).
Axes of the slice: x: 2, y: 2, z: 4, core: 2. Of those that a mesh axis runs over, the one named last changes fastest.
Arguments:
- pair_act: float32 [256, 256, 128], P('narrow', 'wide'), may hold values from -6 to 6
- block_mask: int32 [4, 4], replicated, may hold values from 0 to 1, as said below
- left_weight: bfloat16 [128, 256], replicated, may hold values from -0.5 to 0.5
- right_weight: bfloat16 [128, 256], replicated, may hold values from -0.5 to 0.5
- gate_weight: bfloat16 [128, 128], replicated, may hold values from -0.5 to 0.5
- out_weight: bfloat16 [128, 128], replicated, may hold values from -0.5 to 0.5
Outputs:
- update: float32 [256, 256, 128], P('narrow', 'wide')
The draws below stay inside these ranges and needn't reach their ends.
Inputs may be any that keep to these rules, and one draw needn't show every extreme that they name: `block_mask`: 0 or 1, symmetric; tokens are grouped into up to 4 chains of whole blocks in order, the first chain covering more than half of the blocks; every diagonal block is 1, and all blocks of one pair of chains share a value.
All inputs are finite; a program needn't handle non-finite values.
Results may differ from the reference program's by a relative error of at most 0.008.
Values may be sent and summed in bfloat16 or wider, within the bound.
No kernel may reach another device: no remote copies, remote signals or barrier semaphores. Data moves between devices by JAX's collectives and lax.ppermute only.
A program may use at most 64 MiB of HBM per device.

```python
import jax
import jax.numpy as jnp
from jax import lax

C = 128
BLOCK = 64
TOKENS = 256
BLOCKS = 4


def draw_block_mask(key, part):
    first_key, second_key, third_key = jax.random.split(jax.random.fold_in(key, 17), 3)
    first_cut = jax.random.randint(first_key, (1,), BLOCKS // 2 + 1, BLOCKS)
    later_cuts = jax.random.randint(third_key, (2,), first_cut[0], BLOCKS + 1)
    cuts = jnp.concatenate([first_cut, later_cuts])
    block_ids = jnp.arange(BLOCKS, dtype=jnp.int32)
    chain_ids = jnp.sum((block_ids[:, None] >= cuts[None, :]).astype(jnp.int32), axis=1)
    draws = jax.random.randint(second_key, (4, 4), 0, 5)
    upper_ids = jnp.arange(4, dtype=jnp.int32)
    symmetric = jnp.where(upper_ids[:, None] <= upper_ids[None, :], draws, draws.T)
    keep_table = jnp.maximum((symmetric < 2).astype(jnp.int32), jnp.eye(4, dtype=jnp.int32))
    chain_hot = (chain_ids[:, None] == upper_ids[None, :]).astype(jnp.int32)
    return jnp.dot(jnp.dot(chain_hot, keep_table), chain_hot.T)


def block_scale(rng, extent, cuts, smallest, top_value):
    gain, own = 1.0, jax.random.fold_in(rng, 6)
    for dim, blocks in cuts:
        heights = jnp.exp(jax.random.uniform(jax.random.fold_in(own, dim), (blocks,), jnp.float32, smallest / len(cuts), top_value / len(cuts)))
        gain = gain * jnp.repeat(heights, extent[dim] // blocks).reshape([-1 if axis == dim else 1 for axis in range(len(extent))])
    return gain


def centred(stream_key, extent, width, limit, cuts=(), kind=jnp.bfloat16):
    array = width * jax.random.normal(stream_key, extent, jnp.float32)
    if cuts:
        array = array * block_scale(stream_key, extent, cuts, -0.22, 0.18)
    return jnp.clip(array, -limit, limit).astype(kind)


def setup_inputs(seed: int = 0) -> dict:
    keys = jax.random.split(jax.random.key(seed), 7)
    return {
        "pair_act": centred(keys[0], (TOKENS, TOKENS, C), 1.0, 6.0, ((1, 32),), jnp.float32),
        "block_mask": draw_block_mask(jax.random.fold_in(keys[6], 71), 0),
        "left_weight": centred(keys[2], (C, 2 * C), C ** -0.5, 0.5),
        "right_weight": centred(keys[3], (C, 2 * C), C ** -0.5, 0.5),
        "gate_weight": centred(keys[4], (C, C), C ** -0.5, 0.5),
        "out_weight": centred(keys[5], (C, C), C ** -0.5, 0.5),
    }


def layer_norm(values):
    centre = lax.optimization_barrier(jnp.mean(values, axis=-1, keepdims=True))
    spread = lax.optimization_barrier(jnp.mean(jnp.square(values - centre), axis=-1, keepdims=True))
    return (values - centre) * jax.lax.rsqrt(spread + 1e-05)

def gated_projection(normed, weight, channels):
    mixed_proj = jnp.dot(normed, weight, preferred_element_type=jnp.float32)
    return jax.nn.sigmoid(mixed_proj[:, :channels]) * mixed_proj[:, channels:]

def reference(pair_act, block_mask, left_weight, right_weight, gate_weight, out_weight):
    token_mask = jnp.repeat(jnp.repeat(block_mask, BLOCK, axis=0), BLOCK, axis=1).astype(jnp.float32)
    normed = layer_norm(pair_act).astype(jnp.bfloat16).reshape(TOKENS * TOKENS, C)
    left_proj = (gated_projection(normed, left_weight, C).reshape(TOKENS, TOKENS, C) * token_mask[:, :, None]).astype(jnp.bfloat16)
    right_proj = (gated_projection(normed, right_weight, C).reshape(TOKENS, TOKENS, C) * token_mask[:, :, None]).astype(jnp.bfloat16)
    gate_act = jax.nn.sigmoid(jnp.dot(normed, gate_weight, preferred_element_type=jnp.float32))
    tri_sum = jnp.einsum('ikc,jkc->ijc', left_proj.astype(jnp.float32), right_proj.astype(jnp.float32))
    tri_normed = layer_norm(tri_sum).astype(jnp.bfloat16).reshape(TOKENS * TOKENS, C)
    update = gate_act * jnp.dot(tri_normed, out_weight, preferred_element_type=jnp.float32)
    return update.reshape(TOKENS, TOKENS, C)
```

```python
import jax
import jax.numpy as jnp
from jax import lax
from jax.sharding import PartitionSpec as P

C = 128
BLOCK = 64


def on_device(pair_act, block_mask, left_weight, right_weight, gate_weight, out_weight):
    tile_rows = pair_act.shape[0]
    tile_cols = pair_act.shape[1]
    wide = lax.axis_size("wide")
    narrow = lax.axis_size("narrow")
    per_device = C // wide
    row_ids = lax.axis_index("narrow") * tile_rows + jnp.arange(tile_rows, dtype=jnp.int32)
    col_ids = lax.axis_index("wide") * tile_cols + jnp.arange(tile_cols, dtype=jnp.int32)
    block_ids = jnp.arange(block_mask.shape[0], dtype=jnp.int32)
    row_hot = (row_ids[:, None] // BLOCK == block_ids[None, :]).astype(jnp.float32)
    col_hot = (col_ids[:, None] // BLOCK == block_ids[None, :]).astype(jnp.float32)
    tile_mask = jnp.dot(jnp.dot(row_hot, block_mask.astype(jnp.float32)), col_hot.T).T

    centre = jnp.mean(pair_act, axis=-1, keepdims=True)
    spread = jnp.mean(jnp.square(pair_act - centre), axis=-1, keepdims=True)
    normed = ((pair_act - centre) * lax.rsqrt(spread + 1e-05)).astype(jnp.bfloat16)

    def edges(weight):
        mixed = jnp.einsum("cd,ikc->dki", weight, normed, preferred_element_type=jnp.float32)
        proj = jax.nn.sigmoid(mixed[:C]) * mixed[C:] * tile_mask[None]
        return proj.astype(jnp.bfloat16).reshape(wide, per_device, tile_cols, tile_rows)

    send = jnp.stack([edges(left_weight), edges(right_weight)], axis=1)
    recv = lax.all_to_all(send, "wide", split_axis=0, concat_axis=0, tiled=True)
    left, right = recv[:, 0], recv[:, 1]
    if narrow > 1:
        right = lax.all_gather(right, "narrow", axis=3, tiled=True)
    tri = jnp.einsum("sckj,scki->cji", right, left, preferred_element_type=jnp.float32)
    back = tri.astype(jnp.bfloat16).reshape(per_device, wide, tile_cols, tile_rows)
    back = jnp.transpose(back, (1, 0, 2, 3))
    tri = lax.all_to_all(back, "wide", split_axis=0, concat_axis=0, tiled=True)
    tri = tri.reshape(C, tile_cols, tile_rows).astype(jnp.float32)
    centre = jnp.mean(tri, axis=0, keepdims=True)
    spread = jnp.mean(jnp.square(tri - centre), axis=0, keepdims=True)
    tri_normed = ((tri - centre) * lax.rsqrt(spread + 1e-05)).astype(jnp.bfloat16)
    gate = jax.nn.sigmoid(
        jnp.einsum("ikc,cd->ikd", normed, gate_weight, preferred_element_type=jnp.float32)
    )
    return gate * jnp.einsum(
        "cji,cd->ijd", tri_normed, out_weight, preferred_element_type=jnp.float32
    )


def solution(mesh):
    return jax.shard_map(
        on_device,
        mesh=mesh,
        in_specs=(P("narrow", "wide", None), P(), P(), P(), P(), P()),
        out_specs=P("narrow", "wide", None),
        check_vma=False,
    )
```

```python
import functools

import jax
import jax.numpy as jnp
from jax import lax
from jax.experimental import pallas as pl
from jax.experimental.pallas import tpu as pltpu
from jax.sharding import PartitionSpec as P

C = 128
BLOCK = 64
LANES = 128
SUB = 8


def layer_norm(values, axis):
    centre = jnp.mean(values, axis=axis, keepdims=True)
    spread = jnp.mean(jnp.square(values - centre), axis=axis, keepdims=True)
    return (values - centre) * lax.rsqrt(spread + 1e-05)


def project_kernel(mask_ref, x_ref, wl_ref, wr_ref, send_ref, normed_ref, edge):
    rows = x_ref.shape[0] // SUB
    wide = send_ref.shape[0]
    halves = rows // LANES
    column_block = lax.axis_index("wide") * SUB // BLOCK
    row_block = lax.broadcasted_iota(jnp.int32, (1, rows), 1) // BLOCK
    mask = jnp.zeros((1, rows), jnp.float32)
    for block in range(mask_ref.shape[0]):
        kept = mask_ref[block, column_block].astype(jnp.float32)
        mask = jnp.where(row_block == block, kept, mask)
    weights = jnp.concatenate([wl_ref[...].T, wr_ref[...].T], axis=0)
    for k in range(SUB):
        x = x_ref[pl.ds(k, rows, stride=SUB), :]
        normed = layer_norm(x, 1).astype(jnp.bfloat16)
        normed_ref[k] = normed
        mixed = lax.dot_general(
            weights, normed, (((1,), (1,)), ((), ())), preferred_element_type=jnp.float32
        )
        for side in range(2):
            gate = mixed[2 * side * C : (2 * side + 1) * C]
            value = mixed[(2 * side + 1) * C : (2 * side + 2) * C]
            proj = jax.nn.sigmoid(gate) * value * mask
            for half in range(halves):
                edge[side, half, pl.ds(k, C, stride=SUB), :] = proj[:, half * LANES : (half + 1) * LANES]
    part = C // wide * SUB
    for side in range(2):
        for half in range(halves):
            start = (side * halves + half) * part
            send_ref[:, start : start + part, :] = (
                edge[side, half].reshape(wide, part, LANES).astype(jnp.bfloat16)
            )


def triangle_kernel(recv_ref, send_ref):
    wide = recv_ref.shape[0]
    per_device = C // wide
    part = per_device * SUB
    halves = send_ref.shape[1] // part
    tokens = wide * SUB

    def load(side, channel):
        parts = []
        for half in range(halves):
            start = (side * halves + half) * part + channel * SUB
            pair = recv_ref[:, start : start + 2 * SUB, :].astype(jnp.float32)
            parts.append([
                pair[:, low : low + SUB].reshape(tokens, LANES).astype(jnp.bfloat16)
                for low in (0, SUB)
            ])
        return [jnp.concatenate([p[n] for p in parts], axis=1) for n in range(2)]

    for channel in range(0, per_device, 2):
        left, right = load(0, channel), load(1, channel)
        sums = [
            lax.dot_general(
                right[n], left[n], (((0,), (0,)), ((), ())), preferred_element_type=jnp.float32
            )
            for n in range(2)
        ]
        for half in range(halves):
            pair = jnp.concatenate(
                [s[:, half * LANES : (half + 1) * LANES].reshape(wide, SUB, LANES) for s in sums],
                axis=1,
            )
            start = half * part + channel * SUB
            send_ref[:, start : start + 2 * SUB, :] = pair.astype(jnp.bfloat16)


def update_kernel(recv_ref, normed_ref, wg_ref, wo_ref, out_ref, tri):
    wide = recv_ref.shape[0]
    part = C // wide * SUB
    halves = recv_ref.shape[1] // part
    for half in range(halves):
        sums = recv_ref[:, half * part : (half + 1) * part, :].astype(jnp.float32)
        tri[half] = layer_norm(sums.reshape(C, SUB, LANES), 0).reshape(C * SUB, LANES)
    for j in range(SUB):
        for half in range(halves):
            tri_normed = tri[half, pl.ds(j, C, stride=SUB), :].astype(jnp.bfloat16)
            mixed = lax.dot_general(
                tri_normed, wo_ref[...], (((0,), (0,)), ((), ())), preferred_element_type=jnp.float32
            )
            normed = normed_ref[j, half * LANES : (half + 1) * LANES, :]
            gate = jax.nn.sigmoid(
                jnp.dot(normed, wg_ref[...], preferred_element_type=jnp.float32)
            )
            out_ref[pl.ds(half * LANES * SUB + j, LANES, stride=SUB), :] = gate * mixed


VMEM = pl.BlockSpec(memory_space=pltpu.VMEM)
SMEM = pl.BlockSpec(memory_space=pltpu.SMEM)
PARAMS = pltpu.CompilerParams(vmem_limit_bytes=48 * 1024 * 1024)


def kernels_on_device(pair_act, block_mask, left_weight, right_weight, gate_weight, out_weight):
    rows = pair_act.shape[0]
    wide = lax.axis_size("wide")
    halves = rows // LANES
    part = C // wide * SUB
    exchange = functools.partial(
        lax.all_to_all, axis_name="wide", split_axis=0, concat_axis=0, tiled=True
    )
    send, normed = pl.pallas_call(
        project_kernel,
        out_shape=(
            jax.ShapeDtypeStruct((wide, 2 * halves * part, LANES), jnp.bfloat16),
            jax.ShapeDtypeStruct((SUB, rows, C), jnp.bfloat16),
        ),
        in_specs=[SMEM, VMEM, VMEM, VMEM],
        out_specs=(VMEM, VMEM),
        scratch_shapes=[pltpu.VMEM((2, halves, C * SUB, LANES), jnp.float32)],
        compiler_params=PARAMS,
        name="project",
    )(block_mask, pair_act.reshape(rows * SUB, C), left_weight, right_weight)
    back = pl.pallas_call(
        triangle_kernel,
        out_shape=jax.ShapeDtypeStruct((wide, halves * part, LANES), jnp.bfloat16),
        in_specs=[VMEM],
        out_specs=VMEM,
        compiler_params=PARAMS,
        name="triangle",
    )(exchange(send))
    update = pl.pallas_call(
        update_kernel,
        out_shape=jax.ShapeDtypeStruct((rows * SUB, C), jnp.float32),
        in_specs=[VMEM] * 4,
        out_specs=VMEM,
        scratch_shapes=[pltpu.VMEM((halves, C * SUB, LANES), jnp.float32)],
        compiler_params=PARAMS,
        name="update",
    )(exchange(back), normed, gate_weight, out_weight)
    return update.reshape(rows, SUB, C)


def plain_on_device(pair_act, block_mask, left_weight, right_weight, gate_weight, out_weight):
    tile_rows = pair_act.shape[0]
    tile_cols = pair_act.shape[1]
    wide = lax.axis_size("wide")
    narrow = lax.axis_size("narrow")
    per_device = C // wide
    row_ids = lax.axis_index("narrow") * tile_rows + jnp.arange(tile_rows, dtype=jnp.int32)
    col_ids = lax.axis_index("wide") * tile_cols + jnp.arange(tile_cols, dtype=jnp.int32)
    block_ids = jnp.arange(block_mask.shape[0], dtype=jnp.int32)
    row_hot = (row_ids[:, None] // BLOCK == block_ids[None, :]).astype(jnp.float32)
    col_hot = (col_ids[:, None] // BLOCK == block_ids[None, :]).astype(jnp.float32)
    tile_mask = jnp.dot(jnp.dot(row_hot, block_mask.astype(jnp.float32)), col_hot.T).T
    normed = layer_norm(pair_act, -1).astype(jnp.bfloat16)

    def edges(weight):
        mixed = jnp.einsum("cd,ikc->dki", weight, normed, preferred_element_type=jnp.float32)
        proj = jax.nn.sigmoid(mixed[:C]) * mixed[C:] * tile_mask[None]
        return proj.astype(jnp.bfloat16).reshape(wide, per_device, tile_cols, tile_rows)

    send = jnp.stack([edges(left_weight), edges(right_weight)], axis=1)
    recv = lax.all_to_all(send, "wide", split_axis=0, concat_axis=0, tiled=True)
    left, right = recv[:, 0], recv[:, 1]
    if narrow > 1:
        right = lax.all_gather(right, "narrow", axis=3, tiled=True)
    tri = jnp.einsum("sckj,scki->cji", right, left, preferred_element_type=jnp.float32)
    back = tri.astype(jnp.bfloat16).reshape(per_device, wide, tile_cols, tile_rows)
    back = jnp.transpose(back, (1, 0, 2, 3))
    tri = lax.all_to_all(back, "wide", split_axis=0, concat_axis=0, tiled=True)
    tri = tri.reshape(C, tile_cols, tile_rows).astype(jnp.float32)
    tri_normed = layer_norm(tri, 0).astype(jnp.bfloat16)
    gate = jax.nn.sigmoid(
        jnp.einsum("ikc,cd->ikd", normed, gate_weight, preferred_element_type=jnp.float32)
    )
    return gate * jnp.einsum(
        "cji,cd->ijd", tri_normed, out_weight, preferred_element_type=jnp.float32
    )


def on_device(pair_act, *rest):
    rows, cols = pair_act.shape[:2]
    fits = rows % LANES == 0 and cols == SUB and C // lax.axis_size("wide") % 2 == 0
    if lax.axis_size("narrow") == 1 and fits:
        return kernels_on_device(pair_act, *rest)
    return plain_on_device(pair_act, *rest)


def solution(mesh):
    return jax.shard_map(
        on_device,
        mesh=mesh,
        in_specs=(P("narrow", "wide", None), P(), P(), P(), P(), P()),
        out_specs=P("narrow", "wide", None),
        check_vma=False,
    )
```

```python
import functools

import jax
import jax.numpy as jnp
from jax import lax
from jax.experimental import pallas as pl
from jax.experimental.pallas import tpu as pltpu
from jax.sharding import PartitionSpec as P

C = 128
BLOCK = 64
LANES = 128
SUB = 8


def layer_norm(values, axis):
    centre = jnp.mean(values, axis=axis, keepdims=True)
    spread = jnp.mean(jnp.square(values - centre), axis=axis, keepdims=True)
    return (values - centre) * lax.rsqrt(spread + 1e-05)


def project_kernel(mask_ref, x_hbm, wl_hbm, wr_hbm, *refs):
    *send_refs, normed_ref, x_ref, w_ref, edge, sems = refs
    copies = [
        pltpu.make_async_copy(wl_hbm, w_ref.at[0], sems.at[0]),
        pltpu.make_async_copy(wr_hbm, w_ref.at[1], sems.at[1]),
        pltpu.make_async_copy(x_hbm, x_ref, sems.at[2]),
    ]
    for copy in copies:
        copy.start()
    rows = x_ref.shape[0] // SUB
    wide = len(send_refs)
    halves = rows // LANES
    me = lax.axis_index("wide")
    column_block = me * SUB // BLOCK
    row_block = lax.broadcasted_iota(jnp.int32, (1, rows), 1) // BLOCK
    mask = jnp.zeros((1, rows), jnp.float32)
    for block in range(mask_ref.shape[0]):
        kept = mask_ref[block, column_block].astype(jnp.float32)
        mask = jnp.where(row_block == block, kept, mask)
    copies[0].wait()
    copies[1].wait()
    weights = jnp.concatenate([w_ref[0].T, w_ref[1].T], axis=0)
    copies[2].wait()
    for k in range(SUB):
        x = x_ref[pl.ds(k, rows, stride=SUB), :]
        normed = layer_norm(x, 1).astype(jnp.bfloat16)
        normed_ref[k] = normed
        mixed = lax.dot_general(
            weights, normed, (((1,), (1,)), ((), ())), preferred_element_type=jnp.float32
        )
        for side in range(2):
            gate = mixed[2 * side * C : (2 * side + 1) * C]
            value = mixed[(2 * side + 1) * C : (2 * side + 2) * C]
            proj = jax.nn.sigmoid(gate) * value * mask
            for half in range(halves):
                edge[side, half, pl.ds(k, C, stride=SUB), :] = proj[:, half * LANES : (half + 1) * LANES]
    part = C // wide * SUB
    for slot, send_ref in enumerate(send_refs):
        start = pl.multiple_of((me ^ slot) * part, part)
        for side in range(2):
            for half in range(halves):
                low = (side * halves + half) * part
                send_ref[low : low + part, :] = edge[side, half, pl.ds(start, part), :].astype(jnp.bfloat16)


def triangle_kernel(wide, *refs):
    recv_refs, send_refs, total = refs[:wide], refs[wide : 2 * wide], refs[2 * wide]
    per_device = C // wide
    part = per_device * SUB
    halves = send_refs[0].shape[0] // part
    me = lax.axis_index("wide")

    def load(side, channel):
        parts = []
        for half in range(halves):
            start = (side * halves + half) * part + channel * SUB
            pairs = [r[start : start + 2 * SUB, :].astype(jnp.float32) for r in recv_refs]
            parts.append([
                jnp.concatenate([p[low : low + SUB] for p in pairs], axis=0).astype(jnp.bfloat16)
                for low in (0, SUB)
            ])
        return [jnp.concatenate([p[n] for p in parts], axis=1) for n in range(2)]

    for channel in range(0, per_device, 2):
        left, right = load(0, channel), load(1, channel)
        for n in range(2):
            sums = lax.dot_general(
                right[n], left[n], (((0,), (0,)), ((), ())), preferred_element_type=jnp.float32
            )
            for half in range(halves):
                total[half, channel + n] = sums[:, half * LANES : (half + 1) * LANES]
    for slot, send_ref in enumerate(send_refs):
        start = pl.multiple_of((me ^ slot) * SUB, SUB)
        for half in range(halves):
            chunk = total[half, :, pl.ds(start, SUB), :].reshape(part, LANES)
            send_ref[half * part : (half + 1) * part, :] = chunk.astype(jnp.bfloat16)


def update_kernel(wide, *refs):
    recv_refs = refs[:wide]
    normed_ref, wg_ref, wo_ref, out_ref, tri = refs[wide:]
    part = C // wide * SUB
    halves = recv_refs[0].shape[0] // part
    me = lax.axis_index("wide")
    for slot, recv_ref in enumerate(recv_refs):
        start = pl.multiple_of((me ^ slot) * part, part)
        for half in range(halves):
            sums = recv_ref[half * part : (half + 1) * part, :].astype(jnp.float32)
            tri[half, pl.ds(start, part), :] = sums
    for half in range(halves):
        sums = tri[half].reshape(C, SUB, LANES)
        tri[half] = layer_norm(sums, 0).reshape(C * SUB, LANES)
    for j in range(SUB):
        for half in range(halves):
            tri_normed = tri[half, pl.ds(j, C, stride=SUB), :].astype(jnp.bfloat16)
            mixed = lax.dot_general(
                tri_normed, wo_ref[...], (((0,), (0,)), ((), ())), preferred_element_type=jnp.float32
            )
            normed = normed_ref[j, half * LANES : (half + 1) * LANES, :]
            gate = jax.nn.sigmoid(
                jnp.dot(normed, wg_ref[...], preferred_element_type=jnp.float32)
            )
            out_ref[pl.ds(half * LANES * SUB + j, LANES, stride=SUB), :] = gate * mixed


ANY = pl.BlockSpec(memory_space=pl.ANY)
VMEM = pl.BlockSpec(memory_space=pltpu.VMEM)
SMEM = pl.BlockSpec(memory_space=pltpu.SMEM)
PARAMS = pltpu.CompilerParams(vmem_limit_bytes=48 * 1024 * 1024)


def exchange(slots):
    wide = len(slots)
    received = {0: slots[0]}
    for slot in range(wide - 1, 0, -1):
        pairs = [(device, device ^ slot) for device in range(wide)]
        received[slot] = lax.ppermute(slots[slot], "wide", pairs)
    return [received[slot] for slot in range(wide)]


def kernels_on_device(pair_act, block_mask, left_weight, right_weight, gate_weight, out_weight):
    rows = pair_act.shape[0]
    wide = lax.axis_size("wide")
    halves = rows // LANES
    part = C // wide * SUB
    *send, normed = pl.pallas_call(
        project_kernel,
        out_shape=[jax.ShapeDtypeStruct((2 * halves * part, LANES), jnp.bfloat16)] * wide
        + [jax.ShapeDtypeStruct((SUB, rows, C), jnp.bfloat16)],
        in_specs=[SMEM, ANY, ANY, ANY],
        out_specs=[VMEM] * (wide + 1),
        scratch_shapes=[
            pltpu.VMEM((rows * SUB, C), jnp.float32),
            pltpu.VMEM((2, C, 2 * C), jnp.bfloat16),
            pltpu.VMEM((2, halves, C * SUB, LANES), jnp.float32),
            pltpu.SemaphoreType.DMA((3,)),
        ],
        compiler_params=PARAMS,
        name="project",
    )(block_mask, pair_act.reshape(rows * SUB, C), left_weight, right_weight)
    back = pl.pallas_call(
        functools.partial(triangle_kernel, wide),
        out_shape=[jax.ShapeDtypeStruct((halves * part, LANES), jnp.bfloat16)] * wide,
        in_specs=[VMEM] * wide,
        out_specs=[VMEM] * wide,
        scratch_shapes=[pltpu.VMEM((halves, C // wide, wide * SUB, LANES), jnp.float32)],
        compiler_params=PARAMS,
        name="triangle",
    )(*exchange(send))
    update = pl.pallas_call(
        functools.partial(update_kernel, wide),
        out_shape=jax.ShapeDtypeStruct((rows * SUB, C), jnp.float32),
        in_specs=[VMEM] * (wide + 3),
        out_specs=VMEM,
        scratch_shapes=[pltpu.VMEM((halves, C * SUB, LANES), jnp.float32)],
        compiler_params=PARAMS,
        name="update",
    )(*exchange(back), normed, gate_weight, out_weight)
    return update.reshape(rows, SUB, C)


def plain_on_device(pair_act, block_mask, left_weight, right_weight, gate_weight, out_weight):
    tile_rows = pair_act.shape[0]
    tile_cols = pair_act.shape[1]
    wide = lax.axis_size("wide")
    narrow = lax.axis_size("narrow")
    per_device = C // wide
    row_ids = lax.axis_index("narrow") * tile_rows + jnp.arange(tile_rows, dtype=jnp.int32)
    col_ids = lax.axis_index("wide") * tile_cols + jnp.arange(tile_cols, dtype=jnp.int32)
    block_ids = jnp.arange(block_mask.shape[0], dtype=jnp.int32)
    row_hot = (row_ids[:, None] // BLOCK == block_ids[None, :]).astype(jnp.float32)
    col_hot = (col_ids[:, None] // BLOCK == block_ids[None, :]).astype(jnp.float32)
    tile_mask = jnp.dot(jnp.dot(row_hot, block_mask.astype(jnp.float32)), col_hot.T).T
    normed = layer_norm(pair_act, -1).astype(jnp.bfloat16)

    def edges(weight):
        mixed = jnp.einsum("cd,ikc->dki", weight, normed, preferred_element_type=jnp.float32)
        proj = jax.nn.sigmoid(mixed[:C]) * mixed[C:] * tile_mask[None]
        return proj.astype(jnp.bfloat16).reshape(wide, per_device, tile_cols, tile_rows)

    send = jnp.stack([edges(left_weight), edges(right_weight)], axis=1)
    recv = lax.all_to_all(send, "wide", split_axis=0, concat_axis=0, tiled=True)
    left, right = recv[:, 0], recv[:, 1]
    if narrow > 1:
        right = lax.all_gather(right, "narrow", axis=3, tiled=True)
    tri = jnp.einsum("sckj,scki->cji", right, left, preferred_element_type=jnp.float32)
    back = tri.astype(jnp.bfloat16).reshape(per_device, wide, tile_cols, tile_rows)
    back = jnp.transpose(back, (1, 0, 2, 3))
    tri = lax.all_to_all(back, "wide", split_axis=0, concat_axis=0, tiled=True)
    tri = tri.reshape(C, tile_cols, tile_rows).astype(jnp.float32)
    tri_normed = layer_norm(tri, 0).astype(jnp.bfloat16)
    gate = jax.nn.sigmoid(
        jnp.einsum("ikc,cd->ikd", normed, gate_weight, preferred_element_type=jnp.float32)
    )
    return gate * jnp.einsum(
        "cji,cd->ijd", tri_normed, out_weight, preferred_element_type=jnp.float32
    )


def on_device(pair_act, *rest):
    rows, cols = pair_act.shape[:2]
    wide = lax.axis_size("wide")
    fits = rows % LANES == 0 and rows == wide * SUB and cols == SUB and C % (2 * wide) == 0
    if lax.axis_size("narrow") == 1 and fits:
        return kernels_on_device(pair_act, *rest)
    return plain_on_device(pair_act, *rest)


def solution(mesh):
    return jax.shard_map(
        on_device,
        mesh=mesh,
        in_specs=(P("narrow", "wide", None), P(), P(), P(), P(), P()),
        out_specs=P("narrow", "wide", None),
        check_vma=False,
    )
```

```python
import functools

import jax
import jax.numpy as jnp
from jax import lax
from jax.experimental import pallas as pl
from jax.experimental.pallas import tpu as pltpu
from jax.sharding import PartitionSpec as P

C = 128
BLOCK = 64
LANES = 128
SUB = 8


def layer_norm(values, axis):
    centre = jnp.mean(values, axis=axis, keepdims=True)
    spread = jnp.mean(jnp.square(values - centre), axis=axis, keepdims=True)
    return (values - centre) * lax.rsqrt(spread + 1e-05)


def swap_halves(values):
    flat = values.reshape(-1, LANES)
    return pltpu.roll(flat, LANES // 2, 1).reshape(values.shape)


def pack(low, high):
    lane = lax.broadcasted_iota(jnp.int32, low.shape, low.ndim - 1)
    return jnp.where(lane < LANES // 2, low, swap_halves(high))


def window_start(windowed):
    if not windowed:
        return 0
    return jnp.where(lax.axis_index("wide") * SUB < 3 * BLOCK, 0, BLOCK)


def project_kernel(windowed, wide, mask_hbm, x_hbm, wl_hbm, wr_hbm, send_ref, normed_ref, *scratch):
    mask_ref, x_ref, w_ref, edge, sems = scratch
    rows = x_ref.shape[0] // SUB
    chunks = ((0, LANES), (LANES, rows - LANES))
    first = window_start(windowed)
    copies = [
        pltpu.make_async_copy(wl_hbm, w_ref.at[0], sems.at[0]),
        pltpu.make_async_copy(wr_hbm, w_ref.at[1], sems.at[1]),
        pltpu.make_async_copy(mask_hbm, mask_ref, sems.at[2]),
    ]
    for index, (low, count) in enumerate(chunks):
        source = x_hbm.at[pl.ds(pl.multiple_of((first + low) * SUB, SUB), count * SUB)]
        copies.append(
            pltpu.make_async_copy(source, x_ref.at[pl.ds(low * SUB, count * SUB)], sems.at[3 + index])
        )
    for copy in copies:
        copy.start()
    copies[2].wait()
    column_block = lax.axis_index("wide") * SUB // BLOCK
    row_block = (first + lax.broadcasted_iota(jnp.int32, (1, 2 * LANES), 1)) // BLOCK
    mask = jnp.zeros((1, 2 * LANES), jnp.float32)
    for block in range(mask_hbm.shape[0]):
        kept = mask_ref[block, column_block].astype(jnp.float32)
        mask = jnp.where(row_block == block, kept, mask)
    copies[0].wait()
    copies[1].wait()
    weights = jnp.concatenate([w_ref[0].T, w_ref[1].T], axis=0)
    for index, (low, count) in enumerate(chunks):
        copies[3 + index].wait()
        group = 2 * LANES // count
        chunk_mask = jnp.concatenate([mask[:, low : low + count]] * group, axis=1)
        for start in range(0, SUB, group):
            x = jnp.concatenate(
                [x_ref[pl.ds(low * SUB + start + k, count, stride=SUB), :] for k in range(group)], axis=0
            )
            normed = layer_norm(x, 1).astype(jnp.bfloat16)
            for k in range(group):
                normed_ref[start + k, low : low + count, :] = normed[k * count : (k + 1) * count]
            mixed = lax.dot_general(
                weights, normed, (((1,), (1,)), ((), ())), preferred_element_type=jnp.float32
            )
            for side in range(2):
                gate = mixed[2 * side * C : (2 * side + 1) * C]
                value = mixed[(2 * side + 1) * C : (2 * side + 2) * C]
                proj = jax.nn.sigmoid(gate) * value * chunk_mask
                for k in range(group):
                    at = k * count // LANES * LANES
                    piece = proj[:, at : at + LANES]
                    if k * count % LANES:
                        piece = swap_halves(piece)
                    edge[side, index, pl.ds(start + k, C, stride=SUB), :] = piece
    part = C // wide * SUB
    low = 0
    for side in range(2):
        for index, (_, count) in enumerate(chunks):
            values = edge[side, index].reshape(wide, part, LANES)
            if count < LANES:
                values = pack(values[:, : part // 2], values[:, part // 2 :])
            send_ref[:, low : low + values.shape[1], :] = values.astype(jnp.bfloat16)
            low += values.shape[1]


def triangle_kernel(windowed, recv_ref, send_ref):
    wide = recv_ref.shape[0]
    per_device = C // wide
    part = per_device * SUB
    tokens = wide * SUB
    half = per_device // 2

    def load(side, channel):
        parts = []
        for index in range(2):
            start = side * send_ref.shape[1] + index * part
            swap = windowed and index == 1 and channel >= half
            at = start + (channel - half if swap else channel) * SUB
            pair = recv_ref[:, at : at + 2 * SUB, :].astype(jnp.float32)
            if swap:
                pair = swap_halves(pair)
            parts.append([
                pair[:, low : low + SUB].reshape(tokens, LANES).astype(jnp.bfloat16)
                for low in (0, SUB)
            ])
        return [jnp.concatenate([p[n] for p in parts], axis=1) for n in range(2)]

    def product(right, left):
        return lax.dot_general(
            right, left, (((0,), (0,)), ((), ())), preferred_element_type=jnp.float32
        )

    sums = []
    for channel in range(0, per_device, 2):
        for left, right in zip(load(0, channel), load(1, channel)):
            if windowed:
                cut = 3 * BLOCK
                above = product(right[:cut], left[:cut])[:cut]
                below = product(right[cut:, LANES:], left[cut:])[: tokens - cut]
                sums.append(jnp.concatenate([above, below], axis=0))
            else:
                sums.append(product(right, left))
    first = [s[:, :LANES] for s in sums]
    second = [s[:, LANES:] for s in sums]
    if windowed:
        second = [pack(second[c], second[c + half]) for c in range(half)]
    start = 0
    for channels in (first, second):
        for channel in range(0, len(channels), 2):
            pair = [channels[channel + n].reshape(wide, SUB, LANES) for n in range(2)]
            pair = jnp.concatenate(pair, axis=1).astype(jnp.bfloat16)
            send_ref[:, start : start + 2 * SUB, :] = pair
            start += 2 * SUB


def update_kernel(windowed, recv_ref, normed_ref, wg_ref, wo_ref, out_hbm, tri, out_ref, sems):
    wide = recv_ref.shape[0]
    part = C // wide * SUB
    rows = normed_ref.shape[1]
    chunks = ((0, LANES), (LANES, rows - LANES))
    first = window_start(windowed)
    copies = []
    if windowed:
        rest = out_hbm.shape[0] - rows * SUB
        to = pl.multiple_of(jnp.where(first == 0, rows, 0) * SUB, SUB)
        out_ref[rows * SUB :, :] = jnp.zeros((rest, C), jnp.float32)
        copies.append(
            pltpu.make_async_copy(
                out_ref.at[pl.ds(rows * SUB, rest)], out_hbm.at[pl.ds(to, rest)], sems.at[2]
            )
        )
        copies[0].start()
    for index, (low, count) in enumerate(chunks):
        if count < LANES:
            sums = recv_ref[:, part:, :].astype(jnp.float32)
            sums = jnp.concatenate([sums, swap_halves(sums)], axis=1)
        else:
            sums = recv_ref[:, index * part : (index + 1) * part, :].astype(jnp.float32)
        tri[index] = layer_norm(sums.reshape(C, SUB, LANES), 0).reshape(C * SUB, LANES)
        for j in range(SUB):
            tri_normed = tri[index, pl.ds(j, C, stride=SUB), :].astype(jnp.bfloat16)
            mixed = lax.dot_general(
                tri_normed, wo_ref[...], (((0,), (0,)), ((), ())), preferred_element_type=jnp.float32
            )
            normed = normed_ref[j, low : low + count, :]
            gate = jax.nn.sigmoid(
                jnp.dot(normed, wg_ref[...], preferred_element_type=jnp.float32)
            )
            out_ref[pl.ds(low * SUB + j, count, stride=SUB), :] = gate * mixed[:count]
        to = pl.multiple_of((first + low) * SUB, SUB)
        copies.append(
            pltpu.make_async_copy(
                out_ref.at[pl.ds(low * SUB, count * SUB)],
                out_hbm.at[pl.ds(to, count * SUB)],
                sems.at[index],
            )
        )
        copies[-1].start()
    for copy in copies:
        copy.wait()


HBM = pl.BlockSpec(memory_space=pltpu.HBM)
VMEM = pl.BlockSpec(memory_space=pltpu.VMEM)
PARAMS = pltpu.CompilerParams(vmem_limit_bytes=48 * 1024 * 1024)


def kernels_on_device(
    windowed, pair_act, block_mask, left_weight, right_weight, gate_weight, out_weight
):
    tokens = pair_act.shape[0]
    rows = 3 * BLOCK if windowed else tokens
    wide = lax.axis_size("wide")
    side = rows * C // wide * SUB // LANES
    exchange = functools.partial(
        lax.all_to_all, axis_name="wide", split_axis=0, concat_axis=0, tiled=True
    )
    send, normed = pl.pallas_call(
        functools.partial(project_kernel, windowed, wide),
        out_shape=(
            jax.ShapeDtypeStruct((wide, 2 * side, LANES), jnp.bfloat16),
            jax.ShapeDtypeStruct((SUB, rows, C), jnp.bfloat16),
        ),
        in_specs=[HBM] * 4,
        out_specs=(VMEM, VMEM),
        scratch_shapes=[
            pltpu.SMEM(block_mask.shape, jnp.int32),
            pltpu.VMEM((rows * SUB, C), jnp.float32),
            pltpu.VMEM((2, C, 2 * C), jnp.bfloat16),
            pltpu.VMEM((2, 2, C * SUB, LANES), jnp.float32),
            pltpu.SemaphoreType.DMA((5,)),
        ],
        compiler_params=PARAMS,
        name="project",
    )(block_mask, pair_act.reshape(tokens * SUB, C), left_weight, right_weight)
    back = pl.pallas_call(
        functools.partial(triangle_kernel, windowed),
        out_shape=jax.ShapeDtypeStruct((wide, side, LANES), jnp.bfloat16),
        in_specs=[VMEM],
        out_specs=VMEM,
        compiler_params=PARAMS,
        name="triangle",
    )(exchange(send))
    update = pl.pallas_call(
        functools.partial(update_kernel, windowed),
        out_shape=pltpu.HBM((tokens * SUB, C), jnp.float32),
        in_specs=[VMEM] * 4,
        out_specs=HBM,
        scratch_shapes=[
            pltpu.VMEM((2, C * SUB, LANES), jnp.float32),
            pltpu.VMEM((tokens * SUB, C), jnp.float32),
            pltpu.SemaphoreType.DMA((3,)),
        ],
        compiler_params=PARAMS,
        name="update",
    )(exchange(back), normed, gate_weight, out_weight)
    return update.reshape(tokens, SUB, C)


def plain_on_device(pair_act, block_mask, left_weight, right_weight, gate_weight, out_weight):
    tile_rows = pair_act.shape[0]
    tile_cols = pair_act.shape[1]
    wide = lax.axis_size("wide")
    narrow = lax.axis_size("narrow")
    per_device = C // wide
    row_ids = lax.axis_index("narrow") * tile_rows + jnp.arange(tile_rows, dtype=jnp.int32)
    col_ids = lax.axis_index("wide") * tile_cols + jnp.arange(tile_cols, dtype=jnp.int32)
    block_ids = jnp.arange(block_mask.shape[0], dtype=jnp.int32)
    row_hot = (row_ids[:, None] // BLOCK == block_ids[None, :]).astype(jnp.float32)
    col_hot = (col_ids[:, None] // BLOCK == block_ids[None, :]).astype(jnp.float32)
    tile_mask = jnp.dot(jnp.dot(row_hot, block_mask.astype(jnp.float32)), col_hot.T).T
    normed = layer_norm(pair_act, -1).astype(jnp.bfloat16)

    def edges(weight):
        mixed = jnp.einsum("cd,ikc->dki", weight, normed, preferred_element_type=jnp.float32)
        proj = jax.nn.sigmoid(mixed[:C]) * mixed[C:] * tile_mask[None]
        return proj.astype(jnp.bfloat16).reshape(wide, per_device, tile_cols, tile_rows)

    send = jnp.stack([edges(left_weight), edges(right_weight)], axis=1)
    recv = lax.all_to_all(send, "wide", split_axis=0, concat_axis=0, tiled=True)
    left, right = recv[:, 0], recv[:, 1]
    if narrow > 1:
        right = lax.all_gather(right, "narrow", axis=3, tiled=True)
    tri = jnp.einsum("sckj,scki->cji", right, left, preferred_element_type=jnp.float32)
    back = tri.astype(jnp.bfloat16).reshape(per_device, wide, tile_cols, tile_rows)
    back = jnp.transpose(back, (1, 0, 2, 3))
    tri = lax.all_to_all(back, "wide", split_axis=0, concat_axis=0, tiled=True)
    tri = tri.reshape(C, tile_cols, tile_rows).astype(jnp.float32)
    tri_normed = layer_norm(tri, 0).astype(jnp.bfloat16)
    gate = jax.nn.sigmoid(
        jnp.einsum("ikc,cd->ikd", normed, gate_weight, preferred_element_type=jnp.float32)
    )
    return gate * jnp.einsum(
        "cji,cd->ijd", tri_normed, out_weight, preferred_element_type=jnp.float32
    )


def on_device(pair_act, block_mask, *weights):
    rows, cols = pair_act.shape[:2]
    blocks = block_mask.shape[0]
    fits = rows == 2 * LANES and cols == SUB and C // lax.axis_size("wide") == 4 and blocks == 4
    if lax.axis_size("narrow") > 1 or not fits:
        return plain_on_device(pair_act, block_mask, *weights)
    return lax.cond(
        block_mask[0, 3] == 0,
        functools.partial(kernels_on_device, True),
        functools.partial(kernels_on_device, False),
        pair_act,
        block_mask,
        *weights,
    )


def solution(mesh):
    return jax.shard_map(
        on_device,
        mesh=mesh,
        in_specs=(P("narrow", "wide", None), P(), P(), P(), P(), P()),
        out_specs=P("narrow", "wide", None),
        check_vma=False,
    )
```

```python
import functools

import jax
import jax.numpy as jnp
from jax import lax
from jax.experimental import pallas as pl
from jax.experimental.pallas import tpu as pltpu
from jax.sharding import PartitionSpec as P

C = 128
BLOCK = 64
LANES = 128
SUB = 8
PLANE = 8


def layer_norm(values, axis):
    centre = jnp.mean(values, axis=axis, keepdims=True)
    spread = jnp.mean(jnp.square(values - centre), axis=axis, keepdims=True)
    return (values - centre) * lax.rsqrt(spread + 1e-05)


def swap_halves(values):
    flat = values.reshape(-1, LANES)
    return pltpu.roll(flat, LANES // 2, 1).reshape(values.shape)


def pack(low, high):
    lane = lax.broadcasted_iota(jnp.int32, low.shape, low.ndim - 1)
    return jnp.where(lane < LANES // 2, low, swap_halves(high))


def window_start(windowed):
    if not windowed:
        return 0
    return jnp.where(lax.axis_index("wide") * SUB < 3 * BLOCK, 0, BLOCK)


def other_plane(offset):
    return (lax.axis_index("wide") // PLANE) ^ offset


def project_kernel(windowed, wide, mask_hbm, x_hbm, wl_hbm, wr_hbm, *refs):
    planes = wide // PLANE
    left_refs, right_ref = refs[:planes], refs[planes]
    normed_ref, mask_ref, x_ref, w_ref, edge, sems = refs[planes + 1 :]
    rows = x_ref.shape[0] // SUB
    chunks = ((0, LANES), (LANES, rows - LANES))
    first = window_start(windowed)
    copies = [
        pltpu.make_async_copy(wl_hbm, w_ref.at[0], sems.at[0]),
        pltpu.make_async_copy(wr_hbm, w_ref.at[1], sems.at[1]),
        pltpu.make_async_copy(mask_hbm, mask_ref, sems.at[2]),
    ]
    for index, (low, count) in enumerate(chunks):
        source = x_hbm.at[pl.ds(pl.multiple_of((first + low) * SUB, SUB), count * SUB)]
        copies.append(
            pltpu.make_async_copy(source, x_ref.at[pl.ds(low * SUB, count * SUB)], sems.at[3 + index])
        )
    for copy in copies:
        copy.start()
    copies[2].wait()
    column_block = lax.axis_index("wide") * SUB // BLOCK
    row_block = (first + lax.broadcasted_iota(jnp.int32, (1, 2 * LANES), 1)) // BLOCK
    mask = jnp.zeros((1, 2 * LANES), jnp.float32)
    for block in range(mask_hbm.shape[0]):
        kept = mask_ref[block, column_block].astype(jnp.float32)
        mask = jnp.where(row_block == block, kept, mask)
    copies[0].wait()
    copies[1].wait()
    weights = jnp.concatenate([w_ref[0].T, w_ref[1].T], axis=0)
    for index, (low, count) in enumerate(chunks):
        copies[3 + index].wait()
        group = 2 * LANES // count
        chunk_mask = jnp.concatenate([mask[:, low : low + count]] * group, axis=1)
        for start in range(0, SUB, group):
            x = jnp.concatenate(
                [x_ref[pl.ds(low * SUB + start + k, count, stride=SUB), :] for k in range(group)], axis=0
            )
            normed = layer_norm(x, 1).astype(jnp.bfloat16)
            for k in range(group):
                normed_ref[start + k, low : low + count, :] = normed[k * count : (k + 1) * count]
            mixed = lax.dot_general(
                weights, normed, (((1,), (1,)), ((), ())), preferred_element_type=jnp.float32
            )
            for side in range(2):
                gate = mixed[2 * side * C : (2 * side + 1) * C]
                value = mixed[(2 * side + 1) * C : (2 * side + 2) * C]
                proj = jax.nn.sigmoid(gate) * value * chunk_mask
                for k in range(group):
                    at = k * count // LANES * LANES
                    piece = proj[:, at : at + LANES]
                    if k * count % LANES:
                        piece = swap_halves(piece)
                    edge[side, index, pl.ds(start + k, C, stride=SUB), :] = piece
    part = C // wide * SUB
    for offset in range(planes):
        start = pl.multiple_of(other_plane(offset) * PLANE * part, PLANE * part)
        for side in range(2):
            low = 0
            for index, (_, count) in enumerate(chunks):
                values = edge[side, index, pl.ds(start, PLANE * part), :].reshape(PLANE, part, LANES)
                if count < LANES:
                    values = pack(values[:, : part // 2], values[:, part // 2 :])
                values = values.astype(jnp.bfloat16)
                high = low + values.shape[1]
                if side == 0:
                    left_refs[offset][:, low:high, :] = values
                else:
                    right_ref[:, offset, low:high, :] = values
                low = high


def triangle_kernel(windowed, planes, left_ref, *refs):
    right_refs, first_refs, second_ref = refs[:planes], refs[planes : 2 * planes], refs[2 * planes]
    edge, total = refs[2 * planes + 1 :]
    per_device = C // (planes * PLANE)
    part = per_device * SUB
    step = PLANE * SUB
    tokens = planes * step
    half = per_device // 2

    for offset in range(planes):
        at = pl.multiple_of(other_plane(offset) * step, step)
        for side, rows in enumerate((left_ref.at[:, offset], right_refs[offset])):
            for index in range(2):
                for channel in range(0, per_device, 2):
                    swap = windowed and index == 1 and channel >= half
                    low = index * part + (channel - half if swap else channel) * SUB
                    pair = rows[:, low : low + 2 * SUB, :].astype(jnp.float32)
                    if swap:
                        pair = swap_halves(pair)
                    for n in range(2):
                        values = pair[:, n * SUB : (n + 1) * SUB].reshape(step, LANES)
                        edge[side, channel + n, pl.ds(at, step), index * LANES : (index + 1) * LANES] = (
                            values.astype(jnp.bfloat16)
                        )

    def product(right, left):
        return lax.dot_general(
            right, left, (((0,), (0,)), ((), ())), preferred_element_type=jnp.float32
        )

    for channel in range(per_device):
        left, right = edge[0, channel], edge[1, channel]
        if windowed:
            cut = 3 * BLOCK
            total[channel, :cut] = product(right[:cut], left[:cut])[:cut]
            total[channel, cut:] = product(right[cut:, LANES:], left[cut:])[: tokens - cut]
        else:
            total[channel] = product(right, left)
    for offset in range(planes):
        at = pl.multiple_of(other_plane(offset) * step, step)
        sums = [total[channel, pl.ds(at, step), :] for channel in range(per_device)]
        first = [v[:, :LANES].reshape(PLANE, SUB, LANES) for v in sums]
        second = [v[:, LANES:].reshape(PLANE, SUB, LANES) for v in sums]
        if windowed:
            second = [pack(second[c], second[c + half]) for c in range(half)]
        for n in range(0, len(first), 2):
            pair = jnp.concatenate(first[n : n + 2], axis=1).astype(jnp.bfloat16)
            first_refs[offset][:, n * SUB : (n + 2) * SUB, :] = pair
        for n in range(0, len(second), 2):
            pair = jnp.concatenate(second[n : n + 2], axis=1).astype(jnp.bfloat16)
            second_ref[:, offset, n * SUB : (n + 2) * SUB, :] = pair


def update_kernel(windowed, planes, first_ref, *refs):
    second_refs = refs[:planes]
    normed_ref, wg_ref, wo_ref, out_hbm, tri, out_ref, sems = refs[planes:]
    part = C // planes * SUB
    rows = normed_ref.shape[1]
    chunks = ((0, LANES), (LANES, rows - LANES))
    first = window_start(windowed)
    copies = []
    if windowed:
        rest = out_hbm.shape[0] - rows * SUB
        to = pl.multiple_of(jnp.where(first == 0, rows, 0) * SUB, SUB)
        out_ref[rows * SUB :, :] = jnp.zeros((rest, C), jnp.float32)
        copies.append(
            pltpu.make_async_copy(
                out_ref.at[pl.ds(rows * SUB, rest)], out_hbm.at[pl.ds(to, rest)], sems.at[2]
            )
        )
        copies[0].start()
    for index, (low, count) in enumerate(chunks):
        for offset in range(planes):
            rows_of = first_ref.at[:, offset] if index == 0 else second_refs[offset]
            sums = rows_of[...].astype(jnp.float32)
            if count < LANES:
                sums = jnp.concatenate([sums, swap_halves(sums)], axis=1)
            at = pl.multiple_of(other_plane(offset) * part, part)
            tri[index, pl.ds(at, part), :] = sums.reshape(part, LANES)
        sums = tri[index].reshape(C, SUB, LANES)
        tri[index] = layer_norm(sums, 0).reshape(C * SUB, LANES)
        for j in range(SUB):
            tri_normed = tri[index, pl.ds(j, C, stride=SUB), :].astype(jnp.bfloat16)
            mixed = lax.dot_general(
                tri_normed, wo_ref[...], (((0,), (0,)), ((), ())), preferred_element_type=jnp.float32
            )
            normed = normed_ref[j, low : low + count, :]
            gate = jax.nn.sigmoid(
                jnp.dot(normed, wg_ref[...], preferred_element_type=jnp.float32)
            )
            out_ref[pl.ds(low * SUB + j, count, stride=SUB), :] = gate * mixed[:count]
        to = pl.multiple_of((first + low) * SUB, SUB)
        copies.append(
            pltpu.make_async_copy(
                out_ref.at[pl.ds(low * SUB, count * SUB)],
                out_hbm.at[pl.ds(to, count * SUB)],
                sems.at[index],
            )
        )
        copies[-1].start()
    for copy in copies:
        copy.wait()


HBM = pl.BlockSpec(memory_space=pltpu.HBM)
VMEM = pl.BlockSpec(memory_space=pltpu.VMEM)
PARAMS = pltpu.CompilerParams(vmem_limit_bytes=48 * 1024 * 1024)


def exchange(z_first, plane_first):
    planes = len(z_first)
    wide = planes * PLANE
    groups = [[plane * PLANE + n for n in range(PLANE)] for plane in range(planes)]

    def over_z(slots):
        pairs = lambda offset: [(device, device ^ (offset * PLANE)) for device in range(wide)]
        moved = {o: lax.ppermute(slots[o], "wide", pairs(o)) for o in range(planes - 1, 0, -1)}
        return [moved.get(o, slots[o]) for o in range(planes)]

    def in_plane(array):
        return lax.all_to_all(
            array, "wide", split_axis=0, concat_axis=0, axis_index_groups=groups, tiled=True
        )

    z_first = over_z(z_first)
    plane_first = in_plane(plane_first)
    plane_first = over_z([plane_first[:, offset] for offset in range(planes)])
    return in_plane(jnp.stack(z_first, axis=1)), plane_first


def kernels_on_device(
    windowed, pair_act, block_mask, left_weight, right_weight, gate_weight, out_weight
):
    tokens = pair_act.shape[0]
    rows = 3 * BLOCK if windowed else tokens
    wide = lax.axis_size("wide")
    planes = wide // PLANE
    part = C // wide * SUB
    both = rows * part // LANES
    slot = lambda height: jax.ShapeDtypeStruct((PLANE, height, LANES), jnp.bfloat16)
    slots = lambda height: jax.ShapeDtypeStruct((PLANE, planes, height, LANES), jnp.bfloat16)
    *left, right, normed = pl.pallas_call(
        functools.partial(project_kernel, windowed, wide),
        out_shape=[slot(both)] * planes
        + [slots(both), jax.ShapeDtypeStruct((SUB, rows, C), jnp.bfloat16)],
        in_specs=[HBM] * 4,
        out_specs=[VMEM] * (planes + 2),
        scratch_shapes=[
            pltpu.SMEM(block_mask.shape, jnp.int32),
            pltpu.VMEM((rows * SUB, C), jnp.float32),
            pltpu.VMEM((2, C, 2 * C), jnp.bfloat16),
            pltpu.VMEM((2, 2, C * SUB, LANES), jnp.float32),
            pltpu.SemaphoreType.DMA((5,)),
        ],
        compiler_params=PARAMS,
        name="project",
    )(block_mask, pair_act.reshape(tokens * SUB, C), left_weight, right_weight)
    left, right = exchange(left, right)
    *first, second = pl.pallas_call(
        functools.partial(triangle_kernel, windowed, planes),
        out_shape=[slot(part)] * planes + [slots(both - part)],
        in_specs=[VMEM] * (planes + 1),
        out_specs=[VMEM] * (planes + 1),
        scratch_shapes=[
            pltpu.VMEM((2, C // wide, tokens, 2 * LANES), jnp.bfloat16),
            pltpu.VMEM((C // wide, tokens, 2 * LANES), jnp.float32),
        ],
        compiler_params=PARAMS,
        name="triangle",
    )(left, *right)
    first, second = exchange(first, second)
    update = pl.pallas_call(
        functools.partial(update_kernel, windowed, planes),
        out_shape=pltpu.HBM((tokens * SUB, C), jnp.float32),
        in_specs=[VMEM] * (planes + 4),
        out_specs=HBM,
        scratch_shapes=[
            pltpu.VMEM((2, C * SUB, LANES), jnp.float32),
            pltpu.VMEM((tokens * SUB, C), jnp.float32),
            pltpu.SemaphoreType.DMA((3,)),
        ],
        compiler_params=PARAMS,
        name="update",
    )(first, *second, normed, gate_weight, out_weight)
    return update.reshape(tokens, SUB, C)


def plain_on_device(pair_act, block_mask, left_weight, right_weight, gate_weight, out_weight):
    tile_rows = pair_act.shape[0]
    tile_cols = pair_act.shape[1]
    wide = lax.axis_size("wide")
    narrow = lax.axis_size("narrow")
    per_device = C // wide
    row_ids = lax.axis_index("narrow") * tile_rows + jnp.arange(tile_rows, dtype=jnp.int32)
    col_ids = lax.axis_index("wide") * tile_cols + jnp.arange(tile_cols, dtype=jnp.int32)
    block_ids = jnp.arange(block_mask.shape[0], dtype=jnp.int32)
    row_hot = (row_ids[:, None] // BLOCK == block_ids[None, :]).astype(jnp.float32)
    col_hot = (col_ids[:, None] // BLOCK == block_ids[None, :]).astype(jnp.float32)
    tile_mask = jnp.dot(jnp.dot(row_hot, block_mask.astype(jnp.float32)), col_hot.T).T
    normed = layer_norm(pair_act, -1).astype(jnp.bfloat16)

    def edges(weight):
        mixed = jnp.einsum("cd,ikc->dki", weight, normed, preferred_element_type=jnp.float32)
        proj = jax.nn.sigmoid(mixed[:C]) * mixed[C:] * tile_mask[None]
        return proj.astype(jnp.bfloat16).reshape(wide, per_device, tile_cols, tile_rows)

    send = jnp.stack([edges(left_weight), edges(right_weight)], axis=1)
    recv = lax.all_to_all(send, "wide", split_axis=0, concat_axis=0, tiled=True)
    left, right = recv[:, 0], recv[:, 1]
    if narrow > 1:
        right = lax.all_gather(right, "narrow", axis=3, tiled=True)
    tri = jnp.einsum("sckj,scki->cji", right, left, preferred_element_type=jnp.float32)
    back = tri.astype(jnp.bfloat16).reshape(per_device, wide, tile_cols, tile_rows)
    back = jnp.transpose(back, (1, 0, 2, 3))
    tri = lax.all_to_all(back, "wide", split_axis=0, concat_axis=0, tiled=True)
    tri = tri.reshape(C, tile_cols, tile_rows).astype(jnp.float32)
    tri_normed = layer_norm(tri, 0).astype(jnp.bfloat16)
    gate = jax.nn.sigmoid(
        jnp.einsum("ikc,cd->ikd", normed, gate_weight, preferred_element_type=jnp.float32)
    )
    return gate * jnp.einsum(
        "cji,cd->ijd", tri_normed, out_weight, preferred_element_type=jnp.float32
    )


def on_device(pair_act, block_mask, *weights):
    rows, cols = pair_act.shape[:2]
    blocks = block_mask.shape[0]
    fits = rows == 2 * LANES and cols == SUB and C // lax.axis_size("wide") == 4 and blocks == 4
    if lax.axis_size("narrow") > 1 or not fits:
        return plain_on_device(pair_act, block_mask, *weights)
    return lax.cond(
        block_mask[0, 3] == 0,
        functools.partial(kernels_on_device, True),
        functools.partial(kernels_on_device, False),
        pair_act,
        block_mask,
        *weights,
    )


def solution(mesh):
    return jax.shard_map(
        on_device,
        mesh=mesh,
        in_specs=(P("narrow", "wide", None), P(), P(), P(), P(), P()),
        out_specs=P("narrow", "wide", None),
        check_vma=False,
    )
```

```python
import functools

import jax
import jax.numpy as jnp
from jax import lax
from jax.experimental import pallas as pl
from jax.experimental.pallas import tpu as pltpu
from jax.sharding import PartitionSpec as P

C = 128
BLOCK = 64
LANES = 128
SUB = 8


def layer_norm(values, axis):
    centre = jnp.mean(values, axis=axis, keepdims=True)
    spread = jnp.mean(jnp.square(values - centre), axis=axis, keepdims=True)
    return (values - centre) * lax.rsqrt(spread + 1e-05)


def swap_halves(values):
    flat = values.reshape(-1, LANES)
    return pltpu.roll(flat, LANES // 2, 1).reshape(values.shape)


def pack(low, high):
    lane = lax.broadcasted_iota(jnp.int32, low.shape, low.ndim - 1)
    return jnp.where(lane < LANES // 2, low, swap_halves(high))


def window_start(windowed):
    if not windowed:
        return 0
    return jnp.where(lax.axis_index("wide") * SUB < 3 * BLOCK, 0, BLOCK)


def chunks_of(rows):
    return ((0, LANES), (LANES, rows - LANES))


def project_kernel(mask_hbm, x_hbm, wl_hbm, wr_hbm, *refs):
    whole_ref, window_ref, normed_ref, cut_ref, mask_ref, x_ref, w_ref, edge, sems = refs
    wide = whole_ref.shape[0]
    tokens = x_ref.shape[0] // SUB
    copies = [
        pltpu.make_async_copy(mask_hbm, mask_ref, sems.at[0]),
        pltpu.make_async_copy(wl_hbm, w_ref.at[0], sems.at[1]),
        pltpu.make_async_copy(wr_hbm, w_ref.at[1], sems.at[2]),
    ]
    for index in range(2):
        part = pl.ds(index * LANES * SUB, LANES * SUB)
        copies.append(pltpu.make_async_copy(x_hbm.at[part], x_ref.at[part], sems.at[3 + index]))
    for copy in copies:
        copy.start()
    copies[0].wait()
    cut = mask_ref[0, 3] == 0
    cut_ref[0] = cut.astype(jnp.int32)
    column_block = lax.axis_index("wide") * SUB // BLOCK
    kept = [mask_ref[block, column_block].astype(jnp.float32) for block in range(mask_hbm.shape[0])]
    copies[1].wait()
    copies[2].wait()
    weights = jnp.concatenate([w_ref[0].T, w_ref[1].T], axis=0)

    def project(windowed, send_ref):
        first = window_start(windowed)
        row_block = (first + lax.broadcasted_iota(jnp.int32, (1, 2 * LANES), 1)) // BLOCK
        mask = jnp.zeros((1, 2 * LANES), jnp.float32)
        for block, value in enumerate(kept):
            mask = jnp.where(row_block == block, value, mask)
        if windowed:
            copies[3].wait()
            copies[4].wait()
        chunks = chunks_of(3 * BLOCK if windowed else tokens)
        for index, (low, count) in enumerate(chunks):
            if not windowed:
                copies[3 + index].wait()
            group = 2 * LANES // count
            chunk_mask = jnp.concatenate([mask[:, low : low + count]] * group, axis=1)
            base = pl.multiple_of((first + low) * SUB, SUB)
            for start in range(0, SUB, group):
                x = [x_ref[pl.ds(base + start + k, count, stride=SUB), :] for k in range(group)]
                normed = layer_norm(jnp.concatenate(x, axis=0), 1).astype(jnp.bfloat16)
                for k in range(group):
                    normed_ref[start + k, low : low + count, :] = normed[k * count : (k + 1) * count]
                mixed = lax.dot_general(
                    weights, normed, (((1,), (1,)), ((), ())), preferred_element_type=jnp.float32
                )
                for side in range(2):
                    gate = mixed[2 * side * C : (2 * side + 1) * C]
                    value = mixed[(2 * side + 1) * C : (2 * side + 2) * C]
                    proj = jax.nn.sigmoid(gate) * value * chunk_mask
                    for k in range(group):
                        at = k * count // LANES * LANES
                        piece = proj[:, at : at + LANES]
                        if k * count % LANES:
                            piece = swap_halves(piece)
                        edge[side, index, pl.ds(start + k, C, stride=SUB), :] = piece
        part = C // wide * SUB
        low = 0
        for side in range(2):
            for index, (_, count) in enumerate(chunks):
                values = edge[side, index].reshape(wide, part, LANES)
                if count < LANES:
                    values = pack(values[:, : part // 2], values[:, part // 2 :])
                send_ref[:, low : low + values.shape[1], :] = values.astype(jnp.bfloat16)
                low += values.shape[1]

    pl.when(cut)(lambda: project(True, window_ref))
    pl.when(jnp.logical_not(cut))(lambda: project(False, whole_ref))


def triangle_kernel(windowed, recv_ref, send_ref):
    wide = recv_ref.shape[0]
    per_device = C // wide
    part = per_device * SUB
    tokens = wide * SUB
    half = per_device // 2

    def load(side, channel):
        parts = []
        for index in range(2):
            start = side * send_ref.shape[1] + index * part
            swap = windowed and index == 1 and channel >= half
            at = start + (channel - half if swap else channel) * SUB
            pair = recv_ref[:, at : at + 2 * SUB, :].astype(jnp.float32)
            if swap:
                pair = swap_halves(pair)
            parts.append([
                pair[:, low : low + SUB].reshape(tokens, LANES).astype(jnp.bfloat16)
                for low in (0, SUB)
            ])
        return [jnp.concatenate([p[n] for p in parts], axis=1) for n in range(2)]

    def product(right, left):
        return lax.dot_general(
            right, left, (((0,), (0,)), ((), ())), preferred_element_type=jnp.float32
        )

    sums = []
    for channel in range(0, per_device, 2):
        for left, right in zip(load(0, channel), load(1, channel)):
            if windowed:
                cut = 3 * BLOCK
                above = product(right[:cut], left[:cut])[:cut]
                below = product(right[cut:, LANES:], left[cut:])[: tokens - cut]
                sums.append(jnp.concatenate([above, below], axis=0))
            else:
                sums.append(product(right, left))
    first = [s[:, :LANES] for s in sums]
    second = [s[:, LANES:] for s in sums]
    if windowed:
        second = [pack(second[c], second[c + half]) for c in range(half)]
    start = 0
    for channels in (first, second):
        for channel in range(0, len(channels), 2):
            pair = [channels[channel + n].reshape(wide, SUB, LANES) for n in range(2)]
            pair = jnp.concatenate(pair, axis=1).astype(jnp.bfloat16)
            send_ref[:, start : start + 2 * SUB, :] = pair
            start += 2 * SUB


def update_kernel(windowed, recv_ref, normed_ref, wg_ref, wo_ref, out_hbm, tri, out_ref, sems):
    wide = recv_ref.shape[0]
    part = C // wide * SUB
    rows = 3 * BLOCK if windowed else normed_ref.shape[1]
    chunks = chunks_of(rows)
    first = window_start(windowed)
    copies = []
    if windowed:
        rest = out_hbm.shape[0] - rows * SUB
        to = pl.multiple_of(jnp.where(first == 0, rows, 0) * SUB, SUB)
        out_ref[rows * SUB :, :] = jnp.zeros((rest, C), jnp.float32)
        copies.append(
            pltpu.make_async_copy(
                out_ref.at[pl.ds(rows * SUB, rest)], out_hbm.at[pl.ds(to, rest)], sems.at[2]
            )
        )
        copies[0].start()
    for index, (low, count) in enumerate(chunks):
        if count < LANES:
            sums = recv_ref[:, part:, :].astype(jnp.float32)
            sums = jnp.concatenate([sums, swap_halves(sums)], axis=1)
        else:
            sums = recv_ref[:, index * part : (index + 1) * part, :].astype(jnp.float32)
        tri[index] = layer_norm(sums.reshape(C, SUB, LANES), 0).reshape(C * SUB, LANES)
        for j in range(SUB):
            tri_normed = tri[index, pl.ds(j, C, stride=SUB), :].astype(jnp.bfloat16)
            mixed = lax.dot_general(
                tri_normed, wo_ref[...], (((0,), (0,)), ((), ())), preferred_element_type=jnp.float32
            )
            normed = normed_ref[j, low : low + count, :]
            gate = jax.nn.sigmoid(
                jnp.dot(normed, wg_ref[...], preferred_element_type=jnp.float32)
            )
            out_ref[pl.ds(low * SUB + j, count, stride=SUB), :] = gate * mixed[:count]
        to = pl.multiple_of((first + low) * SUB, SUB)
        copies.append(
            pltpu.make_async_copy(
                out_ref.at[pl.ds(low * SUB, count * SUB)],
                out_hbm.at[pl.ds(to, count * SUB)],
                sems.at[index],
            )
        )
        copies[-1].start()
    for copy in copies:
        copy.wait()


HBM = pl.BlockSpec(memory_space=pltpu.HBM)
VMEM = pl.BlockSpec(memory_space=pltpu.VMEM)
PARAMS = pltpu.CompilerParams(vmem_limit_bytes=48 * 1024 * 1024)


def in_hbm(array):
    return pltpu.with_memory_space_constraint(array, pltpu.HBM)


def exchange(array):
    return lax.all_to_all(array, "wide", split_axis=0, concat_axis=0, tiled=True)


def after_projection(windowed, whole, window, normed, gate_weight, out_weight):
    send = window if windowed else whole
    wide, both, _ = send.shape
    tokens = normed.shape[1]
    back = pl.pallas_call(
        functools.partial(triangle_kernel, windowed),
        out_shape=jax.ShapeDtypeStruct((wide, both // 2, LANES), jnp.bfloat16),
        in_specs=[VMEM],
        out_specs=VMEM,
        compiler_params=PARAMS,
        name="triangle",
    )(exchange(send))
    return pl.pallas_call(
        functools.partial(update_kernel, windowed),
        out_shape=pltpu.HBM((tokens * SUB, C), jnp.float32),
        in_specs=[VMEM] * 4,
        out_specs=HBM,
        scratch_shapes=[
            pltpu.VMEM((2, C * SUB, LANES), jnp.float32),
            pltpu.VMEM((tokens * SUB, C), jnp.float32),
            pltpu.SemaphoreType.DMA((3,)),
        ],
        compiler_params=PARAMS,
        name="update",
    )(exchange(back), normed, gate_weight, out_weight)


def kernels_on_device(pair_act, block_mask, left_weight, right_weight, gate_weight, out_weight):
    tokens = pair_act.shape[0]
    wide = lax.axis_size("wide")
    both = lambda rows: 2 * rows * (C // wide) * SUB // LANES
    whole, window, normed, cut = pl.pallas_call(
        project_kernel,
        out_shape=(
            jax.ShapeDtypeStruct((wide, both(tokens), LANES), jnp.bfloat16),
            jax.ShapeDtypeStruct((wide, both(3 * BLOCK), LANES), jnp.bfloat16),
            jax.ShapeDtypeStruct((SUB, tokens, C), jnp.bfloat16),
            pltpu.SMEM((1,), jnp.int32),
        ),
        in_specs=[HBM] * 4,
        out_specs=(VMEM, VMEM, VMEM, pl.BlockSpec(memory_space=pltpu.SMEM)),
        scratch_shapes=[
            pltpu.SMEM(block_mask.shape, jnp.int32),
            pltpu.VMEM((tokens * SUB, C), jnp.float32),
            pltpu.VMEM((2, C, 2 * C), jnp.bfloat16),
            pltpu.VMEM((2, 2, C * SUB, LANES), jnp.float32),
            pltpu.SemaphoreType.DMA((5,)),
        ],
        compiler_params=PARAMS,
        name="project",
    )(
        in_hbm(block_mask),
        in_hbm(pair_act.reshape(tokens * SUB, C)),
        in_hbm(left_weight),
        in_hbm(right_weight),
    )
    update = lax.switch(
        cut[0],
        [functools.partial(after_projection, windowed) for windowed in (False, True)],
        whole,
        window,
        normed,
        gate_weight,
        out_weight,
    )
    return update.reshape(tokens, SUB, C)


def plain_on_device(pair_act, block_mask, left_weight, right_weight, gate_weight, out_weight):
    tile_rows = pair_act.shape[0]
    tile_cols = pair_act.shape[1]
    wide = lax.axis_size("wide")
    narrow = lax.axis_size("narrow")
    per_device = C // wide
    row_ids = lax.axis_index("narrow") * tile_rows + jnp.arange(tile_rows, dtype=jnp.int32)
    col_ids = lax.axis_index("wide") * tile_cols + jnp.arange(tile_cols, dtype=jnp.int32)
    block_ids = jnp.arange(block_mask.shape[0], dtype=jnp.int32)
    row_hot = (row_ids[:, None] // BLOCK == block_ids[None, :]).astype(jnp.float32)
    col_hot = (col_ids[:, None] // BLOCK == block_ids[None, :]).astype(jnp.float32)
    tile_mask = jnp.dot(jnp.dot(row_hot, block_mask.astype(jnp.float32)), col_hot.T).T
    normed = layer_norm(pair_act, -1).astype(jnp.bfloat16)

    def edges(weight):
        mixed = jnp.einsum("cd,ikc->dki", weight, normed, preferred_element_type=jnp.float32)
        proj = jax.nn.sigmoid(mixed[:C]) * mixed[C:] * tile_mask[None]
        return proj.astype(jnp.bfloat16).reshape(wide, per_device, tile_cols, tile_rows)

    send = jnp.stack([edges(left_weight), edges(right_weight)], axis=1)
    recv = lax.all_to_all(send, "wide", split_axis=0, concat_axis=0, tiled=True)
    left, right = recv[:, 0], recv[:, 1]
    if narrow > 1:
        right = lax.all_gather(right, "narrow", axis=3, tiled=True)
    tri = jnp.einsum("sckj,scki->cji", right, left, preferred_element_type=jnp.float32)
    back = tri.astype(jnp.bfloat16).reshape(per_device, wide, tile_cols, tile_rows)
    back = jnp.transpose(back, (1, 0, 2, 3))
    tri = lax.all_to_all(back, "wide", split_axis=0, concat_axis=0, tiled=True)
    tri = tri.reshape(C, tile_cols, tile_rows).astype(jnp.float32)
    tri_normed = layer_norm(tri, 0).astype(jnp.bfloat16)
    gate = jax.nn.sigmoid(
        jnp.einsum("ikc,cd->ikd", normed, gate_weight, preferred_element_type=jnp.float32)
    )
    return gate * jnp.einsum(
        "cji,cd->ijd", tri_normed, out_weight, preferred_element_type=jnp.float32
    )


def on_device(pair_act, block_mask, *weights):
    rows, cols = pair_act.shape[:2]
    blocks = block_mask.shape[0]
    fits = rows == 2 * LANES and cols == SUB and C // lax.axis_size("wide") == 4 and blocks == 4
    if lax.axis_size("narrow") > 1 or not fits:
        return plain_on_device(pair_act, block_mask, *weights)
    return kernels_on_device(pair_act, block_mask, *weights)


def solution(mesh):
    return jax.shard_map(
        on_device,
        mesh=mesh,
        in_specs=(P("narrow", "wide", None), P(), P(), P(), P(), P()),
        out_specs=P("narrow", "wide", None),
        check_vma=False,
    )
```

```python
import functools

import jax
import jax.numpy as jnp
from jax import lax
from jax.experimental import pallas as pl
from jax.experimental.pallas import tpu as pltpu
from jax.sharding import PartitionSpec as P

C = 128
BLOCK = 64
LANES = 128
SUB = 8
PLANE = 8


def layer_norm(values, axis):
    centre = jnp.mean(values, axis=axis, keepdims=True)
    spread = jnp.mean(jnp.square(values - centre), axis=axis, keepdims=True)
    return (values - centre) * lax.rsqrt(spread + 1e-05)


def swap_halves(values):
    flat = values.reshape(-1, LANES)
    return pltpu.roll(flat, LANES // 2, 1).reshape(values.shape)


def exchange_order(wide):
    planes = wide // PLANE
    inner = sorted(range(PLANE), key=lambda n: (n % 2, n // 2 % 2, n // 4))
    return [plane * PLANE + n for n in inner for plane in range(planes)]


def pack(low, high):
    lane = lax.broadcasted_iota(jnp.int32, low.shape, low.ndim - 1)
    return jnp.where(lane < LANES // 2, low, swap_halves(high))


def window_start(windowed):
    if not windowed:
        return 0
    return jnp.where(lax.axis_index("wide") * SUB < 3 * BLOCK, 0, BLOCK)


def chunks_of(rows):
    return ((0, LANES), (LANES, rows - LANES))


def project_kernel(mask_hbm, x_hbm, wl_hbm, wr_hbm, *refs):
    whole_ref, window_ref, normed_ref, cut_ref, mask_ref, x_ref, w_ref, edge, sems = refs
    wide = whole_ref.shape[0]
    tokens = x_ref.shape[0] // SUB
    copies = [
        pltpu.make_async_copy(mask_hbm, mask_ref, sems.at[0]),
        pltpu.make_async_copy(wl_hbm, w_ref.at[0], sems.at[1]),
        pltpu.make_async_copy(wr_hbm, w_ref.at[1], sems.at[2]),
    ]
    for index in range(2):
        part = pl.ds(index * LANES * SUB, LANES * SUB)
        copies.append(pltpu.make_async_copy(x_hbm.at[part], x_ref.at[part], sems.at[3 + index]))
    for copy in copies:
        copy.start()
    copies[0].wait()
    cut = mask_ref[0, 3] == 0
    cut_ref[0] = cut.astype(jnp.int32)
    column_block = lax.axis_index("wide") * SUB // BLOCK
    kept = [mask_ref[block, column_block].astype(jnp.float32) for block in range(mask_hbm.shape[0])]
    copies[1].wait()
    copies[2].wait()
    weights = jnp.concatenate([w_ref[0].T, w_ref[1].T], axis=0)

    def project(windowed, send_ref):
        first = window_start(windowed)
        row_block = (first + lax.broadcasted_iota(jnp.int32, (1, 2 * LANES), 1)) // BLOCK
        mask = jnp.zeros((1, 2 * LANES), jnp.float32)
        for block, value in enumerate(kept):
            mask = jnp.where(row_block == block, value, mask)
        if windowed:
            copies[3].wait()
            copies[4].wait()
        chunks = chunks_of(3 * BLOCK if windowed else tokens)
        for index, (low, count) in enumerate(chunks):
            if not windowed:
                copies[3 + index].wait()
            group = 2 * LANES // count
            chunk_mask = jnp.concatenate([mask[:, low : low + count]] * group, axis=1)
            base = pl.multiple_of((first + low) * SUB, SUB)
            for start in range(0, SUB, group):
                x = [x_ref[pl.ds(base + start + k, count, stride=SUB), :] for k in range(group)]
                normed = layer_norm(jnp.concatenate(x, axis=0), 1).astype(jnp.bfloat16)
                for k in range(group):
                    normed_ref[start + k, low : low + count, :] = normed[k * count : (k + 1) * count]
                mixed = lax.dot_general(
                    weights, normed, (((1,), (1,)), ((), ())), preferred_element_type=jnp.float32
                )
                for side in range(2):
                    gate = mixed[2 * side * C : (2 * side + 1) * C]
                    value = mixed[(2 * side + 1) * C : (2 * side + 2) * C]
                    proj = jax.nn.sigmoid(gate) * value * chunk_mask
                    for k in range(group):
                        at = k * count // LANES * LANES
                        piece = proj[:, at : at + LANES]
                        if k * count % LANES:
                            piece = swap_halves(piece)
                        edge[side, index, pl.ds(start + k, C, stride=SUB), :] = piece
        part = C // wide * SUB
        low = 0
        for side in range(2):
            for index, (_, count) in enumerate(chunks):
                values = edge[side, index].reshape(wide, part, LANES)
                if count < LANES:
                    values = pack(values[:, : part // 2], values[:, part // 2 :])
                for place, device in enumerate(exchange_order(wide)):
                    send_ref[place, low : low + values.shape[1], :] = values[device].astype(jnp.bfloat16)
                low += values.shape[1]

    pl.when(cut)(lambda: project(True, window_ref))
    pl.when(jnp.logical_not(cut))(lambda: project(False, whole_ref))


def triangle_kernel(windowed, recv_ref, send_ref):
    wide = recv_ref.shape[0]
    per_device = C // wide
    part = per_device * SUB
    tokens = wide * SUB
    half = per_device // 2
    order = exchange_order(wide)
    places = [order.index(device) for device in range(wide)]

    def load(side, channel):
        parts = []
        for index in range(2):
            start = side * send_ref.shape[1] + index * part
            swap = windowed and index == 1 and channel >= half
            at = start + (channel - half if swap else channel) * SUB
            pairs = [recv_ref[place, at : at + 2 * SUB, :].astype(jnp.float32) for place in places]
            parts.append([])
            for low in (0, SUB):
                rows = jnp.concatenate([pair[low : low + SUB] for pair in pairs], axis=0)
                parts[-1].append((swap_halves(rows) if swap else rows).astype(jnp.bfloat16))
        return [jnp.concatenate([p[n] for p in parts], axis=1) for n in range(2)]

    def product(right, left):
        return lax.dot_general(
            right, left, (((0,), (0,)), ((), ())), preferred_element_type=jnp.float32
        )

    sums = []
    for channel in range(0, per_device, 2):
        for left, right in zip(load(0, channel), load(1, channel)):
            if windowed:
                cut = 3 * BLOCK
                above = product(right[:cut], left[:cut])[:cut]
                below = product(right[cut:, LANES:], left[cut:])[: tokens - cut]
                sums.append(jnp.concatenate([above, below], axis=0))
            else:
                sums.append(product(right, left))
    first = [s[:, :LANES] for s in sums]
    second = [s[:, LANES:] for s in sums]
    if windowed:
        second = [pack(second[c], second[c + half]) for c in range(half)]
    start = 0
    for channels in (first, second):
        for channel in range(0, len(channels), 2):
            pair = [channels[channel + n].reshape(wide, SUB, LANES) for n in range(2)]
            pair = jnp.concatenate(pair, axis=1).astype(jnp.bfloat16)
            for place, device in enumerate(order):
                send_ref[place, start : start + 2 * SUB, :] = pair[device]
            start += 2 * SUB


def update_kernel(windowed, recv_ref, normed_ref, wg_ref, wo_ref, out_hbm, tri, out_ref, sems):
    wide = recv_ref.shape[0]
    part = C // wide * SUB
    rows = 3 * BLOCK if windowed else normed_ref.shape[1]
    chunks = chunks_of(rows)
    first = window_start(windowed)
    order = exchange_order(wide)
    places = [order.index(device) for device in range(wide)]
    copies = []
    if windowed:
        rest = out_hbm.shape[0] - rows * SUB
        to = pl.multiple_of(jnp.where(first == 0, rows, 0) * SUB, SUB)
        out_ref[rows * SUB :, :] = jnp.zeros((rest, C), jnp.float32)
        copies.append(
            pltpu.make_async_copy(
                out_ref.at[pl.ds(rows * SUB, rest)], out_hbm.at[pl.ds(to, rest)], sems.at[2]
            )
        )
        copies[0].start()
    for index, (low, count) in enumerate(chunks):
        height = part * count // LANES
        sums = [recv_ref[place, index * part : index * part + height, :] for place in places]
        sums = jnp.stack(sums).astype(jnp.float32)
        if count < LANES:
            sums = jnp.concatenate([sums, swap_halves(sums)], axis=1)
        tri[index] = layer_norm(sums.reshape(C, SUB, LANES), 0).reshape(C * SUB, LANES)
        for j in range(SUB):
            tri_normed = tri[index, pl.ds(j, C, stride=SUB), :].astype(jnp.bfloat16)
            mixed = lax.dot_general(
                tri_normed, wo_ref[...], (((0,), (0,)), ((), ())), preferred_element_type=jnp.float32
            )
            normed = normed_ref[j, low : low + count, :]
            gate = jax.nn.sigmoid(
                jnp.dot(normed, wg_ref[...], preferred_element_type=jnp.float32)
            )
            out_ref[pl.ds(low * SUB + j, count, stride=SUB), :] = gate * mixed[:count]
        to = pl.multiple_of((first + low) * SUB, SUB)
        copies.append(
            pltpu.make_async_copy(
                out_ref.at[pl.ds(low * SUB, count * SUB)],
                out_hbm.at[pl.ds(to, count * SUB)],
                sems.at[index],
            )
        )
        copies[-1].start()
    for copy in copies:
        copy.wait()


HBM = pl.BlockSpec(memory_space=pltpu.HBM)
VMEM = pl.BlockSpec(memory_space=pltpu.VMEM)
PARAMS = pltpu.CompilerParams(vmem_limit_bytes=48 * 1024 * 1024)


def in_hbm(array):
    return pltpu.with_memory_space_constraint(array, pltpu.HBM)


def exchange(array):
    groups = [exchange_order(array.shape[0])]
    return lax.all_to_all(
        array, "wide", split_axis=0, concat_axis=0, axis_index_groups=groups, tiled=True
    )


def after_projection(windowed, whole, window, normed, gate_weight, out_weight):
    send = window if windowed else whole
    wide, both, _ = send.shape
    tokens = normed.shape[1]
    back = pl.pallas_call(
        functools.partial(triangle_kernel, windowed),
        out_shape=jax.ShapeDtypeStruct((wide, both // 2, LANES), jnp.bfloat16),
        in_specs=[VMEM],
        out_specs=VMEM,
        compiler_params=PARAMS,
        name="triangle",
    )(exchange(send))
    return pl.pallas_call(
        functools.partial(update_kernel, windowed),
        out_shape=pltpu.HBM((tokens * SUB, C), jnp.float32),
        in_specs=[VMEM] * 4,
        out_specs=HBM,
        scratch_shapes=[
            pltpu.VMEM((2, C * SUB, LANES), jnp.float32),
            pltpu.VMEM((tokens * SUB, C), jnp.float32),
            pltpu.SemaphoreType.DMA((3,)),
        ],
        compiler_params=PARAMS,
        name="update",
    )(exchange(back), normed, gate_weight, out_weight)


def kernels_on_device(pair_act, block_mask, left_weight, right_weight, gate_weight, out_weight):
    tokens = pair_act.shape[0]
    wide = lax.axis_size("wide")
    both = lambda rows: 2 * rows * (C // wide) * SUB // LANES
    whole, window, normed, cut = pl.pallas_call(
        project_kernel,
        out_shape=(
            jax.ShapeDtypeStruct((wide, both(tokens), LANES), jnp.bfloat16),
            jax.ShapeDtypeStruct((wide, both(3 * BLOCK), LANES), jnp.bfloat16),
            jax.ShapeDtypeStruct((SUB, tokens, C), jnp.bfloat16),
            pltpu.SMEM((1,), jnp.int32),
        ),
        in_specs=[HBM] * 4,
        out_specs=(VMEM, VMEM, VMEM, pl.BlockSpec(memory_space=pltpu.SMEM)),
        scratch_shapes=[
            pltpu.SMEM(block_mask.shape, jnp.int32),
            pltpu.VMEM((tokens * SUB, C), jnp.float32),
            pltpu.VMEM((2, C, 2 * C), jnp.bfloat16),
            pltpu.VMEM((2, 2, C * SUB, LANES), jnp.float32),
            pltpu.SemaphoreType.DMA((5,)),
        ],
        compiler_params=PARAMS,
        name="project",
    )(
        in_hbm(block_mask),
        in_hbm(pair_act.reshape(tokens * SUB, C)),
        in_hbm(left_weight),
        in_hbm(right_weight),
    )
    update = lax.switch(
        cut[0],
        [functools.partial(after_projection, windowed) for windowed in (False, True)],
        whole,
        window,
        normed,
        gate_weight,
        out_weight,
    )
    return update.reshape(tokens, SUB, C)


def plain_on_device(pair_act, block_mask, left_weight, right_weight, gate_weight, out_weight):
    tile_rows = pair_act.shape[0]
    tile_cols = pair_act.shape[1]
    wide = lax.axis_size("wide")
    narrow = lax.axis_size("narrow")
    per_device = C // wide
    row_ids = lax.axis_index("narrow") * tile_rows + jnp.arange(tile_rows, dtype=jnp.int32)
    col_ids = lax.axis_index("wide") * tile_cols + jnp.arange(tile_cols, dtype=jnp.int32)
    block_ids = jnp.arange(block_mask.shape[0], dtype=jnp.int32)
    row_hot = (row_ids[:, None] // BLOCK == block_ids[None, :]).astype(jnp.float32)
    col_hot = (col_ids[:, None] // BLOCK == block_ids[None, :]).astype(jnp.float32)
    tile_mask = jnp.dot(jnp.dot(row_hot, block_mask.astype(jnp.float32)), col_hot.T).T
    normed = layer_norm(pair_act, -1).astype(jnp.bfloat16)

    def edges(weight):
        mixed = jnp.einsum("cd,ikc->dki", weight, normed, preferred_element_type=jnp.float32)
        proj = jax.nn.sigmoid(mixed[:C]) * mixed[C:] * tile_mask[None]
        return proj.astype(jnp.bfloat16).reshape(wide, per_device, tile_cols, tile_rows)

    send = jnp.stack([edges(left_weight), edges(right_weight)], axis=1)
    recv = lax.all_to_all(send, "wide", split_axis=0, concat_axis=0, tiled=True)
    left, right = recv[:, 0], recv[:, 1]
    if narrow > 1:
        right = lax.all_gather(right, "narrow", axis=3, tiled=True)
    tri = jnp.einsum("sckj,scki->cji", right, left, preferred_element_type=jnp.float32)
    back = tri.astype(jnp.bfloat16).reshape(per_device, wide, tile_cols, tile_rows)
    back = jnp.transpose(back, (1, 0, 2, 3))
    tri = lax.all_to_all(back, "wide", split_axis=0, concat_axis=0, tiled=True)
    tri = tri.reshape(C, tile_cols, tile_rows).astype(jnp.float32)
    tri_normed = layer_norm(tri, 0).astype(jnp.bfloat16)
    gate = jax.nn.sigmoid(
        jnp.einsum("ikc,cd->ikd", normed, gate_weight, preferred_element_type=jnp.float32)
    )
    return gate * jnp.einsum(
        "cji,cd->ijd", tri_normed, out_weight, preferred_element_type=jnp.float32
    )


def on_device(pair_act, block_mask, *weights):
    rows, cols = pair_act.shape[:2]
    blocks = block_mask.shape[0]
    fits = rows == 2 * LANES and cols == SUB and C // lax.axis_size("wide") == 4 and blocks == 4
    if lax.axis_size("narrow") > 1 or not fits:
        return plain_on_device(pair_act, block_mask, *weights)
    return kernels_on_device(pair_act, block_mask, *weights)


def solution(mesh):
    return jax.shard_map(
        on_device,
        mesh=mesh,
        in_specs=(P("narrow", "wide", None), P(), P(), P(), P(), P()),
        out_specs=P("narrow", "wide", None),
        check_vma=False,
    )
```

```python
import functools

import jax
import jax.numpy as jnp
from jax import lax
from jax.experimental import pallas as pl
from jax.experimental.pallas import tpu as pltpu
from jax.sharding import PartitionSpec as P

C = 128
BLOCK = 64
LANES = 128
SUB = 8


def layer_norm(values, axis):
    centre = jnp.mean(values, axis=axis, keepdims=True)
    spread = jnp.mean(jnp.square(values - centre), axis=axis, keepdims=True)
    return (values - centre) * lax.rsqrt(spread + 1e-05)


def swap_halves(values):
    flat = values.reshape(-1, LANES)
    return pltpu.roll(flat, LANES // 2, 1).reshape(values.shape)


def pack(low, high):
    lane = lax.broadcasted_iota(jnp.int32, low.shape, low.ndim - 1)
    return jnp.where(lane < LANES // 2, low, swap_halves(high))


def window_start(windowed):
    if not windowed:
        return 0
    return jnp.where(lax.axis_index("wide") * SUB < 3 * BLOCK, 0, BLOCK)


def chunks_of(rows):
    return ((0, LANES), (LANES, rows - LANES))


def sigmoid(values):
    return 0.5 * jnp.tanh(0.5 * values) + 0.5


def project_kernel(mask_hbm, x_hbm, wl_hbm, wr_hbm, *refs):
    whole_ref, window_ref, normed_ref, cut_ref, mask_ref, x_ref, w_ref, edge, sems = refs
    wide = whole_ref.shape[0]
    tokens = x_ref.shape[0] // SUB
    copies = [
        pltpu.make_async_copy(mask_hbm, mask_ref, sems.at[0]),
        pltpu.make_async_copy(wl_hbm, w_ref.at[0], sems.at[1]),
        pltpu.make_async_copy(wr_hbm, w_ref.at[1], sems.at[2]),
    ]
    for index in range(2):
        part = pl.ds(index * LANES * SUB, LANES * SUB)
        copies.append(pltpu.make_async_copy(x_hbm.at[part], x_ref.at[part], sems.at[3 + index]))
    for copy in copies:
        copy.start()
    copies[0].wait()
    cut = mask_ref[0, 3] == 0
    cut_ref[0] = cut.astype(jnp.int32)
    column_block = lax.axis_index("wide") * SUB // BLOCK
    kept = [mask_ref[block, column_block].astype(jnp.float32) for block in range(mask_hbm.shape[0])]
    copies[1].wait()
    copies[2].wait()
    weights = jnp.concatenate([w_ref[0].T, w_ref[1].T], axis=0)

    def project(windowed, send_ref):
        first = window_start(windowed)
        row_block = (first + lax.broadcasted_iota(jnp.int32, (1, 2 * LANES), 1)) // BLOCK
        mask = jnp.zeros((1, 2 * LANES), jnp.float32)
        for block, value in enumerate(kept):
            mask = jnp.where(row_block == block, value, mask)
        if windowed:
            copies[3].wait()
            copies[4].wait()
        chunks = chunks_of(3 * BLOCK if windowed else tokens)
        for index, (low, count) in enumerate(chunks):
            if not windowed:
                copies[3 + index].wait()
            group = 2 * LANES // count
            chunk_mask = jnp.concatenate([mask[:, low : low + count]] * group, axis=1)
            base = pl.multiple_of((first + low) * SUB, SUB)
            for start in range(0, SUB, group):
                x = [x_ref[pl.ds(base + start + k, count, stride=SUB), :] for k in range(group)]
                normed = layer_norm(jnp.concatenate(x, axis=0), 1).astype(jnp.bfloat16)
                for k in range(group):
                    normed_ref[start + k, low : low + count, :] = normed[k * count : (k + 1) * count]
                mixed = lax.dot_general(
                    weights, normed, (((1,), (1,)), ((), ())), preferred_element_type=jnp.float32
                )
                for side in range(2):
                    gate = mixed[2 * side * C : (2 * side + 1) * C]
                    value = mixed[(2 * side + 1) * C : (2 * side + 2) * C]
                    proj = sigmoid(gate) * value * chunk_mask
                    for k in range(group):
                        at = k * count // LANES * LANES
                        piece = proj[:, at : at + LANES]
                        if k * count % LANES:
                            piece = swap_halves(piece)
                        edge[side, index, pl.ds(start + k, C, stride=SUB), :] = piece
        part = C // wide * SUB
        low = 0
        for side in range(2):
            for index, (_, count) in enumerate(chunks):
                values = edge[side, index].reshape(wide, part, LANES)
                if count < LANES:
                    values = pack(values[:, : part // 2], values[:, part // 2 :])
                send_ref[:, low : low + values.shape[1], :] = values.astype(jnp.bfloat16)
                low += values.shape[1]

    pl.when(cut)(lambda: project(True, window_ref))
    pl.when(jnp.logical_not(cut))(lambda: project(False, whole_ref))


def triangle_kernel(windowed, recv_ref, send_ref):
    wide = recv_ref.shape[0]
    per_device = C // wide
    part = per_device * SUB
    tokens = wide * SUB
    half = per_device // 2

    def load(side, channel):
        parts = []
        for index in range(2):
            start = side * send_ref.shape[1] + index * part
            swap = windowed and index == 1 and channel >= half
            at = start + (channel - half if swap else channel) * SUB
            pair = recv_ref[:, at : at + 2 * SUB, :].astype(jnp.float32)
            if swap:
                pair = swap_halves(pair)
            parts.append([
                pair[:, low : low + SUB].reshape(tokens, LANES).astype(jnp.bfloat16)
                for low in (0, SUB)
            ])
        return [jnp.concatenate([p[n] for p in parts], axis=1) for n in range(2)]

    def product(right, left):
        return lax.dot_general(
            right, left, (((0,), (0,)), ((), ())), preferred_element_type=jnp.float32
        )

    sums = []
    for channel in range(0, per_device, 2):
        for left, right in zip(load(0, channel), load(1, channel)):
            if windowed:
                cut = 3 * BLOCK
                above = product(right[:cut], left[:cut])[:cut]
                below = product(right[cut:, LANES:], left[cut:])[: tokens - cut]
                sums.append(jnp.concatenate([above, below], axis=0))
            else:
                sums.append(product(right, left))
    first = [s[:, :LANES] for s in sums]
    second = [s[:, LANES:] for s in sums]
    if windowed:
        second = [pack(second[c], second[c + half]) for c in range(half)]
    start = 0
    for channels in (first, second):
        for channel in range(0, len(channels), 2):
            pair = [channels[channel + n].reshape(wide, SUB, LANES) for n in range(2)]
            pair = jnp.concatenate(pair, axis=1).astype(jnp.bfloat16)
            send_ref[:, start : start + 2 * SUB, :] = pair
            start += 2 * SUB


def gate_kernel(windowed, normed_ref, wg_ref, gate_ref):
    rows = 3 * BLOCK if windowed else normed_ref.shape[1]
    for j in range(SUB):
        mixed = jnp.dot(normed_ref[j, :rows, :], wg_ref[...], preferred_element_type=jnp.float32)
        gate_ref[j, :rows, :] = sigmoid(mixed)


def update_kernel(windowed, recv_ref, gate_ref, wo_ref, out_hbm, tri, out_ref, sems):
    wide = recv_ref.shape[0]
    part = C // wide * SUB
    rows = 3 * BLOCK if windowed else gate_ref.shape[1]
    chunks = chunks_of(rows)
    first = window_start(windowed)
    copies = []
    if windowed:
        rest = out_hbm.shape[0] - rows * SUB
        to = pl.multiple_of(jnp.where(first == 0, rows, 0) * SUB, SUB)
        out_ref[rows * SUB :, :] = jnp.zeros((rest, C), jnp.float32)
        copies.append(
            pltpu.make_async_copy(
                out_ref.at[pl.ds(rows * SUB, rest)], out_hbm.at[pl.ds(to, rest)], sems.at[2]
            )
        )
        copies[0].start()
    for index, (low, count) in enumerate(chunks):
        if count < LANES:
            sums = recv_ref[:, part:, :].astype(jnp.float32)
            sums = jnp.concatenate([sums, swap_halves(sums)], axis=1)
        else:
            sums = recv_ref[:, index * part : (index + 1) * part, :].astype(jnp.float32)
        tri[index] = layer_norm(sums.reshape(C, SUB, LANES), 0).reshape(C * SUB, LANES)
        for j in range(SUB):
            tri_normed = tri[index, pl.ds(j, C, stride=SUB), :].astype(jnp.bfloat16)
            mixed = lax.dot_general(
                tri_normed, wo_ref[...], (((0,), (0,)), ((), ())), preferred_element_type=jnp.float32
            )
            gate = gate_ref[j, low : low + count, :]
            out_ref[pl.ds(low * SUB + j, count, stride=SUB), :] = gate * mixed[:count]
        to = pl.multiple_of((first + low) * SUB, SUB)
        copies.append(
            pltpu.make_async_copy(
                out_ref.at[pl.ds(low * SUB, count * SUB)],
                out_hbm.at[pl.ds(to, count * SUB)],
                sems.at[index],
            )
        )
        copies[-1].start()
    for copy in copies:
        copy.wait()


HBM = pl.BlockSpec(memory_space=pltpu.HBM)
VMEM = pl.BlockSpec(memory_space=pltpu.VMEM)
PARAMS = pltpu.CompilerParams(vmem_limit_bytes=48 * 1024 * 1024)


def in_hbm(array):
    return pltpu.with_memory_space_constraint(array, pltpu.HBM)


def exchange(array):
    return lax.all_to_all(array, "wide", split_axis=0, concat_axis=0, tiled=True)


def after_projection(windowed, whole, window, normed, gate_weight, out_weight):
    send = window if windowed else whole
    wide, both, _ = send.shape
    tokens = normed.shape[1]
    gate = pl.pallas_call(
        functools.partial(gate_kernel, windowed),
        out_shape=jax.ShapeDtypeStruct(normed.shape, jnp.float32),
        in_specs=[VMEM] * 2,
        out_specs=VMEM,
        compiler_params=PARAMS,
        cost_estimate=pl.CostEstimate(
            flops=2 * tokens * SUB * C * C, bytes_accessed=6 * tokens * SUB * C, transcendentals=tokens * SUB * C
        ),
        name="gate",
    )(normed, gate_weight)
    back = pl.pallas_call(
        functools.partial(triangle_kernel, windowed),
        out_shape=jax.ShapeDtypeStruct((wide, both // 2, LANES), jnp.bfloat16),
        in_specs=[VMEM],
        out_specs=VMEM,
        compiler_params=PARAMS,
        name="triangle",
    )(exchange(send))
    return pl.pallas_call(
        functools.partial(update_kernel, windowed),
        out_shape=pltpu.HBM((tokens * SUB, C), jnp.float32),
        in_specs=[VMEM] * 3,
        out_specs=HBM,
        scratch_shapes=[
            pltpu.VMEM((2, C * SUB, LANES), jnp.float32),
            pltpu.VMEM((tokens * SUB, C), jnp.float32),
            pltpu.SemaphoreType.DMA((3,)),
        ],
        compiler_params=PARAMS,
        name="update",
    )(exchange(back), gate, out_weight)


def kernels_on_device(pair_act, block_mask, left_weight, right_weight, gate_weight, out_weight):
    tokens = pair_act.shape[0]
    wide = lax.axis_size("wide")
    both = lambda rows: 2 * rows * (C // wide) * SUB // LANES
    whole, window, normed, cut = pl.pallas_call(
        project_kernel,
        out_shape=(
            jax.ShapeDtypeStruct((wide, both(tokens), LANES), jnp.bfloat16),
            jax.ShapeDtypeStruct((wide, both(3 * BLOCK), LANES), jnp.bfloat16),
            jax.ShapeDtypeStruct((SUB, tokens, C), jnp.bfloat16),
            pltpu.SMEM((1,), jnp.int32),
        ),
        in_specs=[HBM] * 4,
        out_specs=(VMEM, VMEM, VMEM, pl.BlockSpec(memory_space=pltpu.SMEM)),
        scratch_shapes=[
            pltpu.SMEM(block_mask.shape, jnp.int32),
            pltpu.VMEM((tokens * SUB, C), jnp.float32),
            pltpu.VMEM((2, C, 2 * C), jnp.bfloat16),
            pltpu.VMEM((2, 2, C * SUB, LANES), jnp.float32),
            pltpu.SemaphoreType.DMA((5,)),
        ],
        compiler_params=PARAMS,
        name="project",
    )(
        in_hbm(block_mask),
        in_hbm(pair_act.reshape(tokens * SUB, C)),
        in_hbm(left_weight),
        in_hbm(right_weight),
    )
    update = lax.switch(
        cut[0],
        [functools.partial(after_projection, windowed) for windowed in (False, True)],
        whole,
        window,
        normed,
        gate_weight,
        out_weight,
    )
    return update.reshape(tokens, SUB, C)


def plain_on_device(pair_act, block_mask, left_weight, right_weight, gate_weight, out_weight):
    tile_rows = pair_act.shape[0]
    tile_cols = pair_act.shape[1]
    wide = lax.axis_size("wide")
    narrow = lax.axis_size("narrow")
    per_device = C // wide
    row_ids = lax.axis_index("narrow") * tile_rows + jnp.arange(tile_rows, dtype=jnp.int32)
    col_ids = lax.axis_index("wide") * tile_cols + jnp.arange(tile_cols, dtype=jnp.int32)
    block_ids = jnp.arange(block_mask.shape[0], dtype=jnp.int32)
    row_hot = (row_ids[:, None] // BLOCK == block_ids[None, :]).astype(jnp.float32)
    col_hot = (col_ids[:, None] // BLOCK == block_ids[None, :]).astype(jnp.float32)
    tile_mask = jnp.dot(jnp.dot(row_hot, block_mask.astype(jnp.float32)), col_hot.T).T
    normed = layer_norm(pair_act, -1).astype(jnp.bfloat16)

    def edges(weight):
        mixed = jnp.einsum("cd,ikc->dki", weight, normed, preferred_element_type=jnp.float32)
        proj = jax.nn.sigmoid(mixed[:C]) * mixed[C:] * tile_mask[None]
        return proj.astype(jnp.bfloat16).reshape(wide, per_device, tile_cols, tile_rows)

    send = jnp.stack([edges(left_weight), edges(right_weight)], axis=1)
    recv = lax.all_to_all(send, "wide", split_axis=0, concat_axis=0, tiled=True)
    left, right = recv[:, 0], recv[:, 1]
    if narrow > 1:
        right = lax.all_gather(right, "narrow", axis=3, tiled=True)
    tri = jnp.einsum("sckj,scki->cji", right, left, preferred_element_type=jnp.float32)
    back = tri.astype(jnp.bfloat16).reshape(per_device, wide, tile_cols, tile_rows)
    back = jnp.transpose(back, (1, 0, 2, 3))
    tri = lax.all_to_all(back, "wide", split_axis=0, concat_axis=0, tiled=True)
    tri = tri.reshape(C, tile_cols, tile_rows).astype(jnp.float32)
    tri_normed = layer_norm(tri, 0).astype(jnp.bfloat16)
    gate = jax.nn.sigmoid(
        jnp.einsum("ikc,cd->ikd", normed, gate_weight, preferred_element_type=jnp.float32)
    )
    return gate * jnp.einsum(
        "cji,cd->ijd", tri_normed, out_weight, preferred_element_type=jnp.float32
    )


def on_device(pair_act, block_mask, *weights):
    rows, cols = pair_act.shape[:2]
    blocks = block_mask.shape[0]
    fits = rows == 2 * LANES and cols == SUB and C // lax.axis_size("wide") == 4 and blocks == 4
    if lax.axis_size("narrow") > 1 or not fits:
        return plain_on_device(pair_act, block_mask, *weights)
    return kernels_on_device(pair_act, block_mask, *weights)


def solution(mesh):
    return jax.shard_map(
        on_device,
        mesh=mesh,
        in_specs=(P("narrow", "wide", None), P(), P(), P(), P(), P()),
        out_specs=P("narrow", "wide", None),
        check_vma=False,
    )
```

```python
import functools

import jax
import jax.numpy as jnp
from jax import lax
from jax.experimental import pallas as pl
from jax.experimental.pallas import tpu as pltpu
from jax.sharding import PartitionSpec as P

C = 128
BLOCK = 64
LANES = 128
SUB = 8


def layer_norm(values, axis):
    centre = jnp.mean(values, axis=axis, keepdims=True)
    spread = jnp.mean(jnp.square(values - centre), axis=axis, keepdims=True)
    return (values - centre) * lax.rsqrt(spread + 1e-05)


def swap_halves(values):
    flat = values.reshape(-1, LANES)
    return pltpu.roll(flat, LANES // 2, 1).reshape(values.shape)


def pack(low, high):
    lane = lax.broadcasted_iota(jnp.int32, low.shape, low.ndim - 1)
    return jnp.where(lane < LANES // 2, low, swap_halves(high))


def window_start(windowed):
    if not windowed:
        return 0
    return jnp.where(lax.axis_index("wide") * SUB < 3 * BLOCK, 0, BLOCK)


def chunks_of(rows):
    return ((0, LANES), (LANES, rows - LANES))


def sigmoid(values):
    return 0.5 * jnp.tanh(0.5 * values) + 0.5


def project_kernel(mask_hbm, x_hbm, wl_hbm, wr_hbm, *refs):
    whole_ref, window_ref, normed_ref, cut_ref, mask_ref, x_ref, w_ref, edge, sems = refs
    wide = whole_ref.shape[0]
    tokens = x_ref.shape[0] // SUB
    copies = [
        pltpu.make_async_copy(mask_hbm, mask_ref, sems.at[0]),
        pltpu.make_async_copy(wl_hbm, w_ref.at[0], sems.at[1]),
        pltpu.make_async_copy(wr_hbm, w_ref.at[1], sems.at[2]),
    ]
    for index in range(2):
        part = pl.ds(index * LANES * SUB, LANES * SUB)
        copies.append(pltpu.make_async_copy(x_hbm.at[part], x_ref.at[part], sems.at[3 + index]))
    for copy in copies:
        copy.start()
    copies[0].wait()
    cut = mask_ref[0, 3] == 0
    cut_ref[0] = cut.astype(jnp.int32)
    column_block = lax.axis_index("wide") * SUB // BLOCK
    kept = [mask_ref[block, column_block].astype(jnp.float32) for block in range(mask_hbm.shape[0])]
    copies[1].wait()
    copies[2].wait()
    weights = jnp.concatenate([w_ref[0].T, w_ref[1].T], axis=0)

    def project(windowed, send_ref):
        first = window_start(windowed)
        row_block = (first + lax.broadcasted_iota(jnp.int32, (1, 2 * LANES), 1)) // BLOCK
        mask = jnp.zeros((1, 2 * LANES), jnp.float32)
        for block, value in enumerate(kept):
            mask = jnp.where(row_block == block, value, mask)
        if windowed:
            copies[3].wait()
            copies[4].wait()
        chunks = chunks_of(3 * BLOCK if windowed else tokens)
        for index, (low, count) in enumerate(chunks):
            if not windowed:
                copies[3 + index].wait()
            base = pl.multiple_of((first + low) * SUB, SUB)
            x = [x_ref[pl.ds(base + k, count, stride=SUB), :] for k in range(SUB)]
            normed = layer_norm(jnp.concatenate(x, axis=0), 1).astype(jnp.bfloat16)
            for k in range(SUB):
                normed_ref[k, low : low + count, :] = normed[k * count : (k + 1) * count]
            mixed = lax.dot_general(
                weights, normed, (((1,), (1,)), ((), ())), preferred_element_type=jnp.float32
            )
            chunk_mask = jnp.concatenate([mask[:, low : low + count]] * (LANES // count), axis=1)
            for side in range(2):
                for at in range(0, count * SUB, LANES):
                    gate = mixed[2 * side * C : (2 * side + 1) * C, at : at + LANES]
                    value = mixed[(2 * side + 1) * C : (2 * side + 2) * C, at : at + LANES]
                    proj = sigmoid(gate) * value * chunk_mask
                    for k in range(at // count, (at + LANES) // count):
                        piece = swap_halves(proj) if k * count % LANES else proj
                        edge[side, index, pl.ds(k, C, stride=SUB), :] = piece
        part = C // wide * SUB
        low = 0
        for side in range(2):
            for index, (_, count) in enumerate(chunks):
                values = edge[side, index].reshape(wide, part, LANES)
                if count < LANES:
                    values = pack(values[:, : part // 2], values[:, part // 2 :])
                send_ref[:, low : low + values.shape[1], :] = values.astype(jnp.bfloat16)
                low += values.shape[1]

    pl.when(cut)(lambda: project(True, window_ref))
    pl.when(jnp.logical_not(cut))(lambda: project(False, whole_ref))


def triangle_kernel(windowed, recv_ref, send_ref):
    wide = recv_ref.shape[0]
    per_device = C // wide
    part = per_device * SUB
    tokens = wide * SUB
    half = per_device // 2

    def load(side, channel):
        parts = []
        for index in range(2):
            start = side * send_ref.shape[1] + index * part
            swap = windowed and index == 1 and channel >= half
            at = start + (channel - half if swap else channel) * SUB
            pair = recv_ref[:, at : at + 2 * SUB, :].astype(jnp.float32)
            if swap:
                pair = swap_halves(pair)
            parts.append([
                pair[:, low : low + SUB].reshape(tokens, LANES).astype(jnp.bfloat16)
                for low in (0, SUB)
            ])
        return [jnp.concatenate([p[n] for p in parts], axis=1) for n in range(2)]

    def product(right, left):
        return lax.dot_general(
            right, left, (((0,), (0,)), ((), ())), preferred_element_type=jnp.float32
        )

    sums = []
    for channel in range(0, per_device, 2):
        for left, right in zip(load(0, channel), load(1, channel)):
            if windowed:
                cut = 3 * BLOCK
                above = product(right[:cut], left[:cut])[:cut]
                below = product(right[cut:, LANES:], left[cut:])[: tokens - cut]
                sums.append(jnp.concatenate([above, below], axis=0))
            else:
                sums.append(product(right, left))
    first = [s[:, :LANES] for s in sums]
    second = [s[:, LANES:] for s in sums]
    if windowed:
        second = [pack(second[c], second[c + half]) for c in range(half)]
    start = 0
    for channels in (first, second):
        for channel in range(0, len(channels), 2):
            pair = [channels[channel + n].reshape(wide, SUB, LANES) for n in range(2)]
            pair = jnp.concatenate(pair, axis=1).astype(jnp.bfloat16)
            send_ref[:, start : start + 2 * SUB, :] = pair
            start += 2 * SUB


def update_kernel(windowed, recv_ref, normed_ref, wg_ref, wo_ref, out_hbm, tri, out_ref, sems):
    wide = recv_ref.shape[0]
    part = C // wide * SUB
    rows = 3 * BLOCK if windowed else normed_ref.shape[1]
    chunks = chunks_of(rows)
    first = window_start(windowed)
    copies = []
    if windowed:
        rest = out_hbm.shape[0] - rows * SUB
        to = pl.multiple_of(jnp.where(first == 0, rows, 0) * SUB, SUB)
        out_ref[rows * SUB :, :] = jnp.zeros((rest, C), jnp.float32)
        copies.append(
            pltpu.make_async_copy(
                out_ref.at[pl.ds(rows * SUB, rest)], out_hbm.at[pl.ds(to, rest)], sems.at[2]
            )
        )
        copies[0].start()
    for index, (low, count) in enumerate(chunks):
        if count < LANES:
            sums = recv_ref[:, part:, :].astype(jnp.float32)
            sums = jnp.concatenate([sums, swap_halves(sums)], axis=1)
        else:
            sums = recv_ref[:, index * part : (index + 1) * part, :].astype(jnp.float32)
        tri[index] = layer_norm(sums.reshape(C, SUB, LANES), 0).reshape(C * SUB, LANES)
        tri_normed = jnp.concatenate(
            [tri[index, pl.ds(j, C, stride=SUB), :].astype(jnp.bfloat16) for j in range(SUB)], axis=1
        )
        mixed = lax.dot_general(
            tri_normed, wo_ref[...], (((0,), (0,)), ((), ())), preferred_element_type=jnp.float32
        )
        normed = jnp.concatenate([normed_ref[j, low : low + count, :] for j in range(SUB)], axis=0)
        gate = sigmoid(jnp.dot(normed, wg_ref[...], preferred_element_type=jnp.float32))
        for j in range(SUB):
            out_ref[pl.ds(low * SUB + j, count, stride=SUB), :] = (
                gate[j * count : (j + 1) * count] * mixed[j * LANES : j * LANES + count]
            )
        to = pl.multiple_of((first + low) * SUB, SUB)
        copies.append(
            pltpu.make_async_copy(
                out_ref.at[pl.ds(low * SUB, count * SUB)],
                out_hbm.at[pl.ds(to, count * SUB)],
                sems.at[index],
            )
        )
        copies[-1].start()
    for copy in copies:
        copy.wait()


HBM = pl.BlockSpec(memory_space=pltpu.HBM)
VMEM = pl.BlockSpec(memory_space=pltpu.VMEM)
PARAMS = pltpu.CompilerParams(vmem_limit_bytes=48 * 1024 * 1024)


def in_hbm(array):
    return pltpu.with_memory_space_constraint(array, pltpu.HBM)


def exchange(array):
    return lax.all_to_all(array, "wide", split_axis=0, concat_axis=0, tiled=True)


def after_projection(windowed, whole, window, normed, gate_weight, out_weight):
    send = window if windowed else whole
    wide, both, _ = send.shape
    tokens = normed.shape[1]
    back = pl.pallas_call(
        functools.partial(triangle_kernel, windowed),
        out_shape=jax.ShapeDtypeStruct((wide, both // 2, LANES), jnp.bfloat16),
        in_specs=[VMEM],
        out_specs=VMEM,
        compiler_params=PARAMS,
        name="triangle",
    )(exchange(send))
    return pl.pallas_call(
        functools.partial(update_kernel, windowed),
        out_shape=pltpu.HBM((tokens * SUB, C), jnp.float32),
        in_specs=[VMEM] * 4,
        out_specs=HBM,
        scratch_shapes=[
            pltpu.VMEM((2, C * SUB, LANES), jnp.float32),
            pltpu.VMEM((tokens * SUB, C), jnp.float32),
            pltpu.SemaphoreType.DMA((3,)),
        ],
        compiler_params=PARAMS,
        name="update",
    )(exchange(back), normed, gate_weight, out_weight)


def kernels_on_device(pair_act, block_mask, left_weight, right_weight, gate_weight, out_weight):
    tokens = pair_act.shape[0]
    wide = lax.axis_size("wide")
    both = lambda rows: 2 * rows * (C // wide) * SUB // LANES
    whole, window, normed, cut = pl.pallas_call(
        project_kernel,
        out_shape=(
            jax.ShapeDtypeStruct((wide, both(tokens), LANES), jnp.bfloat16),
            jax.ShapeDtypeStruct((wide, both(3 * BLOCK), LANES), jnp.bfloat16),
            jax.ShapeDtypeStruct((SUB, tokens, C), jnp.bfloat16),
            pltpu.SMEM((1,), jnp.int32),
        ),
        in_specs=[HBM] * 4,
        out_specs=(VMEM, VMEM, VMEM, pl.BlockSpec(memory_space=pltpu.SMEM)),
        scratch_shapes=[
            pltpu.SMEM(block_mask.shape, jnp.int32),
            pltpu.VMEM((tokens * SUB, C), jnp.float32),
            pltpu.VMEM((2, C, 2 * C), jnp.bfloat16),
            pltpu.VMEM((2, 2, C * SUB, LANES), jnp.float32),
            pltpu.SemaphoreType.DMA((5,)),
        ],
        compiler_params=PARAMS,
        name="project",
    )(
        in_hbm(block_mask),
        in_hbm(pair_act.reshape(tokens * SUB, C)),
        in_hbm(left_weight),
        in_hbm(right_weight),
    )
    update = lax.switch(
        cut[0],
        [functools.partial(after_projection, windowed) for windowed in (False, True)],
        whole,
        window,
        normed,
        gate_weight,
        out_weight,
    )
    return update.reshape(tokens, SUB, C)


def plain_on_device(pair_act, block_mask, left_weight, right_weight, gate_weight, out_weight):
    tile_rows = pair_act.shape[0]
    tile_cols = pair_act.shape[1]
    wide = lax.axis_size("wide")
    narrow = lax.axis_size("narrow")
    per_device = C // wide
    row_ids = lax.axis_index("narrow") * tile_rows + jnp.arange(tile_rows, dtype=jnp.int32)
    col_ids = lax.axis_index("wide") * tile_cols + jnp.arange(tile_cols, dtype=jnp.int32)
    block_ids = jnp.arange(block_mask.shape[0], dtype=jnp.int32)
    row_hot = (row_ids[:, None] // BLOCK == block_ids[None, :]).astype(jnp.float32)
    col_hot = (col_ids[:, None] // BLOCK == block_ids[None, :]).astype(jnp.float32)
    tile_mask = jnp.dot(jnp.dot(row_hot, block_mask.astype(jnp.float32)), col_hot.T).T
    normed = layer_norm(pair_act, -1).astype(jnp.bfloat16)

    def edges(weight):
        mixed = jnp.einsum("cd,ikc->dki", weight, normed, preferred_element_type=jnp.float32)
        proj = jax.nn.sigmoid(mixed[:C]) * mixed[C:] * tile_mask[None]
        return proj.astype(jnp.bfloat16).reshape(wide, per_device, tile_cols, tile_rows)

    send = jnp.stack([edges(left_weight), edges(right_weight)], axis=1)
    recv = lax.all_to_all(send, "wide", split_axis=0, concat_axis=0, tiled=True)
    left, right = recv[:, 0], recv[:, 1]
    if narrow > 1:
        right = lax.all_gather(right, "narrow", axis=3, tiled=True)
    tri = jnp.einsum("sckj,scki->cji", right, left, preferred_element_type=jnp.float32)
    back = tri.astype(jnp.bfloat16).reshape(per_device, wide, tile_cols, tile_rows)
    back = jnp.transpose(back, (1, 0, 2, 3))
    tri = lax.all_to_all(back, "wide", split_axis=0, concat_axis=0, tiled=True)
    tri = tri.reshape(C, tile_cols, tile_rows).astype(jnp.float32)
    tri_normed = layer_norm(tri, 0).astype(jnp.bfloat16)
    gate = jax.nn.sigmoid(
        jnp.einsum("ikc,cd->ikd", normed, gate_weight, preferred_element_type=jnp.float32)
    )
    return gate * jnp.einsum(
        "cji,cd->ijd", tri_normed, out_weight, preferred_element_type=jnp.float32
    )


def on_device(pair_act, block_mask, *weights):
    rows, cols = pair_act.shape[:2]
    blocks = block_mask.shape[0]
    fits = rows == 2 * LANES and cols == SUB and C // lax.axis_size("wide") == 4 and blocks == 4
    if lax.axis_size("narrow") > 1 or not fits:
        return plain_on_device(pair_act, block_mask, *weights)
    return kernels_on_device(pair_act, block_mask, *weights)


def solution(mesh):
    return jax.shard_map(
        on_device,
        mesh=mesh,
        in_specs=(P("narrow", "wide", None), P(), P(), P(), P(), P()),
        out_specs=P("narrow", "wide", None),
        check_vma=False,
    )
```

```python
import functools

import jax
import jax.numpy as jnp
from jax import lax
from jax.experimental import pallas as pl
from jax.experimental.pallas import tpu as pltpu
from jax.sharding import PartitionSpec as P

C = 128
BLOCK = 64
LANES = 128
SUB = 8
PARTS = 2


def layer_norm(values, axis):
    centre = jnp.mean(values, axis=axis, keepdims=True)
    spread = jnp.mean(jnp.square(values - centre), axis=axis, keepdims=True)
    return (values - centre) * lax.rsqrt(spread + 1e-05)


def swap_halves(values):
    flat = values.reshape(-1, LANES)
    return pltpu.roll(flat, LANES // 2, 1).reshape(values.shape)


def pack(low, high):
    lane = lax.broadcasted_iota(jnp.int32, low.shape, low.ndim - 1)
    return jnp.where(lane < LANES // 2, low, swap_halves(high))


def window_start(windowed):
    if not windowed:
        return 0
    return jnp.where(lax.axis_index("wide") * SUB < 3 * BLOCK, 0, BLOCK)


def chunks_of(rows):
    return ((0, LANES), (LANES, rows - LANES))


def project_kernel(mask_hbm, x_hbm, wl_hbm, wr_hbm, *refs):
    whole_ref, window_ref, normed_ref, cut_ref, mask_ref, x_ref, w_ref, edge, sems = refs
    group_size = whole_ref.shape[0]
    tokens = x_ref.shape[0] // SUB
    copies = [
        pltpu.make_async_copy(mask_hbm, mask_ref, sems.at[0]),
        pltpu.make_async_copy(wl_hbm, w_ref.at[0], sems.at[1]),
        pltpu.make_async_copy(wr_hbm, w_ref.at[1], sems.at[2]),
    ]
    for index in range(2):
        part = pl.ds(index * LANES * SUB, LANES * SUB)
        copies.append(pltpu.make_async_copy(x_hbm.at[part], x_ref.at[part], sems.at[3 + index]))
    for copy in copies:
        copy.start()
    copies[0].wait()
    cut = mask_ref[0, 3] == 0
    cut_ref[0] = cut.astype(jnp.int32)
    column_block = lax.axis_index("wide") * SUB // BLOCK
    kept = [mask_ref[block, column_block].astype(jnp.float32) for block in range(mask_hbm.shape[0])]
    copies[1].wait()
    copies[2].wait()
    weights = jnp.concatenate([w_ref[0].T, w_ref[1].T], axis=0)

    def project(windowed, send_ref):
        first = window_start(windowed)
        row_block = (first + lax.broadcasted_iota(jnp.int32, (1, 2 * LANES), 1)) // BLOCK
        mask = jnp.zeros((1, 2 * LANES), jnp.float32)
        for block, value in enumerate(kept):
            mask = jnp.where(row_block == block, value, mask)
        if windowed:
            copies[3].wait()
            copies[4].wait()
        chunks = chunks_of(3 * BLOCK if windowed else tokens)
        for index, (low, count) in enumerate(chunks):
            if not windowed:
                copies[3 + index].wait()
            group = 2 * LANES // count
            chunk_mask = jnp.concatenate([mask[:, low : low + count]] * group, axis=1)
            base = pl.multiple_of((first + low) * SUB, SUB)
            for start in range(0, SUB, group):
                x = [x_ref[pl.ds(base + start + k, count, stride=SUB), :] for k in range(group)]
                normed = layer_norm(jnp.concatenate(x, axis=0), 1).astype(jnp.bfloat16)
                for k in range(group):
                    normed_ref[start + k, low : low + count, :] = normed[k * count : (k + 1) * count]
                mixed = lax.dot_general(
                    weights, normed, (((1,), (1,)), ((), ())), preferred_element_type=jnp.float32
                )
                for side in range(2):
                    gate = mixed[2 * side * C : (2 * side + 1) * C]
                    value = mixed[(2 * side + 1) * C : (2 * side + 2) * C]
                    proj = jax.nn.sigmoid(gate) * value * chunk_mask
                    for k in range(group):
                        at = k * count // LANES * LANES
                        piece = proj[:, at : at + LANES]
                        if k * count % LANES:
                            piece = swap_halves(piece)
                        edge[side, index, pl.ds(start + k, C, stride=SUB), :] = piece
        part = C // group_size * SUB
        low = 0
        for side in range(2):
            for index, (_, count) in enumerate(chunks):
                values = edge[side, index].reshape(group_size, part, LANES)
                if count < LANES:
                    values = pack(values[:, : part // 2], values[:, part // 2 :])
                send_ref[:, low : low + values.shape[1], :] = values.astype(jnp.bfloat16)
                low += values.shape[1]

    pl.when(cut)(lambda: project(True, window_ref))
    pl.when(jnp.logical_not(cut))(lambda: project(False, whole_ref))


def triangle_kernel(windowed, recv_ref, send_ref):
    group_size = recv_ref.shape[0]
    wide = send_ref.shape[0]
    per_device = C // group_size
    part = per_device * SUB
    columns = group_size * SUB
    half = per_device // 2

    def load(side, channel):
        parts = []
        for index in range(2):
            start = side * send_ref.shape[1] + index * part
            swap = windowed and index == 1 and channel >= half
            at = start + (channel - half if swap else channel) * SUB
            pair = recv_ref[:, at : at + 2 * SUB, :].astype(jnp.float32)
            if swap:
                pair = swap_halves(pair)
            parts.append([
                pair[:, low : low + SUB].reshape(columns, LANES).astype(jnp.bfloat16)
                for low in (0, SUB)
            ])
        return [jnp.concatenate([p[n] for p in parts], axis=1) for n in range(2)]

    def product(right, left):
        return lax.dot_general(
            right, left, (((0,), (0,)), ((), ())), preferred_element_type=jnp.float32
        )

    cut = 3 * BLOCK
    columns_first = lax.axis_index("wide") // group_size * columns
    column = columns_first + lax.broadcasted_iota(jnp.int32, (columns, 1), 0)
    sums = []
    for channel in range(0, per_device, 2):
        for left, right in zip(load(0, channel), load(1, channel)):
            if windowed:
                above = product(right, jnp.where(column < cut, left, 0))[:cut]
                below = product(right[:, LANES:], jnp.where(column < cut, 0, left))
                sums.append(jnp.concatenate([above, below[: wide * SUB - cut]], axis=0))
            else:
                sums.append(product(right, left))
    first = [s[:, :LANES] for s in sums]
    second = [s[:, LANES:] for s in sums]
    if windowed:
        second = [pack(second[c], second[c + half]) for c in range(half)]
    start = 0
    for channels in (first, second):
        for channel in range(0, len(channels), 2):
            pair = [channels[channel + n].reshape(wide, SUB, LANES) for n in range(2)]
            pair = jnp.concatenate(pair, axis=1).astype(jnp.bfloat16)
            send_ref[:, start : start + 2 * SUB, :] = pair
            start += 2 * SUB


def update_kernel(windowed, recv_ref, normed_ref, wg_ref, wo_ref, out_hbm, tri, out_ref, sems):
    group_size = recv_ref.shape[0] // PARTS
    part = C // group_size * SUB
    rows = 3 * BLOCK if windowed else normed_ref.shape[1]
    chunks = chunks_of(rows)
    first = window_start(windowed)
    copies = []
    if windowed:
        rest = out_hbm.shape[0] - rows * SUB
        to = pl.multiple_of(jnp.where(first == 0, rows, 0) * SUB, SUB)
        out_ref[rows * SUB :, :] = jnp.zeros((rest, C), jnp.float32)
        copies.append(
            pltpu.make_async_copy(
                out_ref.at[pl.ds(rows * SUB, rest)], out_hbm.at[pl.ds(to, rest)], sems.at[2]
            )
        )
        copies[0].start()
    for index, (low, count) in enumerate(chunks):
        height = part * count // LANES
        sums = [
            recv_ref[n * group_size : (n + 1) * group_size, index * part : index * part + height, :]
            for n in range(PARTS)
        ]
        sums = sum(values.astype(jnp.float32) for values in sums)
        if count < LANES:
            sums = jnp.concatenate([sums, swap_halves(sums)], axis=1)
        tri[index] = layer_norm(sums.reshape(C, SUB, LANES), 0).reshape(C * SUB, LANES)
        for j in range(SUB):
            tri_normed = tri[index, pl.ds(j, C, stride=SUB), :].astype(jnp.bfloat16)
            mixed = lax.dot_general(
                tri_normed, wo_ref[...], (((0,), (0,)), ((), ())), preferred_element_type=jnp.float32
            )
            normed = normed_ref[j, low : low + count, :]
            gate = jax.nn.sigmoid(
                jnp.dot(normed, wg_ref[...], preferred_element_type=jnp.float32)
            )
            out_ref[pl.ds(low * SUB + j, count, stride=SUB), :] = gate * mixed[:count]
        to = pl.multiple_of((first + low) * SUB, SUB)
        copies.append(
            pltpu.make_async_copy(
                out_ref.at[pl.ds(low * SUB, count * SUB)],
                out_hbm.at[pl.ds(to, count * SUB)],
                sems.at[index],
            )
        )
        copies[-1].start()
    for copy in copies:
        copy.wait()


HBM = pl.BlockSpec(memory_space=pltpu.HBM)
VMEM = pl.BlockSpec(memory_space=pltpu.VMEM)
PARAMS = pltpu.CompilerParams(vmem_limit_bytes=48 * 1024 * 1024)


def in_hbm(array):
    return pltpu.with_memory_space_constraint(array, pltpu.HBM)


def exchange(array):
    wide, size = lax.axis_size("wide"), array.shape[0]
    groups = [list(range(first, first + size)) for first in range(0, wide, size)]
    return lax.all_to_all(
        array, "wide", split_axis=0, concat_axis=0, axis_index_groups=groups, tiled=True
    )


def after_projection(windowed, whole, window, normed, gate_weight, out_weight):
    send = window if windowed else whole
    group_size, both, _ = send.shape
    wide = group_size * PARTS
    tokens = normed.shape[1]
    back = pl.pallas_call(
        functools.partial(triangle_kernel, windowed),
        out_shape=jax.ShapeDtypeStruct((wide, both // 2, LANES), jnp.bfloat16),
        in_specs=[VMEM],
        out_specs=VMEM,
        compiler_params=PARAMS,
        name="triangle",
    )(exchange(send))
    return pl.pallas_call(
        functools.partial(update_kernel, windowed),
        out_shape=pltpu.HBM((tokens * SUB, C), jnp.float32),
        in_specs=[VMEM] * 4,
        out_specs=HBM,
        scratch_shapes=[
            pltpu.VMEM((2, C * SUB, LANES), jnp.float32),
            pltpu.VMEM((tokens * SUB, C), jnp.float32),
            pltpu.SemaphoreType.DMA((3,)),
        ],
        compiler_params=PARAMS,
        name="update",
    )(exchange(back), normed, gate_weight, out_weight)


def kernels_on_device(pair_act, block_mask, left_weight, right_weight, gate_weight, out_weight):
    tokens = pair_act.shape[0]
    wide = lax.axis_size("wide")
    group_size = wide // PARTS
    both = lambda rows: 2 * rows * (C // group_size) * SUB // LANES
    whole, window, normed, cut = pl.pallas_call(
        project_kernel,
        out_shape=(
            jax.ShapeDtypeStruct((group_size, both(tokens), LANES), jnp.bfloat16),
            jax.ShapeDtypeStruct((group_size, both(3 * BLOCK), LANES), jnp.bfloat16),
            jax.ShapeDtypeStruct((SUB, tokens, C), jnp.bfloat16),
            pltpu.SMEM((1,), jnp.int32),
        ),
        in_specs=[HBM] * 4,
        out_specs=(VMEM, VMEM, VMEM, pl.BlockSpec(memory_space=pltpu.SMEM)),
        scratch_shapes=[
            pltpu.SMEM(block_mask.shape, jnp.int32),
            pltpu.VMEM((tokens * SUB, C), jnp.float32),
            pltpu.VMEM((2, C, 2 * C), jnp.bfloat16),
            pltpu.VMEM((2, 2, C * SUB, LANES), jnp.float32),
            pltpu.SemaphoreType.DMA((5,)),
        ],
        compiler_params=PARAMS,
        name="project",
    )(
        in_hbm(block_mask),
        in_hbm(pair_act.reshape(tokens * SUB, C)),
        in_hbm(left_weight),
        in_hbm(right_weight),
    )
    update = lax.switch(
        cut[0],
        [functools.partial(after_projection, windowed) for windowed in (False, True)],
        whole,
        window,
        normed,
        gate_weight,
        out_weight,
    )
    return update.reshape(tokens, SUB, C)


def plain_on_device(pair_act, block_mask, left_weight, right_weight, gate_weight, out_weight):
    tile_rows = pair_act.shape[0]
    tile_cols = pair_act.shape[1]
    wide = lax.axis_size("wide")
    narrow = lax.axis_size("narrow")
    per_device = C // wide
    row_ids = lax.axis_index("narrow") * tile_rows + jnp.arange(tile_rows, dtype=jnp.int32)
    col_ids = lax.axis_index("wide") * tile_cols + jnp.arange(tile_cols, dtype=jnp.int32)
    block_ids = jnp.arange(block_mask.shape[0], dtype=jnp.int32)
    row_hot = (row_ids[:, None] // BLOCK == block_ids[None, :]).astype(jnp.float32)
    col_hot = (col_ids[:, None] // BLOCK == block_ids[None, :]).astype(jnp.float32)
    tile_mask = jnp.dot(jnp.dot(row_hot, block_mask.astype(jnp.float32)), col_hot.T).T
    normed = layer_norm(pair_act, -1).astype(jnp.bfloat16)

    def edges(weight):
        mixed = jnp.einsum("cd,ikc->dki", weight, normed, preferred_element_type=jnp.float32)
        proj = jax.nn.sigmoid(mixed[:C]) * mixed[C:] * tile_mask[None]
        return proj.astype(jnp.bfloat16).reshape(wide, per_device, tile_cols, tile_rows)

    send = jnp.stack([edges(left_weight), edges(right_weight)], axis=1)
    recv = lax.all_to_all(send, "wide", split_axis=0, concat_axis=0, tiled=True)
    left, right = recv[:, 0], recv[:, 1]
    if narrow > 1:
        right = lax.all_gather(right, "narrow", axis=3, tiled=True)
    tri = jnp.einsum("sckj,scki->cji", right, left, preferred_element_type=jnp.float32)
    back = tri.astype(jnp.bfloat16).reshape(per_device, wide, tile_cols, tile_rows)
    back = jnp.transpose(back, (1, 0, 2, 3))
    tri = lax.all_to_all(back, "wide", split_axis=0, concat_axis=0, tiled=True)
    tri = tri.reshape(C, tile_cols, tile_rows).astype(jnp.float32)
    tri_normed = layer_norm(tri, 0).astype(jnp.bfloat16)
    gate = jax.nn.sigmoid(
        jnp.einsum("ikc,cd->ikd", normed, gate_weight, preferred_element_type=jnp.float32)
    )
    return gate * jnp.einsum(
        "cji,cd->ijd", tri_normed, out_weight, preferred_element_type=jnp.float32
    )


def on_device(pair_act, block_mask, *weights):
    rows, cols = pair_act.shape[:2]
    blocks = block_mask.shape[0]
    fits = rows == 2 * LANES and cols == SUB and C // lax.axis_size("wide") == 4 and blocks == 4
    if lax.axis_size("narrow") > 1 or not fits:
        return plain_on_device(pair_act, block_mask, *weights)
    return kernels_on_device(pair_act, block_mask, *weights)


def solution(mesh):
    return jax.shard_map(
        on_device,
        mesh=mesh,
        in_specs=(P("narrow", "wide", None), P(), P(), P(), P(), P()),
        out_specs=P("narrow", "wide", None),
        check_vma=False,
    )
```

```python
import functools

import jax
import jax.numpy as jnp
from jax import lax
from jax.experimental import pallas as pl
from jax.experimental.pallas import tpu as pltpu
from jax.sharding import PartitionSpec as P

C = 128
BLOCK = 64
LANES = 128
SUB = 8
PARTS = 2


def layer_norm(values, axis):
    centre = jnp.mean(values, axis=axis, keepdims=True)
    spread = jnp.mean(jnp.square(values - centre), axis=axis, keepdims=True)
    return (values - centre) * lax.rsqrt(spread + 1e-05)


def swap_halves(values):
    flat = values.reshape(-1, LANES)
    return pltpu.roll(flat, LANES // 2, 1).reshape(values.shape)


def pack(low, high):
    lane = lax.broadcasted_iota(jnp.int32, low.shape, low.ndim - 1)
    return jnp.where(lane < LANES // 2, low, swap_halves(high))


def window_start(windowed):
    if not windowed:
        return 0
    return jnp.where(lax.axis_index("wide") * SUB < 3 * BLOCK, 0, BLOCK)


def chunks_of(rows):
    return ((0, LANES), (LANES, rows - LANES))


def project_kernel(mask_hbm, x_hbm, wl_hbm, wr_hbm, *refs):
    whole_ref, window_ref, normed_ref, cut_ref, mask_ref, x_ref, w_ref, edge, sems = refs
    group_size = whole_ref.shape[0]
    tokens = x_ref.shape[0] // SUB
    copies = [
        pltpu.make_async_copy(mask_hbm, mask_ref, sems.at[0]),
        pltpu.make_async_copy(wl_hbm, w_ref.at[0], sems.at[1]),
        pltpu.make_async_copy(wr_hbm, w_ref.at[1], sems.at[2]),
    ]
    for index in range(2):
        part = pl.ds(index * LANES * SUB, LANES * SUB)
        copies.append(pltpu.make_async_copy(x_hbm.at[part], x_ref.at[part], sems.at[3 + index]))
    for copy in copies:
        copy.start()
    copies[0].wait()
    cut = mask_ref[0, 3] == 0
    cut_ref[0] = cut.astype(jnp.int32)
    column_block = lax.axis_index("wide") * SUB // BLOCK
    kept = [mask_ref[block, column_block].astype(jnp.float32) for block in range(mask_hbm.shape[0])]
    copies[1].wait()
    copies[2].wait()
    weights = [w_ref[side].T for side in range(2)]

    def project(windowed, send_ref):
        first = window_start(windowed)
        row_block = (first + lax.broadcasted_iota(jnp.int32, (1, 2 * LANES), 1)) // BLOCK
        mask = jnp.zeros((1, 2 * LANES), jnp.float32)
        for block, value in enumerate(kept):
            mask = jnp.where(row_block == block, value, mask)
        if windowed:
            copies[3].wait()
            copies[4].wait()
        chunks = chunks_of(3 * BLOCK if windowed else tokens)
        for index, (low, count) in enumerate(chunks):
            if not windowed:
                copies[3 + index].wait()
            group = 2 * LANES // count
            chunk_mask = jnp.concatenate([mask[:, low : low + count]] * group, axis=1)
            base = pl.multiple_of((first + low) * SUB, SUB)
            for start in range(0, SUB, group):
                x = [x_ref[pl.ds(base + start + k, count, stride=SUB), :] for k in range(group)]
                normed = layer_norm(jnp.concatenate(x, axis=0), 1).astype(jnp.bfloat16)
                for k in range(group):
                    normed_ref[start + k, low : low + count, :] = normed[k * count : (k + 1) * count]
                for side in range(2):
                    mixed = lax.dot_general(
                        weights[side], normed, (((1,), (1,)), ((), ())), preferred_element_type=jnp.float32
                    )
                    proj = jax.nn.sigmoid(mixed[:C]) * mixed[C:] * chunk_mask
                    for k in range(group):
                        at = k * count // LANES * LANES
                        piece = proj[:, at : at + LANES]
                        if k * count % LANES:
                            piece = swap_halves(piece)
                        edge[side, index, pl.ds(start + k, C, stride=SUB), :] = piece
            part = C // group_size * SUB
            for side in range(2):
                values = edge[side, index].reshape(group_size, part, LANES)
                if count < LANES:
                    values = pack(values[:, : part // 2], values[:, part // 2 :])
                place = side * send_ref.shape[1] // 2 + index * part
                send_ref[:, place : place + values.shape[1], :] = values.astype(jnp.bfloat16)

    pl.when(cut)(lambda: project(True, window_ref))
    pl.when(jnp.logical_not(cut))(lambda: project(False, whole_ref))


def triangle_kernel(windowed, recv_ref, send_ref):
    group_size = recv_ref.shape[0]
    wide = send_ref.shape[0]
    per_device = C // group_size
    part = per_device * SUB
    columns = group_size * SUB
    half = per_device // 2

    def load(side, channel):
        parts = []
        for index in range(2):
            start = side * send_ref.shape[1] + index * part
            swap = windowed and index == 1 and channel >= half
            at = start + (channel - half if swap else channel) * SUB
            pair = recv_ref[:, at : at + 2 * SUB, :].astype(jnp.float32)
            if swap:
                pair = swap_halves(pair)
            parts.append([
                pair[:, low : low + SUB].reshape(columns, LANES).astype(jnp.bfloat16)
                for low in (0, SUB)
            ])
        return [jnp.concatenate([p[n] for p in parts], axis=1) for n in range(2)]

    def product(right, left):
        return lax.dot_general(
            right, left, (((0,), (0,)), ((), ())), preferred_element_type=jnp.float32
        )

    cut = 3 * BLOCK
    columns_first = lax.axis_index("wide") // group_size * columns
    column = columns_first + lax.broadcasted_iota(jnp.int32, (columns, 1), 0)
    sums = []
    for channel in range(0, per_device, 2):
        for left, right in zip(load(0, channel), load(1, channel)):
            if windowed:
                above = product(right, jnp.where(column < cut, left, 0))[:cut]
                below = product(right[:, LANES:], jnp.where(column < cut, 0, left))
                sums.append(jnp.concatenate([above, below[: wide * SUB - cut]], axis=0))
            else:
                sums.append(product(right, left))
    first = [s[:, :LANES] for s in sums]
    second = [s[:, LANES:] for s in sums]
    if windowed:
        second = [pack(second[c], second[c + half]) for c in range(half)]
    start = 0
    for channels in (first, second):
        for channel in range(0, len(channels), 2):
            pair = [channels[channel + n].reshape(wide, SUB, LANES) for n in range(2)]
            pair = jnp.concatenate(pair, axis=1).astype(jnp.bfloat16)
            send_ref[:, start : start + 2 * SUB, :] = pair
            start += 2 * SUB


def update_kernel(windowed, recv_ref, normed_ref, wg_ref, wo_ref, out_hbm, tri, out_ref, sems):
    group_size = recv_ref.shape[0] // PARTS
    part = C // group_size * SUB
    rows = 3 * BLOCK if windowed else normed_ref.shape[1]
    chunks = chunks_of(rows)
    first = window_start(windowed)
    copies = []
    if windowed:
        rest = out_hbm.shape[0] - rows * SUB
        to = pl.multiple_of(jnp.where(first == 0, rows, 0) * SUB, SUB)
        out_ref[rows * SUB :, :] = jnp.zeros((rest, C), jnp.float32)
        copies.append(
            pltpu.make_async_copy(
                out_ref.at[pl.ds(rows * SUB, rest)], out_hbm.at[pl.ds(to, rest)], sems.at[2]
            )
        )
        copies[0].start()
    for index, (low, count) in enumerate(chunks):
        height = part * count // LANES
        sums = [
            recv_ref[n * group_size : (n + 1) * group_size, index * part : index * part + height, :]
            for n in range(PARTS)
        ]
        sums = sum(values.astype(jnp.float32) for values in sums)
        if count < LANES:
            sums = jnp.concatenate([sums, swap_halves(sums)], axis=1)
        tri[index] = layer_norm(sums.reshape(C, SUB, LANES), 0).reshape(C * SUB, LANES)
        for j in range(SUB):
            tri_normed = tri[index, pl.ds(j, C, stride=SUB), :].astype(jnp.bfloat16)
            mixed = lax.dot_general(
                tri_normed, wo_ref[...], (((0,), (0,)), ((), ())), preferred_element_type=jnp.float32
            )
            normed = normed_ref[j, low : low + count, :]
            gate = jax.nn.sigmoid(
                jnp.dot(normed, wg_ref[...], preferred_element_type=jnp.float32)
            )
            out_ref[pl.ds(low * SUB + j, count, stride=SUB), :] = gate * mixed[:count]
        to = pl.multiple_of((first + low) * SUB, SUB)
        copies.append(
            pltpu.make_async_copy(
                out_ref.at[pl.ds(low * SUB, count * SUB)],
                out_hbm.at[pl.ds(to, count * SUB)],
                sems.at[index],
            )
        )
        copies[-1].start()
    for copy in copies:
        copy.wait()


HBM = pl.BlockSpec(memory_space=pltpu.HBM)
VMEM = pl.BlockSpec(memory_space=pltpu.VMEM)
PARAMS = pltpu.CompilerParams(vmem_limit_bytes=48 * 1024 * 1024)


def in_hbm(array):
    return pltpu.with_memory_space_constraint(array, pltpu.HBM)


def exchange(array):
    wide, size = lax.axis_size("wide"), array.shape[0]
    groups = [list(range(first, first + size)) for first in range(0, wide, size)]
    return lax.all_to_all(
        array, "wide", split_axis=0, concat_axis=0, axis_index_groups=groups, tiled=True
    )


def after_projection(windowed, whole, window, normed, gate_weight, out_weight):
    send = window if windowed else whole
    group_size, both, _ = send.shape
    wide = group_size * PARTS
    tokens = normed.shape[1]
    back = pl.pallas_call(
        functools.partial(triangle_kernel, windowed),
        out_shape=jax.ShapeDtypeStruct((wide, both // 2, LANES), jnp.bfloat16),
        in_specs=[VMEM],
        out_specs=VMEM,
        compiler_params=PARAMS,
        name="triangle",
    )(exchange(send))
    return pl.pallas_call(
        functools.partial(update_kernel, windowed),
        out_shape=pltpu.HBM((tokens * SUB, C), jnp.float32),
        in_specs=[VMEM] * 4,
        out_specs=HBM,
        scratch_shapes=[
            pltpu.VMEM((2, C * SUB, LANES), jnp.float32),
            pltpu.VMEM((tokens * SUB, C), jnp.float32),
            pltpu.SemaphoreType.DMA((3,)),
        ],
        compiler_params=PARAMS,
        name="update",
    )(exchange(back), normed, gate_weight, out_weight)


def kernels_on_device(pair_act, block_mask, left_weight, right_weight, gate_weight, out_weight):
    tokens = pair_act.shape[0]
    wide = lax.axis_size("wide")
    group_size = wide // PARTS
    both = lambda rows: 2 * rows * (C // group_size) * SUB // LANES
    whole, window, normed, cut = pl.pallas_call(
        project_kernel,
        out_shape=(
            jax.ShapeDtypeStruct((group_size, both(tokens), LANES), jnp.bfloat16),
            jax.ShapeDtypeStruct((group_size, both(3 * BLOCK), LANES), jnp.bfloat16),
            jax.ShapeDtypeStruct((SUB, tokens, C), jnp.bfloat16),
            pltpu.SMEM((1,), jnp.int32),
        ),
        in_specs=[HBM] * 4,
        out_specs=(VMEM, VMEM, VMEM, pl.BlockSpec(memory_space=pltpu.SMEM)),
        scratch_shapes=[
            pltpu.SMEM(block_mask.shape, jnp.int32),
            pltpu.VMEM((tokens * SUB, C), jnp.float32),
            pltpu.VMEM((2, C, 2 * C), jnp.bfloat16),
            pltpu.VMEM((2, 2, C * SUB, LANES), jnp.float32),
            pltpu.SemaphoreType.DMA((5,)),
        ],
        compiler_params=PARAMS,
        name="project",
    )(
        in_hbm(block_mask),
        in_hbm(pair_act.reshape(tokens * SUB, C)),
        in_hbm(left_weight),
        in_hbm(right_weight),
    )
    update = lax.switch(
        cut[0],
        [functools.partial(after_projection, windowed) for windowed in (False, True)],
        whole,
        window,
        normed,
        gate_weight,
        out_weight,
    )
    return update.reshape(tokens, SUB, C)


def plain_on_device(pair_act, block_mask, left_weight, right_weight, gate_weight, out_weight):
    tile_rows = pair_act.shape[0]
    tile_cols = pair_act.shape[1]
    wide = lax.axis_size("wide")
    narrow = lax.axis_size("narrow")
    per_device = C // wide
    row_ids = lax.axis_index("narrow") * tile_rows + jnp.arange(tile_rows, dtype=jnp.int32)
    col_ids = lax.axis_index("wide") * tile_cols + jnp.arange(tile_cols, dtype=jnp.int32)
    block_ids = jnp.arange(block_mask.shape[0], dtype=jnp.int32)
    row_hot = (row_ids[:, None] // BLOCK == block_ids[None, :]).astype(jnp.float32)
    col_hot = (col_ids[:, None] // BLOCK == block_ids[None, :]).astype(jnp.float32)
    tile_mask = jnp.dot(jnp.dot(row_hot, block_mask.astype(jnp.float32)), col_hot.T).T
    normed = layer_norm(pair_act, -1).astype(jnp.bfloat16)

    def edges(weight):
        mixed = jnp.einsum("cd,ikc->dki", weight, normed, preferred_element_type=jnp.float32)
        proj = jax.nn.sigmoid(mixed[:C]) * mixed[C:] * tile_mask[None]
        return proj.astype(jnp.bfloat16).reshape(wide, per_device, tile_cols, tile_rows)

    send = jnp.stack([edges(left_weight), edges(right_weight)], axis=1)
    recv = lax.all_to_all(send, "wide", split_axis=0, concat_axis=0, tiled=True)
    left, right = recv[:, 0], recv[:, 1]
    if narrow > 1:
        right = lax.all_gather(right, "narrow", axis=3, tiled=True)
    tri = jnp.einsum("sckj,scki->cji", right, left, preferred_element_type=jnp.float32)
    back = tri.astype(jnp.bfloat16).reshape(per_device, wide, tile_cols, tile_rows)
    back = jnp.transpose(back, (1, 0, 2, 3))
    tri = lax.all_to_all(back, "wide", split_axis=0, concat_axis=0, tiled=True)
    tri = tri.reshape(C, tile_cols, tile_rows).astype(jnp.float32)
    tri_normed = layer_norm(tri, 0).astype(jnp.bfloat16)
    gate = jax.nn.sigmoid(
        jnp.einsum("ikc,cd->ikd", normed, gate_weight, preferred_element_type=jnp.float32)
    )
    return gate * jnp.einsum(
        "cji,cd->ijd", tri_normed, out_weight, preferred_element_type=jnp.float32
    )


def on_device(pair_act, block_mask, *weights):
    rows, cols = pair_act.shape[:2]
    blocks = block_mask.shape[0]
    fits = rows == 2 * LANES and cols == SUB and C // lax.axis_size("wide") == 4 and blocks == 4
    if lax.axis_size("narrow") > 1 or not fits:
        return plain_on_device(pair_act, block_mask, *weights)
    return kernels_on_device(pair_act, block_mask, *weights)


def solution(mesh):
    return jax.shard_map(
        on_device,
        mesh=mesh,
        in_specs=(P("narrow", "wide", None), P(), P(), P(), P(), P()),
        out_specs=P("narrow", "wide", None),
        check_vma=False,
    )
```

```python
import functools

import jax
import jax.numpy as jnp
from jax import lax
from jax.experimental import pallas as pl
from jax.experimental.pallas import tpu as pltpu
from jax.sharding import PartitionSpec as P

C = 128
BLOCK = 64
LANES = 128
SUB = 8
PARTS = 2


def layer_norm(values, axis):
    centre = jnp.mean(values, axis=axis, keepdims=True)
    spread = jnp.mean(jnp.square(values - centre), axis=axis, keepdims=True)
    return (values - centre) * lax.rsqrt(spread + 1e-05)


def swap_halves(values):
    flat = values.reshape(-1, LANES)
    return pltpu.roll(flat, LANES // 2, 1).reshape(values.shape)


def pack(low, high):
    lane = lax.broadcasted_iota(jnp.int32, low.shape, low.ndim - 1)
    return jnp.where(lane < LANES // 2, low, swap_halves(high))


def window_start(windowed):
    if not windowed:
        return 0
    return jnp.where(lax.axis_index("wide") * SUB < 3 * BLOCK, 0, BLOCK)


def chunks_of(rows):
    return ((0, LANES), (LANES, rows - LANES))


def channel_mean(values):
    high = values.astype(jnp.bfloat16)
    low = (values - high.astype(jnp.float32)).astype(jnp.bfloat16)
    ones = jnp.full((2 * C, C), 1 / C, jnp.bfloat16)
    return jnp.dot(jnp.concatenate([high, low], axis=1), ones, preferred_element_type=jnp.float32)


def channel_norm(values):
    centred = values - channel_mean(values)
    return centred * lax.rsqrt(channel_mean(jnp.square(centred)) + 1e-05)


def project_kernel(mask_hbm, x_hbm, wl_hbm, wr_hbm, *refs):
    whole_ref, window_ref, normed_ref, cut_ref, mask_ref, x_ref, w_ref, edge, sems = refs
    group_size = whole_ref.shape[0]
    tokens = x_ref.shape[0] // SUB
    copies = [
        pltpu.make_async_copy(mask_hbm, mask_ref, sems.at[0]),
        pltpu.make_async_copy(wl_hbm, w_ref.at[0], sems.at[1]),
        pltpu.make_async_copy(wr_hbm, w_ref.at[1], sems.at[2]),
    ]
    for index in range(2):
        part = pl.ds(index * LANES * SUB, LANES * SUB)
        copies.append(pltpu.make_async_copy(x_hbm.at[part], x_ref.at[part], sems.at[3 + index]))
    for copy in copies:
        copy.start()
    copies[0].wait()
    cut = mask_ref[0, 3] == 0
    cut_ref[0] = cut.astype(jnp.int32)
    column_block = lax.axis_index("wide") * SUB // BLOCK
    kept = [mask_ref[block, column_block].astype(jnp.float32) for block in range(mask_hbm.shape[0])]
    copies[1].wait()
    copies[2].wait()
    weights = jnp.concatenate([w_ref[0].T, w_ref[1].T], axis=0)

    def project(windowed, send_ref):
        first = window_start(windowed)
        row_block = (first + lax.broadcasted_iota(jnp.int32, (1, 2 * LANES), 1)) // BLOCK
        mask = jnp.zeros((1, 2 * LANES), jnp.float32)
        for block, value in enumerate(kept):
            mask = jnp.where(row_block == block, value, mask)
        if windowed:
            copies[3].wait()
            copies[4].wait()
        chunks = chunks_of(3 * BLOCK if windowed else tokens)
        for index, (low, count) in enumerate(chunks):
            if not windowed:
                copies[3 + index].wait()
            group = 2 * LANES // count
            chunk_mask = jnp.concatenate([mask[:, low : low + count]] * group, axis=1)
            base = pl.multiple_of((first + low) * SUB, SUB)
            for start in range(0, SUB, group):
                x = [x_ref[pl.ds(base + start + k, count, stride=SUB), :] for k in range(group)]
                normed = channel_norm(jnp.concatenate(x, axis=0)).astype(jnp.bfloat16)
                for k in range(group):
                    normed_ref[start + k, low : low + count, :] = normed[k * count : (k + 1) * count]
                mixed = lax.dot_general(
                    weights, normed, (((1,), (1,)), ((), ())), preferred_element_type=jnp.float32
                )
                for side in range(2):
                    gate = mixed[2 * side * C : (2 * side + 1) * C]
                    value = mixed[(2 * side + 1) * C : (2 * side + 2) * C]
                    proj = jax.nn.sigmoid(gate) * value * chunk_mask
                    for k in range(group):
                        at = k * count // LANES * LANES
                        piece = proj[:, at : at + LANES]
                        if k * count % LANES:
                            piece = swap_halves(piece)
                        edge[side, index, pl.ds(start + k, C, stride=SUB), :] = piece
        part = C // group_size * SUB
        low = 0
        for side in range(2):
            for index, (_, count) in enumerate(chunks):
                values = edge[side, index].reshape(group_size, part, LANES)
                if count < LANES:
                    values = pack(values[:, : part // 2], values[:, part // 2 :])
                send_ref[:, low : low + values.shape[1], :] = values.astype(jnp.bfloat16)
                low += values.shape[1]

    pl.when(cut)(lambda: project(True, window_ref))
    pl.when(jnp.logical_not(cut))(lambda: project(False, whole_ref))


def triangle_kernel(windowed, recv_ref, send_ref):
    group_size = recv_ref.shape[0]
    wide = send_ref.shape[0]
    per_device = C // group_size
    part = per_device * SUB
    columns = group_size * SUB
    half = per_device // 2

    def load(side, channel):
        parts = []
        for index in range(2):
            start = side * send_ref.shape[1] + index * part
            swap = windowed and index == 1 and channel >= half
            at = start + (channel - half if swap else channel) * SUB
            pair = recv_ref[:, at : at + 2 * SUB, :].astype(jnp.float32)
            if swap:
                pair = swap_halves(pair)
            parts.append([
                pair[:, low : low + SUB].reshape(columns, LANES).astype(jnp.bfloat16)
                for low in (0, SUB)
            ])
        return [jnp.concatenate([p[n] for p in parts], axis=1) for n in range(2)]

    def product(right, left):
        return lax.dot_general(
            right, left, (((0,), (0,)), ((), ())), preferred_element_type=jnp.float32
        )

    cut = 3 * BLOCK
    columns_first = lax.axis_index("wide") // group_size * columns
    column = columns_first + lax.broadcasted_iota(jnp.int32, (columns, 1), 0)
    sums = []
    for channel in range(0, per_device, 2):
        for left, right in zip(load(0, channel), load(1, channel)):
            if windowed:
                above = product(right, jnp.where(column < cut, left, 0))[:cut]
                below = product(right[:, LANES:], jnp.where(column < cut, 0, left))
                sums.append(jnp.concatenate([above, below[: wide * SUB - cut]], axis=0))
            else:
                sums.append(product(right, left))
    first = [s[:, :LANES] for s in sums]
    second = [s[:, LANES:] for s in sums]
    if windowed:
        second = [pack(second[c], second[c + half]) for c in range(half)]
    start = 0
    for channels in (first, second):
        for channel in range(0, len(channels), 2):
            pair = [channels[channel + n].reshape(wide, SUB, LANES) for n in range(2)]
            pair = jnp.concatenate(pair, axis=1).astype(jnp.bfloat16)
            send_ref[:, start : start + 2 * SUB, :] = pair
            start += 2 * SUB


def update_kernel(windowed, recv_ref, normed_ref, wg_ref, wo_ref, out_hbm, tri, out_ref, sems):
    group_size = recv_ref.shape[0] // PARTS
    part = C // group_size * SUB
    rows = 3 * BLOCK if windowed else normed_ref.shape[1]
    chunks = chunks_of(rows)
    first = window_start(windowed)
    copies = []
    if windowed:
        rest = out_hbm.shape[0] - rows * SUB
        to = pl.multiple_of(jnp.where(first == 0, rows, 0) * SUB, SUB)
        out_ref[rows * SUB :, :] = jnp.zeros((rest, C), jnp.float32)
        copies.append(
            pltpu.make_async_copy(
                out_ref.at[pl.ds(rows * SUB, rest)], out_hbm.at[pl.ds(to, rest)], sems.at[2]
            )
        )
        copies[0].start()
    for index, (low, count) in enumerate(chunks):
        height = part * count // LANES
        sums = [
            recv_ref[n * group_size : (n + 1) * group_size, index * part : index * part + height, :]
            for n in range(PARTS)
        ]
        sums = sum(values.astype(jnp.float32) for values in sums)
        if count < LANES:
            sums = jnp.concatenate([sums, swap_halves(sums)], axis=1)
        tri[index] = layer_norm(sums.reshape(C, SUB, LANES), 0).reshape(C * SUB, LANES)
        for j in range(SUB):
            tri_normed = tri[index, pl.ds(j, C, stride=SUB), :].astype(jnp.bfloat16)
            mixed = lax.dot_general(
                tri_normed, wo_ref[...], (((0,), (0,)), ((), ())), preferred_element_type=jnp.float32
            )
            normed = normed_ref[j, low : low + count, :]
            gate = jax.nn.sigmoid(
                jnp.dot(normed, wg_ref[...], preferred_element_type=jnp.float32)
            )
            out_ref[pl.ds(low * SUB + j, count, stride=SUB), :] = gate * mixed[:count]
        to = pl.multiple_of((first + low) * SUB, SUB)
        copies.append(
            pltpu.make_async_copy(
                out_ref.at[pl.ds(low * SUB, count * SUB)],
                out_hbm.at[pl.ds(to, count * SUB)],
                sems.at[index],
            )
        )
        copies[-1].start()
    for copy in copies:
        copy.wait()


HBM = pl.BlockSpec(memory_space=pltpu.HBM)
VMEM = pl.BlockSpec(memory_space=pltpu.VMEM)
PARAMS = pltpu.CompilerParams(vmem_limit_bytes=48 * 1024 * 1024)


def in_hbm(array):
    return pltpu.with_memory_space_constraint(array, pltpu.HBM)


def exchange(array):
    wide, size = lax.axis_size("wide"), array.shape[0]
    groups = [list(range(first, first + size)) for first in range(0, wide, size)]
    return lax.all_to_all(
        array, "wide", split_axis=0, concat_axis=0, axis_index_groups=groups, tiled=True
    )


def after_projection(windowed, whole, window, normed, gate_weight, out_weight):
    send = window if windowed else whole
    group_size, both, _ = send.shape
    wide = group_size * PARTS
    tokens = normed.shape[1]
    back = pl.pallas_call(
        functools.partial(triangle_kernel, windowed),
        out_shape=jax.ShapeDtypeStruct((wide, both // 2, LANES), jnp.bfloat16),
        in_specs=[VMEM],
        out_specs=VMEM,
        compiler_params=PARAMS,
        name="triangle",
    )(exchange(send))
    return pl.pallas_call(
        functools.partial(update_kernel, windowed),
        out_shape=pltpu.HBM((tokens * SUB, C), jnp.float32),
        in_specs=[VMEM] * 4,
        out_specs=HBM,
        scratch_shapes=[
            pltpu.VMEM((2, C * SUB, LANES), jnp.float32),
            pltpu.VMEM((tokens * SUB, C), jnp.float32),
            pltpu.SemaphoreType.DMA((3,)),
        ],
        compiler_params=PARAMS,
        name="update",
    )(exchange(back), normed, gate_weight, out_weight)


def kernels_on_device(pair_act, block_mask, left_weight, right_weight, gate_weight, out_weight):
    tokens = pair_act.shape[0]
    wide = lax.axis_size("wide")
    group_size = wide // PARTS
    both = lambda rows: 2 * rows * (C // group_size) * SUB // LANES
    whole, window, normed, cut = pl.pallas_call(
        project_kernel,
        out_shape=(
            jax.ShapeDtypeStruct((group_size, both(tokens), LANES), jnp.bfloat16),
            jax.ShapeDtypeStruct((group_size, both(3 * BLOCK), LANES), jnp.bfloat16),
            jax.ShapeDtypeStruct((SUB, tokens, C), jnp.bfloat16),
            pltpu.SMEM((1,), jnp.int32),
        ),
        in_specs=[HBM] * 4,
        out_specs=(VMEM, VMEM, VMEM, pl.BlockSpec(memory_space=pltpu.SMEM)),
        scratch_shapes=[
            pltpu.SMEM(block_mask.shape, jnp.int32),
            pltpu.VMEM((tokens * SUB, C), jnp.float32),
            pltpu.VMEM((2, C, 2 * C), jnp.bfloat16),
            pltpu.VMEM((2, 2, C * SUB, LANES), jnp.float32),
            pltpu.SemaphoreType.DMA((5,)),
        ],
        compiler_params=PARAMS,
        name="project",
    )(
        in_hbm(block_mask),
        in_hbm(pair_act.reshape(tokens * SUB, C)),
        in_hbm(left_weight),
        in_hbm(right_weight),
    )
    update = lax.switch(
        cut[0],
        [functools.partial(after_projection, windowed) for windowed in (False, True)],
        whole,
        window,
        normed,
        gate_weight,
        out_weight,
    )
    return update.reshape(tokens, SUB, C)


def plain_on_device(pair_act, block_mask, left_weight, right_weight, gate_weight, out_weight):
    tile_rows = pair_act.shape[0]
    tile_cols = pair_act.shape[1]
    wide = lax.axis_size("wide")
    narrow = lax.axis_size("narrow")
    per_device = C // wide
    row_ids = lax.axis_index("narrow") * tile_rows + jnp.arange(tile_rows, dtype=jnp.int32)
    col_ids = lax.axis_index("wide") * tile_cols + jnp.arange(tile_cols, dtype=jnp.int32)
    block_ids = jnp.arange(block_mask.shape[0], dtype=jnp.int32)
    row_hot = (row_ids[:, None] // BLOCK == block_ids[None, :]).astype(jnp.float32)
    col_hot = (col_ids[:, None] // BLOCK == block_ids[None, :]).astype(jnp.float32)
    tile_mask = jnp.dot(jnp.dot(row_hot, block_mask.astype(jnp.float32)), col_hot.T).T
    normed = layer_norm(pair_act, -1).astype(jnp.bfloat16)

    def edges(weight):
        mixed = jnp.einsum("cd,ikc->dki", weight, normed, preferred_element_type=jnp.float32)
        proj = jax.nn.sigmoid(mixed[:C]) * mixed[C:] * tile_mask[None]
        return proj.astype(jnp.bfloat16).reshape(wide, per_device, tile_cols, tile_rows)

    send = jnp.stack([edges(left_weight), edges(right_weight)], axis=1)
    recv = lax.all_to_all(send, "wide", split_axis=0, concat_axis=0, tiled=True)
    left, right = recv[:, 0], recv[:, 1]
    if narrow > 1:
        right = lax.all_gather(right, "narrow", axis=3, tiled=True)
    tri = jnp.einsum("sckj,scki->cji", right, left, preferred_element_type=jnp.float32)
    back = tri.astype(jnp.bfloat16).reshape(per_device, wide, tile_cols, tile_rows)
    back = jnp.transpose(back, (1, 0, 2, 3))
    tri = lax.all_to_all(back, "wide", split_axis=0, concat_axis=0, tiled=True)
    tri = tri.reshape(C, tile_cols, tile_rows).astype(jnp.float32)
    tri_normed = layer_norm(tri, 0).astype(jnp.bfloat16)
    gate = jax.nn.sigmoid(
        jnp.einsum("ikc,cd->ikd", normed, gate_weight, preferred_element_type=jnp.float32)
    )
    return gate * jnp.einsum(
        "cji,cd->ijd", tri_normed, out_weight, preferred_element_type=jnp.float32
    )


def on_device(pair_act, block_mask, *weights):
    rows, cols = pair_act.shape[:2]
    blocks = block_mask.shape[0]
    fits = rows == 2 * LANES and cols == SUB and C // lax.axis_size("wide") == 4 and blocks == 4
    if lax.axis_size("narrow") > 1 or not fits:
        return plain_on_device(pair_act, block_mask, *weights)
    return kernels_on_device(pair_act, block_mask, *weights)


def solution(mesh):
    return jax.shard_map(
        on_device,
        mesh=mesh,
        in_specs=(P("narrow", "wide", None), P(), P(), P(), P(), P()),
        out_specs=P("narrow", "wide", None),
        check_vma=False,
    )
```

```python
import functools

import jax
import jax.numpy as jnp
from jax import lax
from jax.experimental import pallas as pl
from jax.experimental.pallas import tpu as pltpu
from jax.sharding import PartitionSpec as P

C = 128
BLOCK = 64
LANES = 128
SUB = 8
PARTS = 2


def layer_norm(values, axis):
    centre = jnp.mean(values, axis=axis, keepdims=True)
    spread = jnp.mean(jnp.square(values - centre), axis=axis, keepdims=True)
    return (values - centre) * lax.rsqrt(spread + 1e-05)


def swap_halves(values):
    flat = values.reshape(-1, LANES)
    return pltpu.roll(flat, LANES // 2, 1).reshape(values.shape)


def pack(low, high):
    lane = lax.broadcasted_iota(jnp.int32, low.shape, low.ndim - 1)
    return jnp.where(lane < LANES // 2, low, swap_halves(high))


def window_start(windowed):
    if not windowed:
        return 0
    return jnp.where(lax.axis_index("wide") * SUB < 3 * BLOCK, 0, BLOCK)


def chunks_of(rows):
    return ((0, LANES), (LANES, rows - LANES))


def project_kernel(mask_hbm, x_hbm, wl_hbm, wr_hbm, *refs):
    whole_ref, window_ref, normed_ref, cut_ref, mask_ref, x_ref, w_ref, edge, sems = refs
    group_size = whole_ref.shape[0]
    tokens = x_ref.shape[0] // SUB
    copies = [
        pltpu.make_async_copy(mask_hbm, mask_ref, sems.at[0]),
        pltpu.make_async_copy(wl_hbm, w_ref.at[0], sems.at[1]),
        pltpu.make_async_copy(wr_hbm, w_ref.at[1], sems.at[2]),
    ]
    for index in range(2):
        part = pl.ds(index * LANES * SUB, LANES * SUB)
        copies.append(pltpu.make_async_copy(x_hbm.at[part], x_ref.at[part], sems.at[3 + index]))
    for copy in copies:
        copy.start()
    copies[0].wait()
    cut = mask_ref[0, 3] == 0
    cut_ref[0] = cut.astype(jnp.int32)
    column_block = lax.axis_index("wide") * SUB // BLOCK
    kept = [mask_ref[block, column_block].astype(jnp.float32) for block in range(mask_hbm.shape[0])]
    copies[1].wait()
    copies[2].wait()
    weights = jnp.concatenate([w_ref[0].T, w_ref[1].T], axis=0)

    def project(windowed, send_ref):
        first = window_start(windowed)
        row_block = (first + lax.broadcasted_iota(jnp.int32, (1, 2 * LANES), 1)) // BLOCK
        mask = jnp.zeros((1, 2 * LANES), jnp.float32)
        for block, value in enumerate(kept):
            mask = jnp.where(row_block == block, value, mask)
        if windowed:
            copies[3].wait()
            copies[4].wait()
        chunks = chunks_of(3 * BLOCK if windowed else tokens)
        for index, (low, count) in enumerate(chunks):
            if not windowed:
                copies[3 + index].wait()
            group = 2 * LANES // count
            chunk_mask = jnp.concatenate([mask[:, low : low + count]] * group, axis=1)
            base = pl.multiple_of((first + low) * SUB, SUB)
            for start in range(0, SUB, group):
                x = [x_ref[pl.ds(base + start + k, count, stride=SUB), :] for k in range(group)]
                normed = layer_norm(jnp.concatenate(x, axis=0), 1).astype(jnp.bfloat16)
                for k in range(group):
                    normed_ref[start + k, low : low + count, :] = normed[k * count : (k + 1) * count]
                mixed = lax.dot_general(
                    weights, normed, (((1,), (1,)), ((), ())), preferred_element_type=jnp.float32
                )
                for side in range(2):
                    gate = mixed[2 * side * C : (2 * side + 1) * C]
                    value = mixed[(2 * side + 1) * C : (2 * side + 2) * C]
                    proj = jax.nn.sigmoid(gate) * value * chunk_mask
                    for k in range(group):
                        at = k * count // LANES * LANES
                        piece = proj[:, at : at + LANES]
                        if k * count % LANES:
                            piece = swap_halves(piece)
                        edge[side, index, pl.ds(start + k, C, stride=SUB), :] = piece
        part = C // group_size * SUB
        low = 0
        for side in range(2):
            for index, (_, count) in enumerate(chunks):
                values = edge[side, index].reshape(group_size, part, LANES)
                if count < LANES:
                    values = pack(values[:, : part // 2], values[:, part // 2 :])
                send_ref[:, low : low + values.shape[1], :] = values.astype(jnp.bfloat16)
                low += values.shape[1]

    pl.when(cut)(lambda: project(True, window_ref))
    pl.when(jnp.logical_not(cut))(lambda: project(False, whole_ref))


def triangle_kernel(windowed, recv_ref, send_ref):
    group_size = recv_ref.shape[0]
    wide = send_ref.shape[0]
    per_device = C // group_size
    part = per_device * SUB
    columns = group_size * SUB
    half = per_device // 2

    def load(side, channel):
        parts = []
        for index in range(2):
            start = side * send_ref.shape[1] + index * part
            swap = windowed and index == 1 and channel >= half
            at = start + (channel - half if swap else channel) * SUB
            pair = recv_ref[:, at : at + 2 * SUB, :].astype(jnp.float32)
            if swap:
                pair = swap_halves(pair)
            parts.append([
                pair[:, low : low + SUB].reshape(columns, LANES).astype(jnp.bfloat16)
                for low in (0, SUB)
            ])
        return [jnp.concatenate([p[n] for p in parts], axis=1) for n in range(2)]

    def product(right, left):
        return lax.dot_general(
            right, left, (((0,), (0,)), ((), ())), preferred_element_type=jnp.float32
        )

    cut = 3 * BLOCK
    columns_first = lax.axis_index("wide") // group_size * columns
    column = columns_first + lax.broadcasted_iota(jnp.int32, (columns, 1), 0)
    sums = []
    for channel in range(0, per_device, 2):
        for left, right in zip(load(0, channel), load(1, channel)):
            if windowed:
                above = product(right, jnp.where(column < cut, left, 0))[:cut]
                below = product(right[:, LANES:], jnp.where(column < cut, 0, left))
                sums.append(jnp.concatenate([above, below[: wide * SUB - cut]], axis=0))
            else:
                sums.append(product(right, left))
    first = [s[:, :LANES] for s in sums]
    second = [s[:, LANES:] for s in sums]
    if windowed:
        second = [pack(second[c], second[c + half]) for c in range(half)]
    start = 0
    for channels in (first, second):
        for channel in range(0, len(channels), 2):
            pair = [channels[channel + n].reshape(wide, SUB, LANES) for n in range(2)]
            pair = jnp.concatenate(pair, axis=1).astype(jnp.bfloat16)
            send_ref[:, start : start + 2 * SUB, :] = pair
            start += 2 * SUB


def update_kernel(windowed, recv_ref, normed_ref, wg_ref, wo_ref, out_hbm, tri, out_ref, sems):
    group_size = recv_ref.shape[0] // PARTS
    part = C // group_size * SUB
    rows = 3 * BLOCK if windowed else normed_ref.shape[1]
    chunks = chunks_of(rows)
    first = window_start(windowed)
    copies = []
    if windowed:
        rest = out_hbm.shape[0] - rows * SUB
        to = pl.multiple_of(jnp.where(first == 0, rows, 0) * SUB, SUB)
        out_ref[rows * SUB :, :] = jnp.zeros((rest, C), jnp.float32)
        copies.append(
            pltpu.make_async_copy(
                out_ref.at[pl.ds(rows * SUB, rest)], out_hbm.at[pl.ds(to, rest)], sems.at[2]
            )
        )
        copies[0].start()
    zeros = jnp.zeros((C, C), jnp.bfloat16)
    weights = jnp.concatenate(
        [
            jnp.concatenate([wg_ref[...], zeros], axis=1),
            jnp.concatenate([zeros, wo_ref[...]], axis=1),
        ],
        axis=0,
    )
    for index, (low, count) in enumerate(chunks):
        height = part * count // LANES
        sums = [
            recv_ref[n * group_size : (n + 1) * group_size, index * part : index * part + height, :]
            for n in range(PARTS)
        ]
        sums = sum(values.astype(jnp.float32) for values in sums)
        if count < LANES:
            sums = jnp.concatenate([sums, swap_halves(sums)], axis=1)
        tri[index] = layer_norm(sums.reshape(C, SUB, LANES), 0).reshape(C * SUB, LANES)
        for j in range(SUB):
            tri_normed = tri[index, pl.ds(j, C, stride=SUB), :].astype(jnp.bfloat16).T
            normed = normed_ref[j, low : low + count, :]
            mixed = jnp.dot(
                jnp.concatenate([normed, tri_normed[:count]], axis=1),
                weights,
                preferred_element_type=jnp.float32,
            )
            update = jax.nn.sigmoid(mixed[:, :C]) * mixed[:, C:]
            out_ref[pl.ds(low * SUB + j, count, stride=SUB), :] = update
        to = pl.multiple_of((first + low) * SUB, SUB)
        copies.append(
            pltpu.make_async_copy(
                out_ref.at[pl.ds(low * SUB, count * SUB)],
                out_hbm.at[pl.ds(to, count * SUB)],
                sems.at[index],
            )
        )
        copies[-1].start()
    for copy in copies:
        copy.wait()


HBM = pl.BlockSpec(memory_space=pltpu.HBM)
VMEM = pl.BlockSpec(memory_space=pltpu.VMEM)
PARAMS = pltpu.CompilerParams(vmem_limit_bytes=48 * 1024 * 1024)


def in_hbm(array):
    return pltpu.with_memory_space_constraint(array, pltpu.HBM)


def exchange(array):
    wide, size = lax.axis_size("wide"), array.shape[0]
    groups = [list(range(first, first + size)) for first in range(0, wide, size)]
    return lax.all_to_all(
        array, "wide", split_axis=0, concat_axis=0, axis_index_groups=groups, tiled=True
    )


def after_projection(windowed, whole, window, normed, gate_weight, out_weight):
    send = window if windowed else whole
    group_size, both, _ = send.shape
    wide = group_size * PARTS
    tokens = normed.shape[1]
    back = pl.pallas_call(
        functools.partial(triangle_kernel, windowed),
        out_shape=jax.ShapeDtypeStruct((wide, both // 2, LANES), jnp.bfloat16),
        in_specs=[VMEM],
        out_specs=VMEM,
        compiler_params=PARAMS,
        name="triangle",
    )(exchange(send))
    return pl.pallas_call(
        functools.partial(update_kernel, windowed),
        out_shape=pltpu.HBM((tokens * SUB, C), jnp.float32),
        in_specs=[VMEM] * 4,
        out_specs=HBM,
        scratch_shapes=[
            pltpu.VMEM((2, C * SUB, LANES), jnp.float32),
            pltpu.VMEM((tokens * SUB, C), jnp.float32),
            pltpu.SemaphoreType.DMA((3,)),
        ],
        compiler_params=PARAMS,
        name="update",
    )(exchange(back), normed, gate_weight, out_weight)


def kernels_on_device(pair_act, block_mask, left_weight, right_weight, gate_weight, out_weight):
    tokens = pair_act.shape[0]
    wide = lax.axis_size("wide")
    group_size = wide // PARTS
    both = lambda rows: 2 * rows * (C // group_size) * SUB // LANES
    whole, window, normed, cut = pl.pallas_call(
        project_kernel,
        out_shape=(
            jax.ShapeDtypeStruct((group_size, both(tokens), LANES), jnp.bfloat16),
            jax.ShapeDtypeStruct((group_size, both(3 * BLOCK), LANES), jnp.bfloat16),
            jax.ShapeDtypeStruct((SUB, tokens, C), jnp.bfloat16),
            pltpu.SMEM((1,), jnp.int32),
        ),
        in_specs=[HBM] * 4,
        out_specs=(VMEM, VMEM, VMEM, pl.BlockSpec(memory_space=pltpu.SMEM)),
        scratch_shapes=[
            pltpu.SMEM(block_mask.shape, jnp.int32),
            pltpu.VMEM((tokens * SUB, C), jnp.float32),
            pltpu.VMEM((2, C, 2 * C), jnp.bfloat16),
            pltpu.VMEM((2, 2, C * SUB, LANES), jnp.float32),
            pltpu.SemaphoreType.DMA((5,)),
        ],
        compiler_params=PARAMS,
        name="project",
    )(
        in_hbm(block_mask),
        in_hbm(pair_act.reshape(tokens * SUB, C)),
        in_hbm(left_weight),
        in_hbm(right_weight),
    )
    update = lax.switch(
        cut[0],
        [functools.partial(after_projection, windowed) for windowed in (False, True)],
        whole,
        window,
        normed,
        gate_weight,
        out_weight,
    )
    return update.reshape(tokens, SUB, C)


def plain_on_device(pair_act, block_mask, left_weight, right_weight, gate_weight, out_weight):
    tile_rows = pair_act.shape[0]
    tile_cols = pair_act.shape[1]
    wide = lax.axis_size("wide")
    narrow = lax.axis_size("narrow")
    per_device = C // wide
    row_ids = lax.axis_index("narrow") * tile_rows + jnp.arange(tile_rows, dtype=jnp.int32)
    col_ids = lax.axis_index("wide") * tile_cols + jnp.arange(tile_cols, dtype=jnp.int32)
    block_ids = jnp.arange(block_mask.shape[0], dtype=jnp.int32)
    row_hot = (row_ids[:, None] // BLOCK == block_ids[None, :]).astype(jnp.float32)
    col_hot = (col_ids[:, None] // BLOCK == block_ids[None, :]).astype(jnp.float32)
    tile_mask = jnp.dot(jnp.dot(row_hot, block_mask.astype(jnp.float32)), col_hot.T).T
    normed = layer_norm(pair_act, -1).astype(jnp.bfloat16)

    def edges(weight):
        mixed = jnp.einsum("cd,ikc->dki", weight, normed, preferred_element_type=jnp.float32)
        proj = jax.nn.sigmoid(mixed[:C]) * mixed[C:] * tile_mask[None]
        return proj.astype(jnp.bfloat16).reshape(wide, per_device, tile_cols, tile_rows)

    send = jnp.stack([edges(left_weight), edges(right_weight)], axis=1)
    recv = lax.all_to_all(send, "wide", split_axis=0, concat_axis=0, tiled=True)
    left, right = recv[:, 0], recv[:, 1]
    if narrow > 1:
        right = lax.all_gather(right, "narrow", axis=3, tiled=True)
    tri = jnp.einsum("sckj,scki->cji", right, left, preferred_element_type=jnp.float32)
    back = tri.astype(jnp.bfloat16).reshape(per_device, wide, tile_cols, tile_rows)
    back = jnp.transpose(back, (1, 0, 2, 3))
    tri = lax.all_to_all(back, "wide", split_axis=0, concat_axis=0, tiled=True)
    tri = tri.reshape(C, tile_cols, tile_rows).astype(jnp.float32)
    tri_normed = layer_norm(tri, 0).astype(jnp.bfloat16)
    gate = jax.nn.sigmoid(
        jnp.einsum("ikc,cd->ikd", normed, gate_weight, preferred_element_type=jnp.float32)
    )
    return gate * jnp.einsum(
        "cji,cd->ijd", tri_normed, out_weight, preferred_element_type=jnp.float32
    )


def on_device(pair_act, block_mask, *weights):
    rows, cols = pair_act.shape[:2]
    blocks = block_mask.shape[0]
    fits = rows == 2 * LANES and cols == SUB and C // lax.axis_size("wide") == 4 and blocks == 4
    if lax.axis_size("narrow") > 1 or not fits:
        return plain_on_device(pair_act, block_mask, *weights)
    return kernels_on_device(pair_act, block_mask, *weights)


def solution(mesh):
    return jax.shard_map(
        on_device,
        mesh=mesh,
        in_specs=(P("narrow", "wide", None), P(), P(), P(), P(), P()),
        out_specs=P("narrow", "wide", None),
        check_vma=False,
    )
```

```python
import functools

import jax
import jax.numpy as jnp
from jax import lax
from jax.experimental import pallas as pl
from jax.experimental.pallas import tpu as pltpu
from jax.sharding import PartitionSpec as P

C = 128
BLOCK = 64
LANES = 128
SUB = 8
PARTS = 2


def layer_norm(values, axis):
    centre = jnp.mean(values, axis=axis, keepdims=True)
    spread = jnp.mean(jnp.square(values - centre), axis=axis, keepdims=True)
    return (values - centre) * lax.rsqrt(spread + 1e-05)


def swap_halves(values):
    flat = values.reshape(-1, LANES)
    return pltpu.roll(flat, LANES // 2, 1).reshape(values.shape)


def pack(low, high):
    lane = lax.broadcasted_iota(jnp.int32, low.shape, low.ndim - 1)
    return jnp.where(lane < LANES // 2, low, swap_halves(high))


def window_start(windowed):
    if not windowed:
        return 0
    return jnp.where(lax.axis_index("wide") * SUB < 3 * BLOCK, 0, BLOCK)


def chunks_of(rows):
    return ((0, LANES), (LANES, rows - LANES))


def project_kernel(mask_hbm, x_hbm, wl_hbm, wr_hbm, *refs):
    whole_ref, window_ref, normed_ref, cut_ref, mask_ref, x_ref, w_ref, edge, sems = refs
    group_size = whole_ref.shape[0]
    tokens = x_hbm.shape[0] // SUB
    copies = [
        pltpu.make_async_copy(mask_hbm, mask_ref, sems.at[0]),
        pltpu.make_async_copy(wl_hbm, w_ref.at[0], sems.at[1]),
        pltpu.make_async_copy(wr_hbm, w_ref.at[1], sems.at[2]),
    ]
    for index in range(2):
        part = pl.ds(index * LANES * SUB, LANES * SUB)
        copies.append(pltpu.make_async_copy(x_hbm.at[part], x_ref.at[part], sems.at[3 + index]))
    for copy in copies:
        copy.start()
    copies[0].wait()
    cut = mask_ref[0, 3] == 0
    cut_ref[0] = cut.astype(jnp.int32)
    column_block = lax.axis_index("wide") * SUB // BLOCK
    kept = [mask_ref[block, column_block].astype(jnp.float32) for block in range(mask_hbm.shape[0])]
    copies[1].wait()
    copies[2].wait()
    weights = jnp.concatenate([w_ref[0].T, w_ref[1].T], axis=0)

    def project(windowed, send_ref):
        first = window_start(windowed)
        row_block = (first + lax.broadcasted_iota(jnp.int32, (1, 2 * LANES), 1)) // BLOCK
        mask = jnp.zeros((1, 2 * LANES), jnp.float32)
        for block, value in enumerate(kept):
            mask = jnp.where(row_block == block, value, mask)
        if windowed:
            copies[3].wait()
            copies[4].wait()
        chunks = chunks_of(3 * BLOCK if windowed else tokens)
        for index, (low, count) in enumerate(chunks):
            if not windowed:
                copies[3 + index].wait()
            group = 2 * LANES // count
            chunk_mask = jnp.concatenate([mask[:, low : low + count]] * group, axis=1)
            base = pl.multiple_of((first + low) * SUB, SUB)
            for start in range(0, SUB, group):
                x = [x_ref[pl.ds(base + start + k, count, stride=SUB), :] for k in range(group)]
                normed = layer_norm(jnp.concatenate(x, axis=0), 1).astype(jnp.bfloat16)
                for k in range(group):
                    normed_ref[start + k, low : low + count, :] = normed[k * count : (k + 1) * count]
                mixed = lax.dot_general(
                    weights, normed, (((1,), (1,)), ((), ())), preferred_element_type=jnp.float32
                )
                for side in range(2):
                    gate = mixed[2 * side * C : (2 * side + 1) * C]
                    value = mixed[(2 * side + 1) * C : (2 * side + 2) * C]
                    proj = jax.nn.sigmoid(gate) * value * chunk_mask
                    for k in range(group):
                        at = k * count // LANES * LANES
                        piece = proj[:, at : at + LANES]
                        if k * count % LANES:
                            piece = swap_halves(piece)
                        edge[side, index, pl.ds(start + k, C, stride=SUB), :] = piece
        part = C // group_size * SUB
        low = 0
        for side in range(2):
            for index, (_, count) in enumerate(chunks):
                values = edge[side, index, : C * SUB, :].reshape(group_size, part, LANES)
                if count < LANES:
                    values = pack(values[:, : part // 2], values[:, part // 2 :])
                send_ref[:, low : low + values.shape[1], :] = values.astype(jnp.bfloat16)
                low += values.shape[1]

    pl.when(cut)(lambda: project(True, window_ref))
    pl.when(jnp.logical_not(cut))(lambda: project(False, whole_ref))


def triangle_kernel(windowed, recv_ref, send_ref):
    group_size = recv_ref.shape[0]
    wide = send_ref.shape[0]
    per_device = C // group_size
    part = per_device * SUB
    columns = group_size * SUB
    half = per_device // 2

    cut = 3 * BLOCK
    columns_first = lax.axis_index("wide") // group_size * columns
    column = columns_first + lax.broadcasted_iota(jnp.int32, (columns, LANES), 0)
    lane = lax.broadcasted_iota(jnp.int32, (columns, LANES), 1)

    def split_at_cut(index, values, swapped):
        if index == 0:
            return jnp.where(column < cut, values, 0.0)
        own = jnp.where(column < cut, values, swapped)
        return jnp.where((column < cut) == (lane < LANES // 2), own, 0.0)

    def load(side, channel):
        parts = []
        for index in range(2):
            start = side * send_ref.shape[1] + index * part
            packed = windowed and index == 1
            swap = packed and channel >= half
            at = start + (channel - half if swap else channel) * SUB
            pair = recv_ref[:, at : at + 2 * SUB, :].astype(jnp.float32)
            parts.append([])
            for low in (0, SUB):
                values = pair[:, low : low + SUB].reshape(columns, LANES)
                swapped = swap_halves(values) if packed else values
                if swap:
                    values, swapped = swapped, values
                if windowed and side == 1:
                    values = split_at_cut(index, values, swapped)
                parts[-1].append(values.astype(jnp.bfloat16))
        return [jnp.concatenate([p[n] for p in parts], axis=1) for n in range(2)]

    sums = []
    for channel in range(0, per_device, 2):
        for left, right in zip(load(0, channel), load(1, channel)):
            sums.append(
                lax.dot_general(
                    right, left, (((0,), (0,)), ((), ())), preferred_element_type=jnp.float32
                )
            )
    first = [s[:, :LANES] for s in sums]
    second = [s[:, LANES:] for s in sums]
    if windowed:
        second = [pack(second[c], second[c + half]) for c in range(half)]
    start = 0
    for channels in (first, second):
        for channel in range(0, len(channels), 2):
            pair = [channels[channel + n].reshape(wide, SUB, LANES) for n in range(2)]
            pair = jnp.concatenate(pair, axis=1).astype(jnp.bfloat16)
            send_ref[:, start : start + 2 * SUB, :] = pair
            start += 2 * SUB


def update_kernel(windowed, recv_ref, normed_ref, wg_ref, wo_ref, out_hbm, tri, out_ref, sems):
    group_size = recv_ref.shape[0] // PARTS
    part = C // group_size * SUB
    rows = 3 * BLOCK if windowed else normed_ref.shape[1]
    chunks = chunks_of(rows)
    first = window_start(windowed)
    copies = []
    if windowed:
        rest = out_hbm.shape[0] - rows * SUB
        to = pl.multiple_of(jnp.where(first == 0, rows, 0) * SUB, SUB)
        out_ref[pl.ds(rows * SUB, rest), :] = jnp.zeros((rest, C), jnp.float32)
        copies.append(
            pltpu.make_async_copy(
                out_ref.at[pl.ds(rows * SUB, rest)], out_hbm.at[pl.ds(to, rest)], sems.at[2]
            )
        )
        copies[0].start()
    for index, (low, count) in enumerate(chunks):
        height = part * count // LANES
        sums = [
            recv_ref[n * group_size : (n + 1) * group_size, index * part : index * part + height, :]
            for n in range(PARTS)
        ]
        sums = sum(values.astype(jnp.float32) for values in sums)
        if count < LANES:
            sums = jnp.concatenate([sums, swap_halves(sums)], axis=1)
        tri[index, : C * SUB, :] = layer_norm(sums.reshape(C, SUB, LANES), 0).reshape(C * SUB, LANES)
        for j in range(SUB):
            tri_normed = tri[index, pl.ds(j, C, stride=SUB), :].astype(jnp.bfloat16)
            mixed = lax.dot_general(
                tri_normed, wo_ref[...], (((0,), (0,)), ((), ())), preferred_element_type=jnp.float32
            )
            normed = normed_ref[j, low : low + count, :]
            gate = jax.nn.sigmoid(
                jnp.dot(normed, wg_ref[...], preferred_element_type=jnp.float32)
            )
            out_ref[pl.ds(low * SUB + j, count, stride=SUB), :] = gate * mixed[:count]
        to = pl.multiple_of((first + low) * SUB, SUB)
        copies.append(
            pltpu.make_async_copy(
                out_ref.at[pl.ds(low * SUB, count * SUB)],
                out_hbm.at[pl.ds(to, count * SUB)],
                sems.at[index],
            )
        )
        copies[-1].start()
    for copy in copies:
        copy.wait()


HBM = pl.BlockSpec(memory_space=pltpu.HBM)
VMEM = pl.BlockSpec(memory_space=pltpu.VMEM)
PARAMS = pltpu.CompilerParams(vmem_limit_bytes=48 * 1024 * 1024)


def in_hbm(array):
    return pltpu.with_memory_space_constraint(array, pltpu.HBM)


def exchange(array):
    wide, size = lax.axis_size("wide"), array.shape[0]
    groups = [list(range(first, first + size)) for first in range(0, wide, size)]
    return lax.all_to_all(
        array, "wide", split_axis=0, concat_axis=0, axis_index_groups=groups, tiled=True
    )


def after_projection(windowed, whole, window, normed, gate_weight, out_weight):
    send = window if windowed else whole
    group_size, both, _ = send.shape
    wide = group_size * PARTS
    tokens = normed.shape[1]
    back = pl.pallas_call(
        functools.partial(triangle_kernel, windowed),
        out_shape=jax.ShapeDtypeStruct((wide, both // 2, LANES), jnp.bfloat16),
        in_specs=[VMEM],
        out_specs=VMEM,
        compiler_params=PARAMS,
        name="triangle",
    )(exchange(send))
    return pl.pallas_call(
        functools.partial(update_kernel, windowed),
        out_shape=pltpu.HBM((tokens * SUB, C), jnp.float32),
        in_specs=[VMEM] * 4,
        out_specs=HBM,
        scratch_shapes=[
            pltpu.VMEM((2, C * SUB + SUB, LANES), jnp.float32),
            pltpu.VMEM((tokens * SUB + SUB, C), jnp.float32),
            pltpu.SemaphoreType.DMA((3,)),
        ],
        compiler_params=PARAMS,
        name="update",
    )(exchange(back), normed, gate_weight, out_weight)


def kernels_on_device(pair_act, block_mask, left_weight, right_weight, gate_weight, out_weight):
    tokens = pair_act.shape[0]
    wide = lax.axis_size("wide")
    group_size = wide // PARTS
    both = lambda rows: 2 * rows * (C // group_size) * SUB // LANES
    whole, window, normed, cut = pl.pallas_call(
        project_kernel,
        out_shape=(
            jax.ShapeDtypeStruct((group_size, both(tokens), LANES), jnp.bfloat16),
            jax.ShapeDtypeStruct((group_size, both(3 * BLOCK), LANES), jnp.bfloat16),
            jax.ShapeDtypeStruct((SUB, tokens, C), jnp.bfloat16),
            pltpu.SMEM((1,), jnp.int32),
        ),
        in_specs=[HBM] * 4,
        out_specs=(VMEM, VMEM, VMEM, pl.BlockSpec(memory_space=pltpu.SMEM)),
        scratch_shapes=[
            pltpu.SMEM(block_mask.shape, jnp.int32),
            pltpu.VMEM((tokens * SUB + SUB, C), jnp.float32),
            pltpu.VMEM((2, C, 2 * C), jnp.bfloat16),
            pltpu.VMEM((2, 2, C * SUB + SUB, LANES), jnp.float32),
            pltpu.SemaphoreType.DMA((5,)),
        ],
        compiler_params=PARAMS,
        name="project",
    )(
        in_hbm(block_mask),
        in_hbm(pair_act.reshape(tokens * SUB, C)),
        in_hbm(left_weight),
        in_hbm(right_weight),
    )
    update = lax.switch(
        cut[0],
        [functools.partial(after_projection, windowed) for windowed in (False, True)],
        whole,
        window,
        normed,
        gate_weight,
        out_weight,
    )
    return update.reshape(tokens, SUB, C)


def plain_on_device(pair_act, block_mask, left_weight, right_weight, gate_weight, out_weight):
    tile_rows = pair_act.shape[0]
    tile_cols = pair_act.shape[1]
    wide = lax.axis_size("wide")
    narrow = lax.axis_size("narrow")
    per_device = C // wide
    row_ids = lax.axis_index("narrow") * tile_rows + jnp.arange(tile_rows, dtype=jnp.int32)
    col_ids = lax.axis_index("wide") * tile_cols + jnp.arange(tile_cols, dtype=jnp.int32)
    block_ids = jnp.arange(block_mask.shape[0], dtype=jnp.int32)
    row_hot = (row_ids[:, None] // BLOCK == block_ids[None, :]).astype(jnp.float32)
    col_hot = (col_ids[:, None] // BLOCK == block_ids[None, :]).astype(jnp.float32)
    tile_mask = jnp.dot(jnp.dot(row_hot, block_mask.astype(jnp.float32)), col_hot.T).T
    normed = layer_norm(pair_act, -1).astype(jnp.bfloat16)

    def edges(weight):
        mixed = jnp.einsum("cd,ikc->dki", weight, normed, preferred_element_type=jnp.float32)
        proj = jax.nn.sigmoid(mixed[:C]) * mixed[C:] * tile_mask[None]
        return proj.astype(jnp.bfloat16).reshape(wide, per_device, tile_cols, tile_rows)

    send = jnp.stack([edges(left_weight), edges(right_weight)], axis=1)
    recv = lax.all_to_all(send, "wide", split_axis=0, concat_axis=0, tiled=True)
    left, right = recv[:, 0], recv[:, 1]
    if narrow > 1:
        right = lax.all_gather(right, "narrow", axis=3, tiled=True)
    tri = jnp.einsum("sckj,scki->cji", right, left, preferred_element_type=jnp.float32)
    back = tri.astype(jnp.bfloat16).reshape(per_device, wide, tile_cols, tile_rows)
    back = jnp.transpose(back, (1, 0, 2, 3))
    tri = lax.all_to_all(back, "wide", split_axis=0, concat_axis=0, tiled=True)
    tri = tri.reshape(C, tile_cols, tile_rows).astype(jnp.float32)
    tri_normed = layer_norm(tri, 0).astype(jnp.bfloat16)
    gate = jax.nn.sigmoid(
        jnp.einsum("ikc,cd->ikd", normed, gate_weight, preferred_element_type=jnp.float32)
    )
    return gate * jnp.einsum(
        "cji,cd->ijd", tri_normed, out_weight, preferred_element_type=jnp.float32
    )


def on_device(pair_act, block_mask, *weights):
    rows, cols = pair_act.shape[:2]
    blocks = block_mask.shape[0]
    fits = rows == 2 * LANES and cols == SUB and C // lax.axis_size("wide") == 4 and blocks == 4
    if lax.axis_size("narrow") > 1 or not fits:
        return plain_on_device(pair_act, block_mask, *weights)
    return kernels_on_device(pair_act, block_mask, *weights)


def solution(mesh):
    return jax.shard_map(
        on_device,
        mesh=mesh,
        in_specs=(P("narrow", "wide", None), P(), P(), P(), P(), P()),
        out_specs=P("narrow", "wide", None),
        check_vma=False,
    )
```

```python
import functools

import jax
import jax.numpy as jnp
from jax import lax
from jax.experimental import pallas as pl
from jax.experimental.pallas import tpu as pltpu
from jax.sharding import PartitionSpec as P

C = 128
BLOCK = 64
LANES = 128
SUB = 8
PARTS = 2


def layer_norm(values, axis):
    centre = jnp.mean(values, axis=axis, keepdims=True)
    spread = jnp.mean(jnp.square(values - centre), axis=axis, keepdims=True)
    return (values - centre) * lax.rsqrt(spread + 1e-05)


def swap_halves(values):
    flat = values.reshape(-1, LANES)
    return pltpu.roll(flat, LANES // 2, 1).reshape(values.shape)


def pack(low, high):
    lane = lax.broadcasted_iota(jnp.int32, low.shape, low.ndim - 1)
    return jnp.where(lane < LANES // 2, low, swap_halves(high))


def window_start(windowed):
    if not windowed:
        return 0
    return jnp.where(lax.axis_index("wide") * SUB < 3 * BLOCK, 0, BLOCK)


def chunks_of(rows):
    return ((0, LANES), (LANES, rows - LANES))


def project_kernel(mask_hbm, x_hbm, wl_hbm, wr_hbm, *refs):
    whole_ref, window_ref, normed_ref, cut_ref, mask_ref, x_ref, w_ref, edge, sems = refs
    group_size = whole_ref.shape[0]
    tokens = x_hbm.shape[0] // SUB
    pieces = []
    for index in range(tokens // BLOCK):
        piece = pl.ds(index * BLOCK * SUB, BLOCK * SUB)
        pieces.append(pltpu.make_async_copy(x_hbm.at[piece], x_ref.at[piece], sems.at[3 + index]))
    copies = [
        pltpu.make_async_copy(mask_hbm, mask_ref, sems.at[0]),
        pltpu.make_async_copy(wl_hbm, w_ref.at[0], sems.at[1]),
        pltpu.make_async_copy(wr_hbm, w_ref.at[1], sems.at[2]),
    ]
    for copy in copies + pieces:
        copy.start()
    copies[0].wait()
    cut = mask_ref[0, 3] == 0
    cut_ref[0] = cut.astype(jnp.int32)
    column_block = lax.axis_index("wide") * SUB // BLOCK
    kept = [mask_ref[block, column_block].astype(jnp.float32) for block in range(mask_hbm.shape[0])]
    copies[1].wait()
    copies[2].wait()
    weights = jnp.concatenate([w_ref[0].T, w_ref[1].T], axis=0)

    def project(windowed, send_ref):
        first = window_start(windowed)
        row_block = (first + lax.broadcasted_iota(jnp.int32, (1, 2 * LANES), 1)) // BLOCK
        mask = jnp.zeros((1, 2 * LANES), jnp.float32)
        for block, value in enumerate(kept):
            mask = jnp.where(row_block == block, value, mask)
        chunks = chunks_of(3 * BLOCK if windowed else tokens)
        needs = (3, 4) if windowed else (2, 4)
        for index, (low, count) in enumerate(chunks):
            for piece in pieces[needs[index - 1] if index else 0 : needs[index]]:
                piece.wait()
            group = 2 * LANES // count
            chunk_mask = jnp.concatenate([mask[:, low : low + count]] * group, axis=1)
            base = pl.multiple_of((first + low) * SUB, SUB)
            for start in range(0, SUB, group):
                x = [x_ref[pl.ds(base + start + k, count, stride=SUB), :] for k in range(group)]
                normed = layer_norm(jnp.concatenate(x, axis=0), 1).astype(jnp.bfloat16)
                for k in range(group):
                    normed_ref[start + k, low : low + count, :] = normed[k * count : (k + 1) * count]
                mixed = lax.dot_general(
                    weights, normed, (((1,), (1,)), ((), ())), preferred_element_type=jnp.float32
                )
                for side in range(2):
                    gate = mixed[2 * side * C : (2 * side + 1) * C]
                    value = mixed[(2 * side + 1) * C : (2 * side + 2) * C]
                    proj = jax.nn.sigmoid(gate) * value * chunk_mask
                    for k in range(group):
                        at = k * count // LANES * LANES
                        piece = proj[:, at : at + LANES]
                        if k * count % LANES:
                            piece = swap_halves(piece)
                        edge[side, index, pl.ds(start + k, C, stride=SUB), :] = piece
        part = C // group_size * SUB
        low = 0
        for side in range(2):
            for index, (_, count) in enumerate(chunks):
                values = edge[side, index, : C * SUB, :].reshape(group_size, part, LANES)
                if count < LANES:
                    values = pack(values[:, : part // 2], values[:, part // 2 :])
                send_ref[:, low : low + values.shape[1], :] = values.astype(jnp.bfloat16)
                low += values.shape[1]

    pl.when(cut)(lambda: project(True, window_ref))
    pl.when(jnp.logical_not(cut))(lambda: project(False, whole_ref))


def triangle_kernel(windowed, recv_ref, send_ref):
    group_size = recv_ref.shape[0]
    wide = send_ref.shape[0]
    per_device = C // group_size
    part = per_device * SUB
    columns = group_size * SUB
    half = per_device // 2

    def load(side, channel):
        parts = []
        for index in range(2):
            start = side * send_ref.shape[1] + index * part
            swap = windowed and index == 1 and channel >= half
            at = start + (channel - half if swap else channel) * SUB
            pair = recv_ref[:, at : at + 2 * SUB, :].astype(jnp.float32)
            if swap:
                pair = swap_halves(pair)
            parts.append([
                pair[:, low : low + SUB].reshape(columns, LANES).astype(jnp.bfloat16)
                for low in (0, SUB)
            ])
        return [jnp.concatenate([p[n] for p in parts], axis=1) for n in range(2)]

    def product(right, left):
        return lax.dot_general(
            right, left, (((0,), (0,)), ((), ())), preferred_element_type=jnp.float32
        )

    cut = 3 * BLOCK
    columns_first = lax.axis_index("wide") // group_size * columns
    column = columns_first + lax.broadcasted_iota(jnp.int32, (columns, 1), 0)
    sums = []
    for channel in range(0, per_device, 2):
        for left, right in zip(load(0, channel), load(1, channel)):
            if windowed:
                above = product(right, jnp.where(column < cut, left, 0))[:cut]
                below = product(right[:, LANES:], jnp.where(column < cut, 0, left))
                sums.append(jnp.concatenate([above, below[: wide * SUB - cut]], axis=0))
            else:
                sums.append(product(right, left))
    first = [s[:, :LANES] for s in sums]
    second = [s[:, LANES:] for s in sums]
    if windowed:
        second = [pack(second[c], second[c + half]) for c in range(half)]
    start = 0
    for channels in (first, second):
        for channel in range(0, len(channels), 2):
            pair = [channels[channel + n].reshape(wide, SUB, LANES) for n in range(2)]
            pair = jnp.concatenate(pair, axis=1).astype(jnp.bfloat16)
            send_ref[:, start : start + 2 * SUB, :] = pair
            start += 2 * SUB


def update_kernel(windowed, recv_ref, normed_ref, wg_ref, wo_ref, out_hbm, tri, out_ref, sems):
    group_size = recv_ref.shape[0] // PARTS
    part = C // group_size * SUB
    rows = 3 * BLOCK if windowed else normed_ref.shape[1]
    chunks = chunks_of(rows)
    first = window_start(windowed)
    copies = []
    if windowed:
        rest = out_hbm.shape[0] - rows * SUB
        to = pl.multiple_of(jnp.where(first == 0, rows, 0) * SUB, SUB)
        out_ref[pl.ds(rows * SUB, rest), :] = jnp.zeros((rest, C), jnp.float32)
        copies.append(
            pltpu.make_async_copy(
                out_ref.at[pl.ds(rows * SUB, rest)], out_hbm.at[pl.ds(to, rest)], sems.at[3]
            )
        )
        copies[0].start()
    for index, (low, count) in enumerate(chunks):
        height = part * count // LANES
        sums = [
            recv_ref[n * group_size : (n + 1) * group_size, index * part : index * part + height, :]
            for n in range(PARTS)
        ]
        sums = sum(values.astype(jnp.float32) for values in sums)
        if count < LANES:
            sums = jnp.concatenate([sums, swap_halves(sums)], axis=1)
        tri[index, : C * SUB, :] = layer_norm(sums.reshape(C, SUB, LANES), 0).reshape(C * SUB, LANES)
        for j in range(SUB):
            tri_normed = tri[index, pl.ds(j, C, stride=SUB), :].astype(jnp.bfloat16)
            mixed = lax.dot_general(
                tri_normed, wo_ref[...], (((0,), (0,)), ((), ())), preferred_element_type=jnp.float32
            )
            normed = normed_ref[j, low : low + count, :]
            gate = jax.nn.sigmoid(
                jnp.dot(normed, wg_ref[...], preferred_element_type=jnp.float32)
            )
            out_ref[pl.ds(low * SUB + j, count, stride=SUB), :] = gate * mixed[:count]
        for piece in range(low, low + count, BLOCK):
            to = pl.multiple_of((first + piece) * SUB, SUB)
            copies.append(
                pltpu.make_async_copy(
                    out_ref.at[pl.ds(piece * SUB, BLOCK * SUB)],
                    out_hbm.at[pl.ds(to, BLOCK * SUB)],
                    sems.at[piece // BLOCK],
                )
            )
            copies[-1].start()
    for copy in copies:
        copy.wait()


HBM = pl.BlockSpec(memory_space=pltpu.HBM)
VMEM = pl.BlockSpec(memory_space=pltpu.VMEM)
PARAMS = pltpu.CompilerParams(vmem_limit_bytes=48 * 1024 * 1024)


def in_hbm(array):
    return pltpu.with_memory_space_constraint(array, pltpu.HBM)


def exchange(array):
    wide, size = lax.axis_size("wide"), array.shape[0]
    groups = [list(range(first, first + size)) for first in range(0, wide, size)]
    return lax.all_to_all(
        array, "wide", split_axis=0, concat_axis=0, axis_index_groups=groups, tiled=True
    )


def after_projection(windowed, whole, window, normed, gate_weight, out_weight):
    send = window if windowed else whole
    group_size, both, _ = send.shape
    wide = group_size * PARTS
    tokens = normed.shape[1]
    back = pl.pallas_call(
        functools.partial(triangle_kernel, windowed),
        out_shape=jax.ShapeDtypeStruct((wide, both // 2, LANES), jnp.bfloat16),
        in_specs=[VMEM],
        out_specs=VMEM,
        compiler_params=PARAMS,
        name="triangle",
    )(exchange(send))
    return pl.pallas_call(
        functools.partial(update_kernel, windowed),
        out_shape=pltpu.HBM((tokens * SUB, C), jnp.float32),
        in_specs=[VMEM] * 4,
        out_specs=HBM,
        scratch_shapes=[
            pltpu.VMEM((2, C * SUB + SUB, LANES), jnp.float32),
            pltpu.VMEM((tokens * SUB + SUB, C), jnp.float32),
            pltpu.SemaphoreType.DMA((4,)),
        ],
        compiler_params=PARAMS,
        name="update",
    )(exchange(back), normed, gate_weight, out_weight)


def kernels_on_device(pair_act, block_mask, left_weight, right_weight, gate_weight, out_weight):
    tokens = pair_act.shape[0]
    wide = lax.axis_size("wide")
    group_size = wide // PARTS
    both = lambda rows: 2 * rows * (C // group_size) * SUB // LANES
    whole, window, normed, cut = pl.pallas_call(
        project_kernel,
        out_shape=(
            jax.ShapeDtypeStruct((group_size, both(tokens), LANES), jnp.bfloat16),
            jax.ShapeDtypeStruct((group_size, both(3 * BLOCK), LANES), jnp.bfloat16),
            jax.ShapeDtypeStruct((SUB, tokens, C), jnp.bfloat16),
            pltpu.SMEM((1,), jnp.int32),
        ),
        in_specs=[HBM] * 4,
        out_specs=(VMEM, VMEM, VMEM, pl.BlockSpec(memory_space=pltpu.SMEM)),
        scratch_shapes=[
            pltpu.SMEM(block_mask.shape, jnp.int32),
            pltpu.VMEM((tokens * SUB + SUB, C), jnp.float32),
            pltpu.VMEM((2, C, 2 * C), jnp.bfloat16),
            pltpu.VMEM((2, 2, C * SUB + SUB, LANES), jnp.float32),
            pltpu.SemaphoreType.DMA((7,)),
        ],
        compiler_params=PARAMS,
        name="project",
    )(
        in_hbm(block_mask),
        in_hbm(pair_act.reshape(tokens * SUB, C)),
        in_hbm(left_weight),
        in_hbm(right_weight),
    )
    update = lax.switch(
        cut[0],
        [functools.partial(after_projection, windowed) for windowed in (False, True)],
        whole,
        window,
        normed,
        gate_weight,
        out_weight,
    )
    return update.reshape(tokens, SUB, C)


def plain_on_device(pair_act, block_mask, left_weight, right_weight, gate_weight, out_weight):
    tile_rows = pair_act.shape[0]
    tile_cols = pair_act.shape[1]
    wide = lax.axis_size("wide")
    narrow = lax.axis_size("narrow")
    per_device = C // wide
    row_ids = lax.axis_index("narrow") * tile_rows + jnp.arange(tile_rows, dtype=jnp.int32)
    col_ids = lax.axis_index("wide") * tile_cols + jnp.arange(tile_cols, dtype=jnp.int32)
    block_ids = jnp.arange(block_mask.shape[0], dtype=jnp.int32)
    row_hot = (row_ids[:, None] // BLOCK == block_ids[None, :]).astype(jnp.float32)
    col_hot = (col_ids[:, None] // BLOCK == block_ids[None, :]).astype(jnp.float32)
    tile_mask = jnp.dot(jnp.dot(row_hot, block_mask.astype(jnp.float32)), col_hot.T).T
    normed = layer_norm(pair_act, -1).astype(jnp.bfloat16)

    def edges(weight):
        mixed = jnp.einsum("cd,ikc->dki", weight, normed, preferred_element_type=jnp.float32)
        proj = jax.nn.sigmoid(mixed[:C]) * mixed[C:] * tile_mask[None]
        return proj.astype(jnp.bfloat16).reshape(wide, per_device, tile_cols, tile_rows)

    send = jnp.stack([edges(left_weight), edges(right_weight)], axis=1)
    recv = lax.all_to_all(send, "wide", split_axis=0, concat_axis=0, tiled=True)
    left, right = recv[:, 0], recv[:, 1]
    if narrow > 1:
        right = lax.all_gather(right, "narrow", axis=3, tiled=True)
    tri = jnp.einsum("sckj,scki->cji", right, left, preferred_element_type=jnp.float32)
    back = tri.astype(jnp.bfloat16).reshape(per_device, wide, tile_cols, tile_rows)
    back = jnp.transpose(back, (1, 0, 2, 3))
    tri = lax.all_to_all(back, "wide", split_axis=0, concat_axis=0, tiled=True)
    tri = tri.reshape(C, tile_cols, tile_rows).astype(jnp.float32)
    tri_normed = layer_norm(tri, 0).astype(jnp.bfloat16)
    gate = jax.nn.sigmoid(
        jnp.einsum("ikc,cd->ikd", normed, gate_weight, preferred_element_type=jnp.float32)
    )
    return gate * jnp.einsum(
        "cji,cd->ijd", tri_normed, out_weight, preferred_element_type=jnp.float32
    )


def on_device(pair_act, block_mask, *weights):
    rows, cols = pair_act.shape[:2]
    blocks = block_mask.shape[0]
    fits = rows == 2 * LANES and cols == SUB and C // lax.axis_size("wide") == 4 and blocks == 4
    if lax.axis_size("narrow") > 1 or not fits:
        return plain_on_device(pair_act, block_mask, *weights)
    return kernels_on_device(pair_act, block_mask, *weights)


def solution(mesh):
    return jax.shard_map(
        on_device,
        mesh=mesh,
        in_specs=(P("narrow", "wide", None), P(), P(), P(), P(), P()),
        out_specs=P("narrow", "wide", None),
        check_vma=False,
    )
```

```python
import functools

import jax
import jax.numpy as jnp
from jax import lax
from jax.experimental import pallas as pl
from jax.experimental.pallas import tpu as pltpu
from jax.sharding import PartitionSpec as P

C = 128
BLOCK = 64
LANES = 128
SUB = 8
PARTS = 2


def layer_norm(values, axis):
    centre = jnp.mean(values, axis=axis, keepdims=True)
    spread = jnp.mean(jnp.square(values - centre), axis=axis, keepdims=True)
    return (values - centre) * lax.rsqrt(spread + 1e-05)


def swap_halves(values):
    flat = values.reshape(-1, LANES)
    return pltpu.roll(flat, LANES // 2, 1).reshape(values.shape)


def pack(low, high):
    lane = lax.broadcasted_iota(jnp.int32, low.shape, low.ndim - 1)
    return jnp.where(lane < LANES // 2, low, swap_halves(high))


def window_start(windowed):
    if not windowed:
        return 0
    return jnp.where(lax.axis_index("wide") * SUB < 3 * BLOCK, 0, BLOCK)


def chunks_of(rows):
    return ((0, LANES), (LANES, rows - LANES))


def project_kernel(mask_hbm, x_hbm, wl_hbm, wr_hbm, *refs):
    whole_ref, window_ref, normed_ref, cut_ref, mask_ref, x_ref, w_ref, edge, sems = refs
    group_size = whole_ref.shape[0]
    tokens = x_hbm.shape[0] // SUB
    copies = [
        pltpu.make_async_copy(x_hbm, x_ref.at[pl.ds(0, tokens * SUB)], sems.at[0]),
        pltpu.make_async_copy(mask_hbm, mask_ref, sems.at[1]),
        pltpu.make_async_copy(wl_hbm, w_ref.at[0], sems.at[2]),
        pltpu.make_async_copy(wr_hbm, w_ref.at[1], sems.at[3]),
    ]
    for copy in copies:
        copy.start()
    for copy in copies:
        copy.wait()
    cut = mask_ref[0, 3] == 0
    cut_ref[0] = cut.astype(jnp.int32)
    column_block = lax.axis_index("wide") * SUB // BLOCK
    kept = [mask_ref[block, column_block].astype(jnp.float32) for block in range(mask_hbm.shape[0])]
    weights = jnp.concatenate([w_ref[0].T, w_ref[1].T], axis=0)

    def project(windowed, send_ref):
        first = window_start(windowed)
        row_block = (first + lax.broadcasted_iota(jnp.int32, (1, 2 * LANES), 1)) // BLOCK
        mask = jnp.zeros((1, 2 * LANES), jnp.float32)
        for block, value in enumerate(kept):
            mask = jnp.where(row_block == block, value, mask)
        chunks = chunks_of(3 * BLOCK if windowed else tokens)
        for index, (low, count) in enumerate(chunks):
            group = 2 * LANES // count
            chunk_mask = jnp.concatenate([mask[:, low : low + count]] * group, axis=1)
            base = pl.multiple_of((first + low) * SUB, SUB)
            for start in range(0, SUB, group):
                x = [x_ref[pl.ds(base + start + k, count, stride=SUB), :] for k in range(group)]
                normed = layer_norm(jnp.concatenate(x, axis=0), 1).astype(jnp.bfloat16)
                for k in range(group):
                    normed_ref[start + k, low : low + count, :] = normed[k * count : (k + 1) * count]
                mixed = lax.dot_general(
                    weights, normed, (((1,), (1,)), ((), ())), preferred_element_type=jnp.float32
                )
                for side in range(2):
                    gate = mixed[2 * side * C : (2 * side + 1) * C]
                    value = mixed[(2 * side + 1) * C : (2 * side + 2) * C]
                    proj = jax.nn.sigmoid(gate) * value * chunk_mask
                    for k in range(group):
                        at = k * count // LANES * LANES
                        piece = proj[:, at : at + LANES]
                        if k * count % LANES:
                            piece = swap_halves(piece)
                        edge[side, index, pl.ds(start + k, C, stride=SUB), :] = piece
        part = C // group_size * SUB
        low = 0
        for side in range(2):
            for index, (_, count) in enumerate(chunks):
                values = edge[side, index, : C * SUB, :].reshape(group_size, part, LANES)
                if count < LANES:
                    values = pack(values[:, : part // 2], values[:, part // 2 :])
                send_ref[:, low : low + values.shape[1], :] = values.astype(jnp.bfloat16)
                low += values.shape[1]

    pl.when(cut)(lambda: project(True, window_ref))
    pl.when(jnp.logical_not(cut))(lambda: project(False, whole_ref))


def triangle_kernel(windowed, recv_ref, send_ref):
    group_size = recv_ref.shape[0]
    wide = send_ref.shape[0]
    per_device = C // group_size
    part = per_device * SUB
    columns = group_size * SUB
    half = per_device // 2

    def load(side, channel):
        parts = []
        for index in range(2):
            start = side * send_ref.shape[1] + index * part
            swap = windowed and index == 1 and channel >= half
            at = start + (channel - half if swap else channel) * SUB
            pair = recv_ref[:, at : at + 2 * SUB, :].astype(jnp.float32)
            if swap:
                pair = swap_halves(pair)
            parts.append([
                pair[:, low : low + SUB].reshape(columns, LANES).astype(jnp.bfloat16)
                for low in (0, SUB)
            ])
        return [jnp.concatenate([p[n] for p in parts], axis=1) for n in range(2)]

    def product(right, left):
        return lax.dot_general(
            right, left, (((0,), (0,)), ((), ())), preferred_element_type=jnp.float32
        )

    cut = 3 * BLOCK
    columns_first = lax.axis_index("wide") // group_size * columns
    column = columns_first + lax.broadcasted_iota(jnp.int32, (columns, 1), 0)
    sums = []
    for channel in range(0, per_device, 2):
        for left, right in zip(load(0, channel), load(1, channel)):
            if windowed:
                above = product(right, jnp.where(column < cut, left, 0))[:cut]
                below = product(right[:, LANES:], jnp.where(column < cut, 0, left))
                sums.append(jnp.concatenate([above, below[: wide * SUB - cut]], axis=0))
            else:
                sums.append(product(right, left))
    first = [s[:, :LANES] for s in sums]
    second = [s[:, LANES:] for s in sums]
    if windowed:
        second = [pack(second[c], second[c + half]) for c in range(half)]
    start = 0
    for channels in (first, second):
        for channel in range(0, len(channels), 2):
            pair = [channels[channel + n].reshape(wide, SUB, LANES) for n in range(2)]
            pair = jnp.concatenate(pair, axis=1).astype(jnp.bfloat16)
            send_ref[:, start : start + 2 * SUB, :] = pair
            start += 2 * SUB


def update_kernel(windowed, recv_ref, normed_ref, wg_ref, wo_ref, out_hbm, tri, out_ref, sems):
    group_size = recv_ref.shape[0] // PARTS
    part = C // group_size * SUB
    rows = 3 * BLOCK if windowed else normed_ref.shape[1]
    chunks = chunks_of(rows)
    first = window_start(windowed)
    copies = []
    if windowed:
        rest = out_hbm.shape[0] - rows * SUB
        to = pl.multiple_of(jnp.where(first == 0, rows, 0) * SUB, SUB)
        out_ref[pl.ds(rows * SUB, rest), :] = jnp.zeros((rest, C), jnp.float32)
        copies.append(
            pltpu.make_async_copy(
                out_ref.at[pl.ds(rows * SUB, rest)], out_hbm.at[pl.ds(to, rest)], sems.at[2]
            )
        )
        copies[0].start()
    for index, (low, count) in enumerate(chunks):
        height = part * count // LANES
        sums = [
            recv_ref[n * group_size : (n + 1) * group_size, index * part : index * part + height, :]
            for n in range(PARTS)
        ]
        sums = sum(values.astype(jnp.float32) for values in sums)
        if count < LANES:
            sums = jnp.concatenate([sums, swap_halves(sums)], axis=1)
        tri[index, : C * SUB, :] = layer_norm(sums.reshape(C, SUB, LANES), 0).reshape(C * SUB, LANES)
        for j in range(SUB):
            tri_normed = tri[index, pl.ds(j, C, stride=SUB), :].astype(jnp.bfloat16)
            mixed = lax.dot_general(
                tri_normed, wo_ref[...], (((0,), (0,)), ((), ())), preferred_element_type=jnp.float32
            )
            normed = normed_ref[j, low : low + count, :]
            gate = jax.nn.sigmoid(
                jnp.dot(normed, wg_ref[...], preferred_element_type=jnp.float32)
            )
            out_ref[pl.ds(low * SUB + j, count, stride=SUB), :] = gate * mixed[:count]
        to = pl.multiple_of((first + low) * SUB, SUB)
        copies.append(
            pltpu.make_async_copy(
                out_ref.at[pl.ds(low * SUB, count * SUB)],
                out_hbm.at[pl.ds(to, count * SUB)],
                sems.at[index],
            )
        )
        copies[-1].start()
    for copy in copies:
        copy.wait()


HBM = pl.BlockSpec(memory_space=pltpu.HBM)
VMEM = pl.BlockSpec(memory_space=pltpu.VMEM)
PARAMS = pltpu.CompilerParams(vmem_limit_bytes=48 * 1024 * 1024)


def in_hbm(array):
    return pltpu.with_memory_space_constraint(array, pltpu.HBM)


def exchange(array):
    wide, size = lax.axis_size("wide"), array.shape[0]
    groups = [list(range(first, first + size)) for first in range(0, wide, size)]
    return lax.all_to_all(
        array, "wide", split_axis=0, concat_axis=0, axis_index_groups=groups, tiled=True
    )


def after_projection(windowed, whole, window, normed, gate_weight, out_weight):
    send = window if windowed else whole
    group_size, both, _ = send.shape
    wide = group_size * PARTS
    tokens = normed.shape[1]
    back = pl.pallas_call(
        functools.partial(triangle_kernel, windowed),
        out_shape=jax.ShapeDtypeStruct((wide, both // 2, LANES), jnp.bfloat16),
        in_specs=[VMEM],
        out_specs=VMEM,
        compiler_params=PARAMS,
        name="triangle",
    )(exchange(send))
    return pl.pallas_call(
        functools.partial(update_kernel, windowed),
        out_shape=pltpu.HBM((tokens * SUB, C), jnp.float32),
        in_specs=[VMEM] * 4,
        out_specs=HBM,
        scratch_shapes=[
            pltpu.VMEM((2, C * SUB + SUB, LANES), jnp.float32),
            pltpu.VMEM((tokens * SUB + SUB, C), jnp.float32),
            pltpu.SemaphoreType.DMA((3,)),
        ],
        compiler_params=PARAMS,
        name="update",
    )(exchange(back), normed, gate_weight, out_weight)


def kernels_on_device(pair_act, block_mask, left_weight, right_weight, gate_weight, out_weight):
    tokens = pair_act.shape[0]
    wide = lax.axis_size("wide")
    group_size = wide // PARTS
    both = lambda rows: 2 * rows * (C // group_size) * SUB // LANES
    whole, window, normed, cut = pl.pallas_call(
        project_kernel,
        out_shape=(
            jax.ShapeDtypeStruct((group_size, both(tokens), LANES), jnp.bfloat16),
            jax.ShapeDtypeStruct((group_size, both(3 * BLOCK), LANES), jnp.bfloat16),
            jax.ShapeDtypeStruct((SUB, tokens, C), jnp.bfloat16),
            pltpu.SMEM((1,), jnp.int32),
        ),
        in_specs=[HBM] * 4,
        out_specs=(VMEM, VMEM, VMEM, pl.BlockSpec(memory_space=pltpu.SMEM)),
        scratch_shapes=[
            pltpu.SMEM(block_mask.shape, jnp.int32),
            pltpu.VMEM((tokens * SUB + SUB, C), jnp.float32),
            pltpu.VMEM((2, C, 2 * C), jnp.bfloat16),
            pltpu.VMEM((2, 2, C * SUB + SUB, LANES), jnp.float32),
            pltpu.SemaphoreType.DMA((4,)),
        ],
        compiler_params=PARAMS,
        name="project",
    )(
        in_hbm(block_mask),
        in_hbm(pair_act.reshape(tokens * SUB, C)),
        in_hbm(left_weight),
        in_hbm(right_weight),
    )
    update = lax.switch(
        cut[0],
        [functools.partial(after_projection, windowed) for windowed in (False, True)],
        whole,
        window,
        normed,
        gate_weight,
        out_weight,
    )
    return update.reshape(tokens, SUB, C)


def plain_on_device(pair_act, block_mask, left_weight, right_weight, gate_weight, out_weight):
    tile_rows = pair_act.shape[0]
    tile_cols = pair_act.shape[1]
    wide = lax.axis_size("wide")
    narrow = lax.axis_size("narrow")
    per_device = C // wide
    row_ids = lax.axis_index("narrow") * tile_rows + jnp.arange(tile_rows, dtype=jnp.int32)
    col_ids = lax.axis_index("wide") * tile_cols + jnp.arange(tile_cols, dtype=jnp.int32)
    block_ids = jnp.arange(block_mask.shape[0], dtype=jnp.int32)
    row_hot = (row_ids[:, None] // BLOCK == block_ids[None, :]).astype(jnp.float32)
    col_hot = (col_ids[:, None] // BLOCK == block_ids[None, :]).astype(jnp.float32)
    tile_mask = jnp.dot(jnp.dot(row_hot, block_mask.astype(jnp.float32)), col_hot.T).T
    normed = layer_norm(pair_act, -1).astype(jnp.bfloat16)

    def edges(weight):
        mixed = jnp.einsum("cd,ikc->dki", weight, normed, preferred_element_type=jnp.float32)
        proj = jax.nn.sigmoid(mixed[:C]) * mixed[C:] * tile_mask[None]
        return proj.astype(jnp.bfloat16).reshape(wide, per_device, tile_cols, tile_rows)

    send = jnp.stack([edges(left_weight), edges(right_weight)], axis=1)
    recv = lax.all_to_all(send, "wide", split_axis=0, concat_axis=0, tiled=True)
    left, right = recv[:, 0], recv[:, 1]
    if narrow > 1:
        right = lax.all_gather(right, "narrow", axis=3, tiled=True)
    tri = jnp.einsum("sckj,scki->cji", right, left, preferred_element_type=jnp.float32)
    back = tri.astype(jnp.bfloat16).reshape(per_device, wide, tile_cols, tile_rows)
    back = jnp.transpose(back, (1, 0, 2, 3))
    tri = lax.all_to_all(back, "wide", split_axis=0, concat_axis=0, tiled=True)
    tri = tri.reshape(C, tile_cols, tile_rows).astype(jnp.float32)
    tri_normed = layer_norm(tri, 0).astype(jnp.bfloat16)
    gate = jax.nn.sigmoid(
        jnp.einsum("ikc,cd->ikd", normed, gate_weight, preferred_element_type=jnp.float32)
    )
    return gate * jnp.einsum(
        "cji,cd->ijd", tri_normed, out_weight, preferred_element_type=jnp.float32
    )


def on_device(pair_act, block_mask, *weights):
    rows, cols = pair_act.shape[:2]
    blocks = block_mask.shape[0]
    fits = rows == 2 * LANES and cols == SUB and C // lax.axis_size("wide") == 4 and blocks == 4
    if lax.axis_size("narrow") > 1 or not fits:
        return plain_on_device(pair_act, block_mask, *weights)
    return kernels_on_device(pair_act, block_mask, *weights)


def solution(mesh):
    return jax.shard_map(
        on_device,
        mesh=mesh,
        in_specs=(P("narrow", "wide", None), P(), P(), P(), P(), P()),
        out_specs=P("narrow", "wide", None),
        check_vma=False,
    )
```

```python
import functools

import jax
import jax.numpy as jnp
from jax import lax
from jax.experimental import pallas as pl
from jax.experimental.pallas import tpu as pltpu
from jax.sharding import PartitionSpec as P

C = 128
BLOCK = 64
LANES = 128
SUB = 8
PARTS = 2


def layer_norm(values, axis):
    centre = jnp.mean(values, axis=axis, keepdims=True)
    spread = jnp.mean(jnp.square(values - centre), axis=axis, keepdims=True)
    return (values - centre) * lax.rsqrt(spread + 1e-05)


def swap_halves(values):
    flat = values.reshape(-1, LANES)
    return pltpu.roll(flat, LANES // 2, 1).reshape(values.shape)


def pack(low, high):
    lane = lax.broadcasted_iota(jnp.int32, low.shape, low.ndim - 1)
    return jnp.where(lane < LANES // 2, low, swap_halves(high))


def window_start(windowed):
    if not windowed:
        return 0
    return jnp.where(lax.axis_index("wide") * SUB < 3 * BLOCK, 0, BLOCK)


def chunks_of(rows):
    return ((0, LANES), (LANES, rows - LANES))


def project_kernel(mask_hbm, x_hbm, wl_hbm, wr_hbm, *refs):
    whole_ref, window_ref, normed_ref, cut_ref, mask_ref, x_ref, w_ref, edge, sems = refs
    group_size = whole_ref.shape[0]
    tokens = x_hbm.shape[0] // SUB
    copies = [
        pltpu.make_async_copy(mask_hbm, mask_ref, sems.at[0]),
        pltpu.make_async_copy(wl_hbm, w_ref.at[0], sems.at[1]),
        pltpu.make_async_copy(wr_hbm, w_ref.at[1], sems.at[2]),
    ]
    for index in range(2):
        part = pl.ds(index * LANES * SUB, LANES * SUB)
        copies.append(pltpu.make_async_copy(x_hbm.at[part], x_ref.at[part], sems.at[3 + index]))
    for copy in copies:
        copy.start()
    copies[0].wait()
    cut = mask_ref[0, 3] == 0
    cut_ref[0] = cut.astype(jnp.int32)
    column_block = lax.axis_index("wide") * SUB // BLOCK
    kept = [mask_ref[block, column_block].astype(jnp.float32) for block in range(mask_hbm.shape[0])]
    copies[1].wait()
    copies[2].wait()
    weights = jnp.concatenate([w_ref[0].T, w_ref[1].T], axis=0)

    def project(windowed, send_ref):
        first = window_start(windowed)
        row_block = (first + lax.broadcasted_iota(jnp.int32, (1, 2 * LANES), 1)) // BLOCK
        mask = jnp.zeros((1, 2 * LANES), jnp.float32)
        for block, value in enumerate(kept):
            mask = jnp.where(row_block == block, value, mask)
        if windowed:
            copies[3].wait()
            copies[4].wait()
        chunks = chunks_of(3 * BLOCK if windowed else tokens)
        for index, (low, count) in enumerate(chunks):
            if not windowed:
                copies[3 + index].wait()
            group = 2 * LANES // count
            chunk_mask = jnp.concatenate([mask[:, low : low + count]] * group, axis=1)
            base = pl.multiple_of((first + low) * SUB, SUB)
            for start in range(0, SUB, group):
                x = [x_ref[pl.ds(base + start + k, count, stride=SUB), :] for k in range(group)]
                normed = layer_norm(jnp.concatenate(x, axis=0), 1).astype(jnp.bfloat16)
                for k in range(group):
                    normed_ref[start + k, low : low + count, :] = normed[k * count : (k + 1) * count]
                mixed = lax.dot_general(
                    weights, normed, (((1,), (1,)), ((), ())), preferred_element_type=jnp.float32
                )
                for side in range(2):
                    gate = mixed[2 * side * C : (2 * side + 1) * C]
                    value = mixed[(2 * side + 1) * C : (2 * side + 2) * C]
                    proj = jax.nn.sigmoid(gate) * value * chunk_mask
                    for k in range(group):
                        at = k * count // LANES * LANES
                        piece = proj[:, at : at + LANES]
                        if k * count % LANES:
                            piece = swap_halves(piece)
                        edge[side, index, pl.ds(start + k, C, stride=SUB), :] = piece
        part = C // group_size * SUB
        low = 0
        for side in range(2):
            for index, (_, count) in enumerate(chunks):
                values = edge[side, index, : C * SUB, :].reshape(group_size, part, LANES)
                if count < LANES:
                    values = pack(values[:, : part // 2], values[:, part // 2 :])
                send_ref[:, low : low + values.shape[1], :] = values.astype(jnp.bfloat16)
                low += values.shape[1]

    pl.when(cut)(lambda: project(True, window_ref))
    pl.when(jnp.logical_not(cut))(lambda: project(False, whole_ref))


def triangle_kernel(windowed, recv_ref, send_ref):
    group_size = recv_ref.shape[0]
    wide = send_ref.shape[0]
    per_device = C // group_size
    part = per_device * SUB
    columns = group_size * SUB
    half = per_device // 2

    def load(side, channel):
        parts = []
        for index in range(2):
            start = side * send_ref.shape[1] + index * part
            swap = windowed and index == 1 and channel >= half
            at = start + (channel - half if swap else channel) * SUB
            pair = recv_ref[:, at : at + 2 * SUB, :].astype(jnp.float32)
            if swap:
                pair = swap_halves(pair)
            parts.append([
                pair[:, low : low + SUB].reshape(columns, LANES).astype(jnp.bfloat16)
                for low in (0, SUB)
            ])
        return [jnp.concatenate([p[n] for p in parts], axis=1) for n in range(2)]

    def product(right, left):
        return lax.dot_general(
            right, left, (((0,), (0,)), ((), ())), preferred_element_type=jnp.float32
        )

    cut = 3 * BLOCK
    columns_first = lax.axis_index("wide") // group_size * columns
    column = columns_first + lax.broadcasted_iota(jnp.int32, (columns, 1), 0)
    sums = []
    for channel in range(0, per_device, 2):
        for left, right in zip(load(0, channel), load(1, channel)):
            if windowed:
                above = product(right, jnp.where(column < cut, left, 0))[:cut]
                below = product(right[:, LANES:], jnp.where(column < cut, 0, left))
                sums.append(jnp.concatenate([above, below[: wide * SUB - cut]], axis=0))
            else:
                sums.append(product(right, left))
    first = [s[:, :LANES] for s in sums]
    second = [s[:, LANES:] for s in sums]
    if windowed:
        second = [pack(second[c], second[c + half]) for c in range(half)]
    start = 0
    for channels in (first, second):
        for channel in range(0, len(channels), 2):
            pair = [channels[channel + n].reshape(wide, SUB, LANES) for n in range(2)]
            pair = jnp.concatenate(pair, axis=1).astype(jnp.bfloat16)
            send_ref[:, start : start + 2 * SUB, :] = pair
            start += 2 * SUB


def update_kernel(windowed, recv_ref, normed_ref, wg_ref, wo_ref, out_hbm, tri, out_ref, sems):
    group_size = recv_ref.shape[0] // PARTS
    part = C // group_size * SUB
    rows = 3 * BLOCK if windowed else normed_ref.shape[1]
    chunks = chunks_of(rows)
    first = window_start(windowed)
    copies = []
    if windowed:
        rest = out_hbm.shape[0] - rows * SUB
        to = pl.multiple_of(jnp.where(first == 0, rows, 0) * SUB, SUB)
        out_ref[pl.ds(rows * SUB, rest), :] = jnp.zeros((rest, C), jnp.float32)
        copies.append(
            pltpu.make_async_copy(
                out_ref.at[pl.ds(rows * SUB, rest)], out_hbm.at[pl.ds(to, rest)], sems.at[2]
            )
        )
        copies[0].start()
    for index, (low, count) in enumerate(chunks):
        height = part * count // LANES
        sums = [
            recv_ref[n * group_size : (n + 1) * group_size, index * part : index * part + height, :]
            for n in range(PARTS)
        ]
        sums = sum(values.astype(jnp.float32) for values in sums)
        if count < LANES:
            sums = jnp.concatenate([sums, swap_halves(sums)], axis=1)
        tri[index, : C * SUB, :] = layer_norm(sums.reshape(C, SUB, LANES), 0).reshape(C * SUB, LANES)
        for j in range(SUB):
            tri_normed = tri[index, pl.ds(j, C, stride=SUB), :].astype(jnp.bfloat16)
            mixed = lax.dot_general(
                tri_normed, wo_ref[...], (((0,), (0,)), ((), ())), preferred_element_type=jnp.float32
            )
            normed = normed_ref[j, low : low + count, :]
            gate = jax.nn.sigmoid(
                jnp.dot(normed, wg_ref[...], preferred_element_type=jnp.float32)
            )
            out_ref[pl.ds(low * SUB + j, count, stride=SUB), :] = gate * mixed[:count]
        to = pl.multiple_of((first + low) * SUB, SUB)
        copies.append(
            pltpu.make_async_copy(
                out_ref.at[pl.ds(low * SUB, count * SUB)],
                out_hbm.at[pl.ds(to, count * SUB)],
                sems.at[index],
            )
        )
        copies[-1].start()
    for copy in copies:
        copy.wait()


HBM = pl.BlockSpec(memory_space=pltpu.HBM)
VMEM = pl.BlockSpec(memory_space=pltpu.VMEM)
PARAMS = pltpu.CompilerParams(vmem_limit_bytes=48 * 1024 * 1024)


def in_hbm(array):
    return pltpu.with_memory_space_constraint(array, pltpu.HBM)


def exchange(array):
    wide, size = lax.axis_size("wide"), array.shape[0]
    groups = [list(range(first, first + size)) for first in range(0, wide, size)]
    return lax.all_to_all(
        array, "wide", split_axis=0, concat_axis=0, axis_index_groups=groups, tiled=True
    )


def after_projection(windowed, whole, window, normed, gate_weight, out_weight):
    send = window if windowed else whole
    group_size, both, _ = send.shape
    wide = group_size * PARTS
    tokens = normed.shape[1]
    back = pl.pallas_call(
        functools.partial(triangle_kernel, windowed),
        out_shape=jax.ShapeDtypeStruct((wide, both // 2, LANES), jnp.bfloat16),
        in_specs=[VMEM],
        out_specs=VMEM,
        compiler_params=PARAMS,
        name="triangle",
    )(exchange(send))
    return pl.pallas_call(
        functools.partial(update_kernel, windowed),
        out_shape=pltpu.HBM((tokens * SUB, C), jnp.float32),
        in_specs=[VMEM] * 4,
        out_specs=HBM,
        scratch_shapes=[
            pltpu.VMEM((2, C * SUB + SUB, LANES), jnp.float32),
            pltpu.VMEM((tokens * SUB + SUB, C), jnp.float32),
            pltpu.SemaphoreType.DMA((3,)),
        ],
        compiler_params=PARAMS,
        name="update",
    )(exchange(back), normed, gate_weight, out_weight)


def kernels_on_device(pair_act, block_mask, left_weight, right_weight, gate_weight, out_weight):
    tokens = pair_act.shape[0]
    wide = lax.axis_size("wide")
    group_size = wide // PARTS
    both = lambda rows: 2 * rows * (C // group_size) * SUB // LANES
    whole, window, normed, cut = pl.pallas_call(
        project_kernel,
        out_shape=(
            jax.ShapeDtypeStruct((group_size, both(tokens), LANES), jnp.bfloat16),
            jax.ShapeDtypeStruct((group_size, both(3 * BLOCK), LANES), jnp.bfloat16),
            jax.ShapeDtypeStruct((SUB, tokens, C), jnp.bfloat16),
            pltpu.SMEM((1,), jnp.int32),
        ),
        in_specs=[HBM] * 4,
        out_specs=(VMEM, VMEM, VMEM, pl.BlockSpec(memory_space=pltpu.SMEM)),
        scratch_shapes=[
            pltpu.SMEM(block_mask.shape, jnp.int32),
            pltpu.VMEM((tokens * SUB + SUB, C), jnp.float32),
            pltpu.VMEM((2, C, 2 * C), jnp.bfloat16),
            pltpu.VMEM((2, 2, C * SUB + SUB, LANES), jnp.float32),
            pltpu.SemaphoreType.DMA((5,)),
        ],
        compiler_params=PARAMS,
        name="project",
    )(
        in_hbm(block_mask),
        in_hbm(pair_act.reshape(tokens * SUB, C)),
        in_hbm(left_weight),
        in_hbm(right_weight),
    )
    update = lax.switch(
        cut[0],
        [functools.partial(after_projection, windowed) for windowed in (False, True)],
        whole,
        window,
        normed,
        gate_weight,
        out_weight,
    )
    return update.reshape(tokens, SUB, C)


def plain_on_device(pair_act, block_mask, left_weight, right_weight, gate_weight, out_weight):
    tile_rows = pair_act.shape[0]
    tile_cols = pair_act.shape[1]
    wide = lax.axis_size("wide")
    narrow = lax.axis_size("narrow")
    per_device = C // wide
    row_ids = lax.axis_index("narrow") * tile_rows + jnp.arange(tile_rows, dtype=jnp.int32)
    col_ids = lax.axis_index("wide") * tile_cols + jnp.arange(tile_cols, dtype=jnp.int32)
    block_ids = jnp.arange(block_mask.shape[0], dtype=jnp.int32)
    row_hot = (row_ids[:, None] // BLOCK == block_ids[None, :]).astype(jnp.float32)
    col_hot = (col_ids[:, None] // BLOCK == block_ids[None, :]).astype(jnp.float32)
    tile_mask = jnp.dot(jnp.dot(row_hot, block_mask.astype(jnp.float32)), col_hot.T).T
    normed = layer_norm(pair_act, -1).astype(jnp.bfloat16)

    def edges(weight):
        mixed = jnp.einsum("cd,ikc->dki", weight, normed, preferred_element_type=jnp.float32)
        proj = jax.nn.sigmoid(mixed[:C]) * mixed[C:] * tile_mask[None]
        return proj.astype(jnp.bfloat16).reshape(wide, per_device, tile_cols, tile_rows)

    send = jnp.stack([edges(left_weight), edges(right_weight)], axis=1)
    recv = lax.all_to_all(send, "wide", split_axis=0, concat_axis=0, tiled=True)
    left, right = recv[:, 0], recv[:, 1]
    if narrow > 1:
        right = lax.all_gather(right, "narrow", axis=3, tiled=True)
    tri = jnp.einsum("sckj,scki->cji", right, left, preferred_element_type=jnp.float32)
    back = tri.astype(jnp.bfloat16).reshape(per_device, wide, tile_cols, tile_rows)
    back = jnp.transpose(back, (1, 0, 2, 3))
    tri = lax.all_to_all(back, "wide", split_axis=0, concat_axis=0, tiled=True)
    tri = tri.reshape(C, tile_cols, tile_rows).astype(jnp.float32)
    tri_normed = layer_norm(tri, 0).astype(jnp.bfloat16)
    gate = jax.nn.sigmoid(
        jnp.einsum("ikc,cd->ikd", normed, gate_weight, preferred_element_type=jnp.float32)
    )
    return gate * jnp.einsum(
        "cji,cd->ijd", tri_normed, out_weight, preferred_element_type=jnp.float32
    )


def on_device(pair_act, block_mask, *weights):
    rows, cols = pair_act.shape[:2]
    blocks = block_mask.shape[0]
    fits = rows == 2 * LANES and cols == SUB and C // lax.axis_size("wide") == 4 and blocks == 4
    if lax.axis_size("narrow") > 1 or not fits:
        return plain_on_device(pair_act, block_mask, *weights)
    return kernels_on_device(pair_act, block_mask, *weights)


def solution(mesh):
    return jax.shard_map(
        on_device,
        mesh=mesh,
        in_specs=(P("narrow", "wide", None), P(), P(), P(), P(), P()),
        out_specs=P("narrow", "wide", None),
        check_vma=False,
    )
```

```python
import functools

import jax
import jax.numpy as jnp
from jax import lax
from jax.experimental import pallas as pl
from jax.experimental.pallas import tpu as pltpu
from jax.sharding import PartitionSpec as P

C = 128
BLOCK = 64
LANES = 128
SUB = 8
PARTS = 2


def layer_norm(values, axis):
    centre = jnp.mean(values, axis=axis, keepdims=True)
    spread = jnp.mean(jnp.square(values - centre), axis=axis, keepdims=True)
    return (values - centre) * lax.rsqrt(spread + 1e-05)


def swap_halves(values):
    flat = values.reshape(-1, LANES)
    return pltpu.roll(flat, LANES // 2, 1).reshape(values.shape)


def pack(low, high):
    lane = lax.broadcasted_iota(jnp.int32, low.shape, low.ndim - 1)
    return jnp.where(lane < LANES // 2, low, swap_halves(high))


def window_start(windowed):
    if not windowed:
        return 0
    return jnp.where(lax.axis_index("wide") * SUB < 3 * BLOCK, 0, BLOCK)


def chunks_of(rows):
    return ((0, LANES), (LANES, rows - LANES))


def project_kernel(mask_hbm, x_hbm, wl_hbm, wr_hbm, *refs):
    whole_ref, window_ref, normed_ref, cut_ref, mask_ref, x_ref, w_ref, sems = refs
    group_size = whole_ref.shape[0]
    tokens = x_hbm.shape[0] // SUB
    copies = [
        pltpu.make_async_copy(mask_hbm, mask_ref, sems.at[0]),
        pltpu.make_async_copy(wl_hbm, w_ref.at[0], sems.at[1]),
        pltpu.make_async_copy(wr_hbm, w_ref.at[1], sems.at[2]),
    ]
    for index in range(2):
        part = pl.ds(index * LANES * SUB, LANES * SUB)
        copies.append(pltpu.make_async_copy(x_hbm.at[part], x_ref.at[part], sems.at[3 + index]))
    for copy in copies:
        copy.start()
    copies[0].wait()
    cut = mask_ref[0, 3] == 0
    cut_ref[0] = cut.astype(jnp.int32)
    column_block = lax.axis_index("wide") * SUB // BLOCK
    kept = [mask_ref[block, column_block].astype(jnp.float32) for block in range(mask_hbm.shape[0])]
    copies[1].wait()
    copies[2].wait()
    weights = jnp.concatenate([w_ref[0].T, w_ref[1].T], axis=0)

    def project(windowed, send_ref):
        first = window_start(windowed)
        row_block = (first + lax.broadcasted_iota(jnp.int32, (1, 2 * LANES), 1)) // BLOCK
        mask = jnp.zeros((1, 2 * LANES), jnp.float32)
        for block, value in enumerate(kept):
            mask = jnp.where(row_block == block, value, mask)
        if windowed:
            copies[3].wait()
            copies[4].wait()
        chunks = chunks_of(3 * BLOCK if windowed else tokens)
        for index, (low, count) in enumerate(chunks):
            if not windowed:
                copies[3 + index].wait()
            group = 2 * LANES // count
            chunk_mask = jnp.concatenate([mask[:, low : low + count]] * group, axis=1)
            base = pl.multiple_of((first + low) * SUB, SUB)
            for start in range(0, SUB, group):
                x = [x_ref[pl.ds(base + start + k, count, stride=SUB), :] for k in range(group)]
                normed = layer_norm(jnp.concatenate(x, axis=0), 1).astype(jnp.bfloat16)
                for k in range(group):
                    normed_ref[start + k, low : low + count, :] = normed[k * count : (k + 1) * count]
                mixed = lax.dot_general(
                    weights, normed, (((1,), (1,)), ((), ())), preferred_element_type=jnp.float32
                )
                for side in range(2):
                    gate = mixed[2 * side * C : (2 * side + 1) * C]
                    value = mixed[(2 * side + 1) * C : (2 * side + 2) * C]
                    proj = jax.nn.sigmoid(gate) * value * chunk_mask
                    pair = jnp.concatenate(
                        [
                            proj[:, at : at + LANES].reshape(group_size, SUB, LANES)
                            for at in (0, LANES)
                        ],
                        axis=1,
                    )
                    place = side * send_ref.shape[1] // 2 + index * SUB * SUB + start // group * 2 * SUB
                    send_ref[:, place : place + 2 * SUB, :] = pair.astype(jnp.bfloat16)

    pl.when(cut)(lambda: project(True, window_ref))
    pl.when(jnp.logical_not(cut))(lambda: project(False, whole_ref))


def triangle_kernel(windowed, recv_ref, send_ref, edge):
    group_size = recv_ref.shape[0]
    wide = send_ref.shape[0]
    per_device = C // group_size
    part = per_device * SUB
    columns = group_size * SUB
    half = per_device // 2
    side_rows = send_ref.shape[1]
    for side in range(2):
        for index in range(2):
            height = min(part, side_rows - index * part)
            start = side * side_rows + index * part
            values = recv_ref[:, start : start + height, :].astype(jnp.float32)
            edge[side, index, : group_size * height, :] = values.reshape(group_size * height, LANES)

    def load(side, channel):
        parts = []
        for parity in range(2):
            rows = pl.ds(parity * SUB + channel, columns // 2, stride=2 * SUB)
            first = edge[side, 0, rows, :]
            if windowed:
                second = edge[side, 1, pl.ds(channel, columns // 2, stride=SUB), :]
                if parity:
                    second = swap_halves(second)
            else:
                second = edge[side, 1, rows, :]
            parts.append(jnp.concatenate([first, second], axis=1))
        return jnp.concatenate(parts, axis=0).astype(jnp.bfloat16)

    def product(right, left):
        return lax.dot_general(
            right, left, (((0,), (0,)), ((), ())), preferred_element_type=jnp.float32
        )

    cut = 3 * BLOCK
    columns_first = lax.axis_index("wide") // group_size * columns
    place = lax.broadcasted_iota(jnp.int32, (columns, 1), 0) % (columns // 2)
    column = columns_first + 2 * place
    sums = []
    for channel in range(per_device):
        left, right = load(0, channel), load(1, channel)
        if windowed:
            above = product(right, jnp.where(column < cut, left, 0))[:cut]
            below = product(right[:, LANES:], jnp.where(column < cut, 0, left))
            sums.append(jnp.concatenate([above, below[: wide * SUB - cut]], axis=0))
        else:
            sums.append(product(right, left))
    first = [s[:, :LANES] for s in sums]
    second = [s[:, LANES:] for s in sums]
    if windowed:
        second = [pack(second[c], second[c + half]) for c in range(half)]
    start = 0
    for channels in (first, second):
        for channel in range(0, len(channels), 2):
            pair = [channels[channel + n].reshape(wide, SUB, LANES) for n in range(2)]
            pair = jnp.concatenate(pair, axis=1).astype(jnp.bfloat16)
            send_ref[:, start : start + 2 * SUB, :] = pair
            start += 2 * SUB


def update_kernel(windowed, recv_ref, normed_ref, wg_ref, wo_ref, out_hbm, tri, out_ref, sems):
    group_size = recv_ref.shape[0] // PARTS
    part = C // group_size * SUB
    rows = 3 * BLOCK if windowed else normed_ref.shape[1]
    chunks = chunks_of(rows)
    first = window_start(windowed)
    copies = []
    if windowed:
        rest = out_hbm.shape[0] - rows * SUB
        to = pl.multiple_of(jnp.where(first == 0, rows, 0) * SUB, SUB)
        out_ref[pl.ds(rows * SUB, rest), :] = jnp.zeros((rest, C), jnp.float32)
        copies.append(
            pltpu.make_async_copy(
                out_ref.at[pl.ds(rows * SUB, rest)], out_hbm.at[pl.ds(to, rest)], sems.at[2]
            )
        )
        copies[0].start()
    for index, (low, count) in enumerate(chunks):
        height = part * count // LANES
        sums = [
            recv_ref[n * group_size : (n + 1) * group_size, index * part : index * part + height, :]
            for n in range(PARTS)
        ]
        sums = sum(values.astype(jnp.float32) for values in sums)
        if count < LANES:
            sums = jnp.concatenate([sums, swap_halves(sums)], axis=1)
        tri[index, : C * SUB, :] = layer_norm(sums.reshape(C, SUB, LANES), 0).reshape(C * SUB, LANES)
        for j in range(SUB):
            tri_normed = tri[index, pl.ds(j, C, stride=SUB), :].astype(jnp.bfloat16)
            mixed = lax.dot_general(
                tri_normed, wo_ref[...], (((0,), (0,)), ((), ())), preferred_element_type=jnp.float32
            )
            normed = normed_ref[j, low : low + count, :]
            gate = jax.nn.sigmoid(
                jnp.dot(normed, wg_ref[...], preferred_element_type=jnp.float32)
            )
            out_ref[pl.ds(low * SUB + j, count, stride=SUB), :] = gate * mixed[:count]
        to = pl.multiple_of((first + low) * SUB, SUB)
        copies.append(
            pltpu.make_async_copy(
                out_ref.at[pl.ds(low * SUB, count * SUB)],
                out_hbm.at[pl.ds(to, count * SUB)],
                sems.at[index],
            )
        )
        copies[-1].start()
    for copy in copies:
        copy.wait()


HBM = pl.BlockSpec(memory_space=pltpu.HBM)
VMEM = pl.BlockSpec(memory_space=pltpu.VMEM)
PARAMS = pltpu.CompilerParams(vmem_limit_bytes=48 * 1024 * 1024)


def in_hbm(array):
    return pltpu.with_memory_space_constraint(array, pltpu.HBM)


def exchange(array):
    wide, size = lax.axis_size("wide"), array.shape[0]
    groups = [list(range(first, first + size)) for first in range(0, wide, size)]
    return lax.all_to_all(
        array, "wide", split_axis=0, concat_axis=0, axis_index_groups=groups, tiled=True
    )


def after_projection(windowed, whole, window, normed, gate_weight, out_weight):
    send = window if windowed else whole
    group_size, both, _ = send.shape
    wide = group_size * PARTS
    tokens = normed.shape[1]
    back = pl.pallas_call(
        functools.partial(triangle_kernel, windowed),
        out_shape=jax.ShapeDtypeStruct((wide, both // 2, LANES), jnp.bfloat16),
        in_specs=[VMEM],
        out_specs=VMEM,
        scratch_shapes=[pltpu.VMEM((2, 2, C * SUB + 2 * SUB, LANES), jnp.float32)],
        compiler_params=PARAMS,
        name="triangle",
    )(exchange(send))
    return pl.pallas_call(
        functools.partial(update_kernel, windowed),
        out_shape=pltpu.HBM((tokens * SUB, C), jnp.float32),
        in_specs=[VMEM] * 4,
        out_specs=HBM,
        scratch_shapes=[
            pltpu.VMEM((2, C * SUB + SUB, LANES), jnp.float32),
            pltpu.VMEM((tokens * SUB + SUB, C), jnp.float32),
            pltpu.SemaphoreType.DMA((3,)),
        ],
        compiler_params=PARAMS,
        name="update",
    )(exchange(back), normed, gate_weight, out_weight)


def kernels_on_device(pair_act, block_mask, left_weight, right_weight, gate_weight, out_weight):
    tokens = pair_act.shape[0]
    wide = lax.axis_size("wide")
    group_size = wide // PARTS
    both = lambda rows: 2 * rows * (C // group_size) * SUB // LANES
    whole, window, normed, cut = pl.pallas_call(
        project_kernel,
        out_shape=(
            jax.ShapeDtypeStruct((group_size, both(tokens), LANES), jnp.bfloat16),
            jax.ShapeDtypeStruct((group_size, both(3 * BLOCK), LANES), jnp.bfloat16),
            jax.ShapeDtypeStruct((SUB, tokens, C), jnp.bfloat16),
            pltpu.SMEM((1,), jnp.int32),
        ),
        in_specs=[HBM] * 4,
        out_specs=(VMEM, VMEM, VMEM, pl.BlockSpec(memory_space=pltpu.SMEM)),
        scratch_shapes=[
            pltpu.SMEM(block_mask.shape, jnp.int32),
            pltpu.VMEM((tokens * SUB + SUB, C), jnp.float32),
            pltpu.VMEM((2, C, 2 * C), jnp.bfloat16),
            pltpu.SemaphoreType.DMA((5,)),
        ],
        compiler_params=PARAMS,
        name="project",
    )(
        in_hbm(block_mask),
        in_hbm(pair_act.reshape(tokens * SUB, C)),
        in_hbm(left_weight),
        in_hbm(right_weight),
    )
    update = lax.switch(
        cut[0],
        [functools.partial(after_projection, windowed) for windowed in (False, True)],
        whole,
        window,
        normed,
        gate_weight,
        out_weight,
    )
    return update.reshape(tokens, SUB, C)


def plain_on_device(pair_act, block_mask, left_weight, right_weight, gate_weight, out_weight):
    tile_rows = pair_act.shape[0]
    tile_cols = pair_act.shape[1]
    wide = lax.axis_size("wide")
    narrow = lax.axis_size("narrow")
    per_device = C // wide
    row_ids = lax.axis_index("narrow") * tile_rows + jnp.arange(tile_rows, dtype=jnp.int32)
    col_ids = lax.axis_index("wide") * tile_cols + jnp.arange(tile_cols, dtype=jnp.int32)
    block_ids = jnp.arange(block_mask.shape[0], dtype=jnp.int32)
    row_hot = (row_ids[:, None] // BLOCK == block_ids[None, :]).astype(jnp.float32)
    col_hot = (col_ids[:, None] // BLOCK == block_ids[None, :]).astype(jnp.float32)
    tile_mask = jnp.dot(jnp.dot(row_hot, block_mask.astype(jnp.float32)), col_hot.T).T
    normed = layer_norm(pair_act, -1).astype(jnp.bfloat16)

    def edges(weight):
        mixed = jnp.einsum("cd,ikc->dki", weight, normed, preferred_element_type=jnp.float32)
        proj = jax.nn.sigmoid(mixed[:C]) * mixed[C:] * tile_mask[None]
        return proj.astype(jnp.bfloat16).reshape(wide, per_device, tile_cols, tile_rows)

    send = jnp.stack([edges(left_weight), edges(right_weight)], axis=1)
    recv = lax.all_to_all(send, "wide", split_axis=0, concat_axis=0, tiled=True)
    left, right = recv[:, 0], recv[:, 1]
    if narrow > 1:
        right = lax.all_gather(right, "narrow", axis=3, tiled=True)
    tri = jnp.einsum("sckj,scki->cji", right, left, preferred_element_type=jnp.float32)
    back = tri.astype(jnp.bfloat16).reshape(per_device, wide, tile_cols, tile_rows)
    back = jnp.transpose(back, (1, 0, 2, 3))
    tri = lax.all_to_all(back, "wide", split_axis=0, concat_axis=0, tiled=True)
    tri = tri.reshape(C, tile_cols, tile_rows).astype(jnp.float32)
    tri_normed = layer_norm(tri, 0).astype(jnp.bfloat16)
    gate = jax.nn.sigmoid(
        jnp.einsum("ikc,cd->ikd", normed, gate_weight, preferred_element_type=jnp.float32)
    )
    return gate * jnp.einsum(
        "cji,cd->ijd", tri_normed, out_weight, preferred_element_type=jnp.float32
    )


def on_device(pair_act, block_mask, *weights):
    rows, cols = pair_act.shape[:2]
    blocks = block_mask.shape[0]
    fits = rows == 2 * LANES and cols == SUB and C // lax.axis_size("wide") == 4 and blocks == 4
    if lax.axis_size("narrow") > 1 or not fits:
        return plain_on_device(pair_act, block_mask, *weights)
    return kernels_on_device(pair_act, block_mask, *weights)


def solution(mesh):
    return jax.shard_map(
        on_device,
        mesh=mesh,
        in_specs=(P("narrow", "wide", None), P(), P(), P(), P(), P()),
        out_specs=P("narrow", "wide", None),
        check_vma=False,
    )
```

```python
import functools

import jax
import jax.numpy as jnp
from jax import lax
from jax.experimental import pallas as pl
from jax.experimental.pallas import tpu as pltpu
from jax.sharding import PartitionSpec as P

C = 128
BLOCK = 64
LANES = 128
SUB = 8
PARTS = 2


def layer_norm(values, axis):
    centre = jnp.mean(values, axis=axis, keepdims=True)
    spread = jnp.mean(jnp.square(values - centre), axis=axis, keepdims=True)
    return (values - centre) * lax.rsqrt(spread + 1e-05)


def swap_halves(values):
    flat = values.reshape(-1, LANES)
    return pltpu.roll(flat, LANES // 2, 1).reshape(values.shape)


def pack(low, high):
    lane = lax.broadcasted_iota(jnp.int32, low.shape, low.ndim - 1)
    return jnp.where(lane < LANES // 2, low, swap_halves(high))


def window_start(windowed):
    if not windowed:
        return 0
    return jnp.where(lax.axis_index("wide") * SUB < 3 * BLOCK, 0, BLOCK)


def chunks_of(rows):
    return ((0, LANES), (LANES, rows - LANES))


def project_kernel(mask_hbm, x_hbm, wl_hbm, wr_hbm, *refs):
    whole_ref, window_ref, normed_ref, cut_ref, mask_ref, x_ref, w_ref, edge, sems = refs
    group_size = whole_ref.shape[0]
    tokens = x_hbm.shape[0] // SUB
    copies = [
        pltpu.make_async_copy(mask_hbm, mask_ref, sems.at[0]),
        pltpu.make_async_copy(wl_hbm, w_ref.at[0], sems.at[1]),
        pltpu.make_async_copy(wr_hbm, w_ref.at[1], sems.at[2]),
    ]
    for index in range(2):
        part = pl.ds(index * LANES * SUB, LANES * SUB)
        copies.append(pltpu.make_async_copy(x_hbm.at[part], x_ref.at[part], sems.at[3 + index]))
    for copy in copies:
        copy.start()
    copies[0].wait()
    cut = mask_ref[0, 3] == 0
    cut_ref[0] = cut.astype(jnp.int32)
    column_block = lax.axis_index("wide") * SUB // BLOCK
    kept = [mask_ref[block, column_block].astype(jnp.float32) for block in range(mask_hbm.shape[0])]
    copies[1].wait()
    copies[2].wait()
    weights = jnp.concatenate([w_ref[0].T, w_ref[1].T], axis=0)

    def project(windowed, send_ref):
        first = window_start(windowed)
        row_block = (first + lax.broadcasted_iota(jnp.int32, (1, 2 * LANES), 1)) // BLOCK
        mask = jnp.zeros((1, 2 * LANES), jnp.float32)
        for block, value in enumerate(kept):
            mask = jnp.where(row_block == block, value, mask)
        if windowed:
            copies[3].wait()
            copies[4].wait()
        chunks = chunks_of(3 * BLOCK if windowed else tokens)
        for index, (low, count) in enumerate(chunks):
            if not windowed:
                copies[3 + index].wait()
            group = 2 * LANES // count
            chunk_mask = jnp.concatenate([mask[:, low : low + count]] * group, axis=1)
            base = pl.multiple_of((first + low) * SUB, SUB)
            for start in range(0, SUB, group):
                x = [x_ref[pl.ds(base + start + k, count, stride=SUB), :] for k in range(group)]
                normed = layer_norm(jnp.concatenate(x, axis=0), 1).astype(jnp.bfloat16)
                for k in range(group):
                    normed_ref[start + k, low : low + count, :] = normed[k * count : (k + 1) * count]
                mixed = lax.dot_general(
                    weights, normed, (((1,), (1,)), ((), ())), preferred_element_type=jnp.float32
                )
                for side in range(2):
                    gate = mixed[2 * side * C : (2 * side + 1) * C]
                    value = mixed[(2 * side + 1) * C : (2 * side + 2) * C]
                    proj = jax.nn.sigmoid(gate) * value * chunk_mask
                    parts = [proj[:, at : at + LANES] for at in (0, LANES)]
                    if windowed:
                        pair = [p.reshape(group_size, SUB, LANES) for p in parts]
                        pair = jnp.concatenate(pair, axis=1).astype(jnp.bfloat16)
                        place = side * send_ref.shape[1] // 2 + index * SUB * SUB + start // group * 2 * SUB
                        send_ref[:, place : place + 2 * SUB, :] = pair
                    else:
                        for k in range(2):
                            edge[side, index, pl.ds(start + k, C, stride=SUB), :] = parts[k]
        if windowed:
            return
        part = C // group_size * SUB
        for side in range(2):
            for index in range(2):
                values = edge[side, index, : C * SUB, :].reshape(group_size, part, LANES)
                low = (side * 2 + index) * part
                send_ref[:, low : low + part, :] = values.astype(jnp.bfloat16)

    pl.when(cut)(lambda: project(True, window_ref))
    pl.when(jnp.logical_not(cut))(lambda: project(False, whole_ref))


def whole_triangle_kernel(windowed, recv_ref, send_ref):
    group_size = recv_ref.shape[0]
    wide = send_ref.shape[0]
    per_device = C // group_size
    part = per_device * SUB
    columns = group_size * SUB
    half = per_device // 2

    def load(side, channel):
        parts = []
        for index in range(2):
            start = side * send_ref.shape[1] + index * part
            swap = windowed and index == 1 and channel >= half
            at = start + (channel - half if swap else channel) * SUB
            pair = recv_ref[:, at : at + 2 * SUB, :].astype(jnp.float32)
            if swap:
                pair = swap_halves(pair)
            parts.append([
                pair[:, low : low + SUB].reshape(columns, LANES).astype(jnp.bfloat16)
                for low in (0, SUB)
            ])
        return [jnp.concatenate([p[n] for p in parts], axis=1) for n in range(2)]

    def product(right, left):
        return lax.dot_general(
            right, left, (((0,), (0,)), ((), ())), preferred_element_type=jnp.float32
        )

    cut = 3 * BLOCK
    columns_first = lax.axis_index("wide") // group_size * columns
    column = columns_first + lax.broadcasted_iota(jnp.int32, (columns, 1), 0)
    sums = []
    for channel in range(0, per_device, 2):
        for left, right in zip(load(0, channel), load(1, channel)):
            if windowed:
                above = product(right, jnp.where(column < cut, left, 0))[:cut]
                below = product(right[:, LANES:], jnp.where(column < cut, 0, left))
                sums.append(jnp.concatenate([above, below[: wide * SUB - cut]], axis=0))
            else:
                sums.append(product(right, left))
    first = [s[:, :LANES] for s in sums]
    second = [s[:, LANES:] for s in sums]
    if windowed:
        second = [pack(second[c], second[c + half]) for c in range(half)]
    start = 0
    for channels in (first, second):
        for channel in range(0, len(channels), 2):
            pair = [channels[channel + n].reshape(wide, SUB, LANES) for n in range(2)]
            pair = jnp.concatenate(pair, axis=1).astype(jnp.bfloat16)
            send_ref[:, start : start + 2 * SUB, :] = pair
            start += 2 * SUB


def window_triangle_kernel(windowed, recv_ref, send_ref, edge):
    group_size = recv_ref.shape[0]
    wide = send_ref.shape[0]
    per_device = C // group_size
    part = per_device * SUB
    columns = group_size * SUB
    half = per_device // 2
    side_rows = send_ref.shape[1]
    for side in range(2):
        for index in range(2):
            height = min(part, side_rows - index * part)
            start = side * side_rows + index * part
            values = recv_ref[:, start : start + height, :].astype(jnp.float32)
            edge[side, index, : group_size * height, :] = values.reshape(group_size * height, LANES)

    def load(side, channel):
        parts = []
        for parity in range(2):
            rows = pl.ds(parity * SUB + channel, columns // 2, stride=2 * SUB)
            first = edge[side, 0, rows, :]
            if windowed:
                second = edge[side, 1, pl.ds(channel, columns // 2, stride=SUB), :]
                if parity:
                    second = swap_halves(second)
            else:
                second = edge[side, 1, rows, :]
            parts.append(jnp.concatenate([first, second], axis=1))
        return jnp.concatenate(parts, axis=0).astype(jnp.bfloat16)

    def product(right, left):
        return lax.dot_general(
            right, left, (((0,), (0,)), ((), ())), preferred_element_type=jnp.float32
        )

    cut = 3 * BLOCK
    columns_first = lax.axis_index("wide") // group_size * columns
    place = lax.broadcasted_iota(jnp.int32, (columns, 1), 0) % (columns // 2)
    column = columns_first + 2 * place
    sums = []
    for channel in range(per_device):
        left, right = load(0, channel), load(1, channel)
        if windowed:
            above = product(right, jnp.where(column < cut, left, 0))[:cut]
            below = product(right[:, LANES:], jnp.where(column < cut, 0, left))
            sums.append(jnp.concatenate([above, below[: wide * SUB - cut]], axis=0))
        else:
            sums.append(product(right, left))
    first = [s[:, :LANES] for s in sums]
    second = [s[:, LANES:] for s in sums]
    if windowed:
        second = [pack(second[c], second[c + half]) for c in range(half)]
    start = 0
    for channels in (first, second):
        for channel in range(0, len(channels), 2):
            pair = [channels[channel + n].reshape(wide, SUB, LANES) for n in range(2)]
            pair = jnp.concatenate(pair, axis=1).astype(jnp.bfloat16)
            send_ref[:, start : start + 2 * SUB, :] = pair
            start += 2 * SUB


def update_kernel(windowed, recv_ref, normed_ref, wg_ref, wo_ref, out_hbm, tri, out_ref, sems):
    group_size = recv_ref.shape[0] // PARTS
    part = C // group_size * SUB
    rows = 3 * BLOCK if windowed else normed_ref.shape[1]
    chunks = chunks_of(rows)
    first = window_start(windowed)
    copies = []
    if windowed:
        rest = out_hbm.shape[0] - rows * SUB
        to = pl.multiple_of(jnp.where(first == 0, rows, 0) * SUB, SUB)
        out_ref[pl.ds(rows * SUB, rest), :] = jnp.zeros((rest, C), jnp.float32)
        copies.append(
            pltpu.make_async_copy(
                out_ref.at[pl.ds(rows * SUB, rest)], out_hbm.at[pl.ds(to, rest)], sems.at[2]
            )
        )
        copies[0].start()
    for index, (low, count) in enumerate(chunks):
        height = part * count // LANES
        sums = [
            recv_ref[n * group_size : (n + 1) * group_size, index * part : index * part + height, :]
            for n in range(PARTS)
        ]
        sums = sum(values.astype(jnp.float32) for values in sums)
        if count < LANES:
            sums = jnp.concatenate([sums, swap_halves(sums)], axis=1)
        tri[index, : C * SUB, :] = layer_norm(sums.reshape(C, SUB, LANES), 0).reshape(C * SUB, LANES)
        for j in range(SUB):
            tri_normed = tri[index, pl.ds(j, C, stride=SUB), :].astype(jnp.bfloat16)
            mixed = lax.dot_general(
                tri_normed, wo_ref[...], (((0,), (0,)), ((), ())), preferred_element_type=jnp.float32
            )
            normed = normed_ref[j, low : low + count, :]
            gate = jax.nn.sigmoid(
                jnp.dot(normed, wg_ref[...], preferred_element_type=jnp.float32)
            )
            out_ref[pl.ds(low * SUB + j, count, stride=SUB), :] = gate * mixed[:count]
        to = pl.multiple_of((first + low) * SUB, SUB)
        copies.append(
            pltpu.make_async_copy(
                out_ref.at[pl.ds(low * SUB, count * SUB)],
                out_hbm.at[pl.ds(to, count * SUB)],
                sems.at[index],
            )
        )
        copies[-1].start()
    for copy in copies:
        copy.wait()


HBM = pl.BlockSpec(memory_space=pltpu.HBM)
VMEM = pl.BlockSpec(memory_space=pltpu.VMEM)
PARAMS = pltpu.CompilerParams(vmem_limit_bytes=48 * 1024 * 1024)


def in_hbm(array):
    return pltpu.with_memory_space_constraint(array, pltpu.HBM)


def exchange(array):
    wide, size = lax.axis_size("wide"), array.shape[0]
    groups = [list(range(first, first + size)) for first in range(0, wide, size)]
    return lax.all_to_all(
        array, "wide", split_axis=0, concat_axis=0, axis_index_groups=groups, tiled=True
    )


def after_projection(windowed, whole, window, normed, gate_weight, out_weight):
    send = window if windowed else whole
    group_size, both, _ = send.shape
    wide = group_size * PARTS
    tokens = normed.shape[1]
    back = pl.pallas_call(
        functools.partial(window_triangle_kernel if windowed else whole_triangle_kernel, windowed),
        out_shape=jax.ShapeDtypeStruct((wide, both // 2, LANES), jnp.bfloat16),
        in_specs=[VMEM],
        out_specs=VMEM,
        scratch_shapes=[pltpu.VMEM((2, 2, C * SUB + 2 * SUB, LANES), jnp.float32)] * windowed,
        compiler_params=PARAMS,
        name="triangle",
    )(exchange(send))
    return pl.pallas_call(
        functools.partial(update_kernel, windowed),
        out_shape=pltpu.HBM((tokens * SUB, C), jnp.float32),
        in_specs=[VMEM] * 4,
        out_specs=HBM,
        scratch_shapes=[
            pltpu.VMEM((2, C * SUB + SUB, LANES), jnp.float32),
            pltpu.VMEM((tokens * SUB + SUB, C), jnp.float32),
            pltpu.SemaphoreType.DMA((3,)),
        ],
        compiler_params=PARAMS,
        name="update",
    )(exchange(back), normed, gate_weight, out_weight)


def kernels_on_device(pair_act, block_mask, left_weight, right_weight, gate_weight, out_weight):
    tokens = pair_act.shape[0]
    wide = lax.axis_size("wide")
    group_size = wide // PARTS
    both = lambda rows: 2 * rows * (C // group_size) * SUB // LANES
    whole, window, normed, cut = pl.pallas_call(
        project_kernel,
        out_shape=(
            jax.ShapeDtypeStruct((group_size, both(tokens), LANES), jnp.bfloat16),
            jax.ShapeDtypeStruct((group_size, both(3 * BLOCK), LANES), jnp.bfloat16),
            jax.ShapeDtypeStruct((SUB, tokens, C), jnp.bfloat16),
            pltpu.SMEM((1,), jnp.int32),
        ),
        in_specs=[HBM] * 4,
        out_specs=(VMEM, VMEM, VMEM, pl.BlockSpec(memory_space=pltpu.SMEM)),
        scratch_shapes=[
            pltpu.SMEM(block_mask.shape, jnp.int32),
            pltpu.VMEM((tokens * SUB + SUB, C), jnp.float32),
            pltpu.VMEM((2, C, 2 * C), jnp.bfloat16),
            pltpu.VMEM((2, 2, C * SUB + SUB, LANES), jnp.float32),
            pltpu.SemaphoreType.DMA((5,)),
        ],
        compiler_params=PARAMS,
        name="project",
    )(
        in_hbm(block_mask),
        in_hbm(pair_act.reshape(tokens * SUB, C)),
        in_hbm(left_weight),
        in_hbm(right_weight),
    )
    update = lax.switch(
        cut[0],
        [functools.partial(after_projection, windowed) for windowed in (False, True)],
        whole,
        window,
        normed,
        gate_weight,
        out_weight,
    )
    return update.reshape(tokens, SUB, C)


def plain_on_device(pair_act, block_mask, left_weight, right_weight, gate_weight, out_weight):
    tile_rows = pair_act.shape[0]
    tile_cols = pair_act.shape[1]
    wide = lax.axis_size("wide")
    narrow = lax.axis_size("narrow")
    per_device = C // wide
    row_ids = lax.axis_index("narrow") * tile_rows + jnp.arange(tile_rows, dtype=jnp.int32)
    col_ids = lax.axis_index("wide") * tile_cols + jnp.arange(tile_cols, dtype=jnp.int32)
    block_ids = jnp.arange(block_mask.shape[0], dtype=jnp.int32)
    row_hot = (row_ids[:, None] // BLOCK == block_ids[None, :]).astype(jnp.float32)
    col_hot = (col_ids[:, None] // BLOCK == block_ids[None, :]).astype(jnp.float32)
    tile_mask = jnp.dot(jnp.dot(row_hot, block_mask.astype(jnp.float32)), col_hot.T).T
    normed = layer_norm(pair_act, -1).astype(jnp.bfloat16)

    def edges(weight):
        mixed = jnp.einsum("cd,ikc->dki", weight, normed, preferred_element_type=jnp.float32)
        proj = jax.nn.sigmoid(mixed[:C]) * mixed[C:] * tile_mask[None]
        return proj.astype(jnp.bfloat16).reshape(wide, per_device, tile_cols, tile_rows)

    send = jnp.stack([edges(left_weight), edges(right_weight)], axis=1)
    recv = lax.all_to_all(send, "wide", split_axis=0, concat_axis=0, tiled=True)
    left, right = recv[:, 0], recv[:, 1]
    if narrow > 1:
        right = lax.all_gather(right, "narrow", axis=3, tiled=True)
    tri = jnp.einsum("sckj,scki->cji", right, left, preferred_element_type=jnp.float32)
    back = tri.astype(jnp.bfloat16).reshape(per_device, wide, tile_cols, tile_rows)
    back = jnp.transpose(back, (1, 0, 2, 3))
    tri = lax.all_to_all(back, "wide", split_axis=0, concat_axis=0, tiled=True)
    tri = tri.reshape(C, tile_cols, tile_rows).astype(jnp.float32)
    tri_normed = layer_norm(tri, 0).astype(jnp.bfloat16)
    gate = jax.nn.sigmoid(
        jnp.einsum("ikc,cd->ikd", normed, gate_weight, preferred_element_type=jnp.float32)
    )
    return gate * jnp.einsum(
        "cji,cd->ijd", tri_normed, out_weight, preferred_element_type=jnp.float32
    )


def on_device(pair_act, block_mask, *weights):
    rows, cols = pair_act.shape[:2]
    blocks = block_mask.shape[0]
    fits = rows == 2 * LANES and cols == SUB and C // lax.axis_size("wide") == 4 and blocks == 4
    if lax.axis_size("narrow") > 1 or not fits:
        return plain_on_device(pair_act, block_mask, *weights)
    return kernels_on_device(pair_act, block_mask, *weights)


def solution(mesh):
    return jax.shard_map(
        on_device,
        mesh=mesh,
        in_specs=(P("narrow", "wide", None), P(), P(), P(), P(), P()),
        out_specs=P("narrow", "wide", None),
        check_vma=False,
    )
```

```python
import functools

import jax
import jax.numpy as jnp
from jax import lax
from jax.experimental import pallas as pl
from jax.experimental.pallas import tpu as pltpu
from jax.sharding import PartitionSpec as P

C = 128
BLOCK = 64
LANES = 128
SUB = 8
PARTS = 2


def layer_norm(values, axis):
    centre = jnp.mean(values, axis=axis, keepdims=True)
    spread = jnp.mean(jnp.square(values - centre), axis=axis, keepdims=True)
    return (values - centre) * lax.rsqrt(spread + 1e-05)


def swap_halves(values):
    flat = values.reshape(-1, LANES)
    return pltpu.roll(flat, LANES // 2, 1).reshape(values.shape)


def pack(low, high):
    lane = lax.broadcasted_iota(jnp.int32, low.shape, low.ndim - 1)
    return jnp.where(lane < LANES // 2, low, swap_halves(high))


def window_start(windowed):
    if not windowed:
        return 0
    return jnp.where(lax.axis_index("wide") * SUB < 3 * BLOCK, 0, BLOCK)


def chunks_of(rows):
    return ((0, LANES), (LANES, rows - LANES))


def sigmoid(values):
    return 0.5 * jnp.tanh(0.5 * values) + 0.5


def project_kernel(mask_hbm, x_hbm, wl_hbm, wr_hbm, *refs):
    whole_ref, window_ref, normed_ref, cut_ref, mask_ref, x_ref, w_ref, edge, sems = refs
    group_size = whole_ref.shape[0]
    tokens = x_hbm.shape[0] // SUB
    copies = [
        pltpu.make_async_copy(mask_hbm, mask_ref, sems.at[0]),
        pltpu.make_async_copy(wl_hbm, w_ref.at[0], sems.at[1]),
        pltpu.make_async_copy(wr_hbm, w_ref.at[1], sems.at[2]),
    ]
    for index in range(2):
        part = pl.ds(index * LANES * SUB, LANES * SUB)
        copies.append(pltpu.make_async_copy(x_hbm.at[part], x_ref.at[part], sems.at[3 + index]))
    for copy in copies:
        copy.start()
    copies[0].wait()
    cut = mask_ref[0, 3] == 0
    cut_ref[0] = cut.astype(jnp.int32)
    column_block = lax.axis_index("wide") * SUB // BLOCK
    kept = [mask_ref[block, column_block].astype(jnp.float32) for block in range(mask_hbm.shape[0])]
    copies[1].wait()
    copies[2].wait()
    weights = jnp.concatenate([w_ref[0].T, w_ref[1].T], axis=0)

    def project(windowed, send_ref):
        first = window_start(windowed)
        row_block = (first + lax.broadcasted_iota(jnp.int32, (1, 2 * LANES), 1)) // BLOCK
        mask = jnp.zeros((1, 2 * LANES), jnp.float32)
        for block, value in enumerate(kept):
            mask = jnp.where(row_block == block, value, mask)
        if windowed:
            copies[3].wait()
            copies[4].wait()
        chunks = chunks_of(3 * BLOCK if windowed else tokens)
        for index, (low, count) in enumerate(chunks):
            if not windowed:
                copies[3 + index].wait()
            group = 2 * LANES // count
            chunk_mask = jnp.concatenate([mask[:, low : low + count]] * group, axis=1)
            base = pl.multiple_of((first + low) * SUB, SUB)
            for start in range(0, SUB, group):
                x = [x_ref[pl.ds(base + start + k, count, stride=SUB), :] for k in range(group)]
                normed = layer_norm(jnp.concatenate(x, axis=0), 1).astype(jnp.bfloat16)
                for k in range(group):
                    normed_ref[start + k, low : low + count, :] = normed[k * count : (k + 1) * count]
                mixed = lax.dot_general(
                    weights, normed, (((1,), (1,)), ((), ())), preferred_element_type=jnp.float32
                )
                for side in range(2):
                    gate = mixed[2 * side * C : (2 * side + 1) * C]
                    value = mixed[(2 * side + 1) * C : (2 * side + 2) * C]
                    proj = sigmoid(gate) * value * chunk_mask
                    parts = [proj[:, at : at + LANES] for at in (0, LANES)]
                    if windowed:
                        pair = [p.reshape(group_size, SUB, LANES) for p in parts]
                        pair = jnp.concatenate(pair, axis=1).astype(jnp.bfloat16)
                        place = side * send_ref.shape[1] // 2 + index * SUB * SUB + start // group * 2 * SUB
                        send_ref[:, place : place + 2 * SUB, :] = pair
                    else:
                        for k in range(2):
                            edge[side, index, pl.ds(start + k, C, stride=SUB), :] = parts[k]
        if windowed:
            return
        part = C // group_size * SUB
        for side in range(2):
            for index in range(2):
                values = edge[side, index, : C * SUB, :].reshape(group_size, part, LANES)
                low = (side * 2 + index) * part
                send_ref[:, low : low + part, :] = values.astype(jnp.bfloat16)

    pl.when(cut)(lambda: project(True, window_ref))
    pl.when(jnp.logical_not(cut))(lambda: project(False, whole_ref))


def whole_triangle_kernel(windowed, recv_ref, send_ref):
    group_size = recv_ref.shape[0]
    wide = send_ref.shape[0]
    per_device = C // group_size
    part = per_device * SUB
    columns = group_size * SUB
    half = per_device // 2

    def load(side, channel):
        parts = []
        for index in range(2):
            start = side * send_ref.shape[1] + index * part
            swap = windowed and index == 1 and channel >= half
            at = start + (channel - half if swap else channel) * SUB
            pair = recv_ref[:, at : at + 2 * SUB, :].astype(jnp.float32)
            if swap:
                pair = swap_halves(pair)
            parts.append([
                pair[:, low : low + SUB].reshape(columns, LANES).astype(jnp.bfloat16)
                for low in (0, SUB)
            ])
        return [jnp.concatenate([p[n] for p in parts], axis=1) for n in range(2)]

    def product(right, left):
        return lax.dot_general(
            right, left, (((0,), (0,)), ((), ())), preferred_element_type=jnp.float32
        )

    cut = 3 * BLOCK
    columns_first = lax.axis_index("wide") // group_size * columns
    column = columns_first + lax.broadcasted_iota(jnp.int32, (columns, 1), 0)
    sums = []
    for channel in range(0, per_device, 2):
        for left, right in zip(load(0, channel), load(1, channel)):
            if windowed:
                above = product(right, jnp.where(column < cut, left, 0))[:cut]
                below = product(right[:, LANES:], jnp.where(column < cut, 0, left))
                sums.append(jnp.concatenate([above, below[: wide * SUB - cut]], axis=0))
            else:
                sums.append(product(right, left))
    first = [s[:, :LANES] for s in sums]
    second = [s[:, LANES:] for s in sums]
    if windowed:
        second = [pack(second[c], second[c + half]) for c in range(half)]
    start = 0
    for channels in (first, second):
        for channel in range(0, len(channels), 2):
            pair = [channels[channel + n].reshape(wide, SUB, LANES) for n in range(2)]
            pair = jnp.concatenate(pair, axis=1).astype(jnp.bfloat16)
            send_ref[:, start : start + 2 * SUB, :] = pair
            start += 2 * SUB


def window_triangle_kernel(windowed, recv_ref, send_ref, edge):
    group_size = recv_ref.shape[0]
    wide = send_ref.shape[0]
    per_device = C // group_size
    part = per_device * SUB
    columns = group_size * SUB
    half = per_device // 2
    side_rows = send_ref.shape[1]
    for side in range(2):
        for index in range(2):
            height = min(part, side_rows - index * part)
            start = side * side_rows + index * part
            values = recv_ref[:, start : start + height, :].astype(jnp.float32)
            edge[side, index, : group_size * height, :] = values.reshape(group_size * height, LANES)

    def load(side, channel):
        parts = []
        for parity in range(2):
            rows = pl.ds(parity * SUB + channel, columns // 2, stride=2 * SUB)
            first = edge[side, 0, rows, :]
            if windowed:
                second = edge[side, 1, pl.ds(channel, columns // 2, stride=SUB), :]
                if parity:
                    second = swap_halves(second)
            else:
                second = edge[side, 1, rows, :]
            parts.append(jnp.concatenate([first, second], axis=1))
        return jnp.concatenate(parts, axis=0).astype(jnp.bfloat16)

    def product(right, left):
        return lax.dot_general(
            right, left, (((0,), (0,)), ((), ())), preferred_element_type=jnp.float32
        )

    cut = 3 * BLOCK
    columns_first = lax.axis_index("wide") // group_size * columns
    place = lax.broadcasted_iota(jnp.int32, (columns, 1), 0) % (columns // 2)
    column = columns_first + 2 * place
    sums = []
    for channel in range(per_device):
        left, right = load(0, channel), load(1, channel)
        if windowed:
            above = product(right, jnp.where(column < cut, left, 0))[:cut]
            below = product(right[:, LANES:], jnp.where(column < cut, 0, left))
            sums.append(jnp.concatenate([above, below[: wide * SUB - cut]], axis=0))
        else:
            sums.append(product(right, left))
    first = [s[:, :LANES] for s in sums]
    second = [s[:, LANES:] for s in sums]
    if windowed:
        second = [pack(second[c], second[c + half]) for c in range(half)]
    start = 0
    for channels in (first, second):
        for channel in range(0, len(channels), 2):
            pair = [channels[channel + n].reshape(wide, SUB, LANES) for n in range(2)]
            pair = jnp.concatenate(pair, axis=1).astype(jnp.bfloat16)
            send_ref[:, start : start + 2 * SUB, :] = pair
            start += 2 * SUB


def update_kernel(windowed, recv_ref, normed_ref, wg_ref, wo_ref, out_hbm, tri, out_ref, sems):
    group_size = recv_ref.shape[0] // PARTS
    part = C // group_size * SUB
    rows = 3 * BLOCK if windowed else normed_ref.shape[1]
    chunks = chunks_of(rows)
    first = window_start(windowed)
    copies = []
    if windowed:
        rest = out_hbm.shape[0] - rows * SUB
        to = pl.multiple_of(jnp.where(first == 0, rows, 0) * SUB, SUB)
        out_ref[pl.ds(rows * SUB, rest), :] = jnp.zeros((rest, C), jnp.float32)
        copies.append(
            pltpu.make_async_copy(
                out_ref.at[pl.ds(rows * SUB, rest)], out_hbm.at[pl.ds(to, rest)], sems.at[2]
            )
        )
        copies[0].start()
    for index, (low, count) in enumerate(chunks):
        height = part * count // LANES
        sums = [
            recv_ref[n * group_size : (n + 1) * group_size, index * part : index * part + height, :]
            for n in range(PARTS)
        ]
        sums = sum(values.astype(jnp.float32) for values in sums)
        if count < LANES:
            sums = jnp.concatenate([sums, swap_halves(sums)], axis=1)
        tri[index, : C * SUB, :] = layer_norm(sums.reshape(C, SUB, LANES), 0).reshape(C * SUB, LANES)
        for j in range(SUB):
            tri_normed = tri[index, pl.ds(j, C, stride=SUB), :].astype(jnp.bfloat16)
            mixed = lax.dot_general(
                tri_normed, wo_ref[...], (((0,), (0,)), ((), ())), preferred_element_type=jnp.float32
            )
            normed = normed_ref[j, low : low + count, :]
            gate = sigmoid(
                jnp.dot(normed, wg_ref[...], preferred_element_type=jnp.float32)
            )
            out_ref[pl.ds(low * SUB + j, count, stride=SUB), :] = gate * mixed[:count]
        to = pl.multiple_of((first + low) * SUB, SUB)
        copies.append(
            pltpu.make_async_copy(
                out_ref.at[pl.ds(low * SUB, count * SUB)],
                out_hbm.at[pl.ds(to, count * SUB)],
                sems.at[index],
            )
        )
        copies[-1].start()
    for copy in copies:
        copy.wait()


HBM = pl.BlockSpec(memory_space=pltpu.HBM)
VMEM = pl.BlockSpec(memory_space=pltpu.VMEM)
PARAMS = pltpu.CompilerParams(vmem_limit_bytes=48 * 1024 * 1024)


def in_hbm(array):
    return pltpu.with_memory_space_constraint(array, pltpu.HBM)


def exchange(array):
    wide, size = lax.axis_size("wide"), array.shape[0]
    groups = [list(range(first, first + size)) for first in range(0, wide, size)]
    return lax.all_to_all(
        array, "wide", split_axis=0, concat_axis=0, axis_index_groups=groups, tiled=True
    )


def after_projection(windowed, whole, window, normed, gate_weight, out_weight):
    send = window if windowed else whole
    group_size, both, _ = send.shape
    wide = group_size * PARTS
    tokens = normed.shape[1]
    back = pl.pallas_call(
        functools.partial(window_triangle_kernel if windowed else whole_triangle_kernel, windowed),
        out_shape=jax.ShapeDtypeStruct((wide, both // 2, LANES), jnp.bfloat16),
        in_specs=[VMEM],
        out_specs=VMEM,
        scratch_shapes=[pltpu.VMEM((2, 2, C * SUB + 2 * SUB, LANES), jnp.float32)] * windowed,
        compiler_params=PARAMS,
        name="triangle",
    )(exchange(send))
    return pl.pallas_call(
        functools.partial(update_kernel, windowed),
        out_shape=pltpu.HBM((tokens * SUB, C), jnp.float32),
        in_specs=[VMEM] * 4,
        out_specs=HBM,
        scratch_shapes=[
            pltpu.VMEM((2, C * SUB + SUB, LANES), jnp.float32),
            pltpu.VMEM((tokens * SUB + SUB, C), jnp.float32),
            pltpu.SemaphoreType.DMA((3,)),
        ],
        compiler_params=PARAMS,
        name="update",
    )(exchange(back), normed, gate_weight, out_weight)


def kernels_on_device(pair_act, block_mask, left_weight, right_weight, gate_weight, out_weight):
    tokens = pair_act.shape[0]
    wide = lax.axis_size("wide")
    group_size = wide // PARTS
    both = lambda rows: 2 * rows * (C // group_size) * SUB // LANES
    whole, window, normed, cut = pl.pallas_call(
        project_kernel,
        out_shape=(
            jax.ShapeDtypeStruct((group_size, both(tokens), LANES), jnp.bfloat16),
            jax.ShapeDtypeStruct((group_size, both(3 * BLOCK), LANES), jnp.bfloat16),
            jax.ShapeDtypeStruct((SUB, tokens, C), jnp.bfloat16),
            pltpu.SMEM((1,), jnp.int32),
        ),
        in_specs=[HBM] * 4,
        out_specs=(VMEM, VMEM, VMEM, pl.BlockSpec(memory_space=pltpu.SMEM)),
        scratch_shapes=[
            pltpu.SMEM(block_mask.shape, jnp.int32),
            pltpu.VMEM((tokens * SUB + SUB, C), jnp.float32),
            pltpu.VMEM((2, C, 2 * C), jnp.bfloat16),
            pltpu.VMEM((2, 2, C * SUB + SUB, LANES), jnp.float32),
            pltpu.SemaphoreType.DMA((5,)),
        ],
        compiler_params=PARAMS,
        name="project",
    )(
        in_hbm(block_mask),
        in_hbm(pair_act.reshape(tokens * SUB, C)),
        in_hbm(left_weight),
        in_hbm(right_weight),
    )
    update = lax.switch(
        cut[0],
        [functools.partial(after_projection, windowed) for windowed in (False, True)],
        whole,
        window,
        normed,
        gate_weight,
        out_weight,
    )
    return update.reshape(tokens, SUB, C)


def plain_on_device(pair_act, block_mask, left_weight, right_weight, gate_weight, out_weight):
    tile_rows = pair_act.shape[0]
    tile_cols = pair_act.shape[1]
    wide = lax.axis_size("wide")
    narrow = lax.axis_size("narrow")
    per_device = C // wide
    row_ids = lax.axis_index("narrow") * tile_rows + jnp.arange(tile_rows, dtype=jnp.int32)
    col_ids = lax.axis_index("wide") * tile_cols + jnp.arange(tile_cols, dtype=jnp.int32)
    block_ids = jnp.arange(block_mask.shape[0], dtype=jnp.int32)
    row_hot = (row_ids[:, None] // BLOCK == block_ids[None, :]).astype(jnp.float32)
    col_hot = (col_ids[:, None] // BLOCK == block_ids[None, :]).astype(jnp.float32)
    tile_mask = jnp.dot(jnp.dot(row_hot, block_mask.astype(jnp.float32)), col_hot.T).T
    normed = layer_norm(pair_act, -1).astype(jnp.bfloat16)

    def edges(weight):
        mixed = jnp.einsum("cd,ikc->dki", weight, normed, preferred_element_type=jnp.float32)
        proj = jax.nn.sigmoid(mixed[:C]) * mixed[C:] * tile_mask[None]
        return proj.astype(jnp.bfloat16).reshape(wide, per_device, tile_cols, tile_rows)

    send = jnp.stack([edges(left_weight), edges(right_weight)], axis=1)
    recv = lax.all_to_all(send, "wide", split_axis=0, concat_axis=0, tiled=True)
    left, right = recv[:, 0], recv[:, 1]
    if narrow > 1:
        right = lax.all_gather(right, "narrow", axis=3, tiled=True)
    tri = jnp.einsum("sckj,scki->cji", right, left, preferred_element_type=jnp.float32)
    back = tri.astype(jnp.bfloat16).reshape(per_device, wide, tile_cols, tile_rows)
    back = jnp.transpose(back, (1, 0, 2, 3))
    tri = lax.all_to_all(back, "wide", split_axis=0, concat_axis=0, tiled=True)
    tri = tri.reshape(C, tile_cols, tile_rows).astype(jnp.float32)
    tri_normed = layer_norm(tri, 0).astype(jnp.bfloat16)
    gate = jax.nn.sigmoid(
        jnp.einsum("ikc,cd->ikd", normed, gate_weight, preferred_element_type=jnp.float32)
    )
    return gate * jnp.einsum(
        "cji,cd->ijd", tri_normed, out_weight, preferred_element_type=jnp.float32
    )


def on_device(pair_act, block_mask, *weights):
    rows, cols = pair_act.shape[:2]
    blocks = block_mask.shape[0]
    fits = rows == 2 * LANES and cols == SUB and C // lax.axis_size("wide") == 4 and blocks == 4
    if lax.axis_size("narrow") > 1 or not fits:
        return plain_on_device(pair_act, block_mask, *weights)
    return kernels_on_device(pair_act, block_mask, *weights)


def solution(mesh):
    return jax.shard_map(
        on_device,
        mesh=mesh,
        in_specs=(P("narrow", "wide", None), P(), P(), P(), P(), P()),
        out_specs=P("narrow", "wide", None),
        check_vma=False,
    )
```

```python
import functools

import jax
import jax.numpy as jnp
from jax import lax
from jax.experimental import pallas as pl
from jax.experimental.pallas import tpu as pltpu
from jax.sharding import PartitionSpec as P

C = 128
BLOCK = 64
LANES = 128
SUB = 8
PARTS = 2


def layer_norm(values, axis):
    centre = jnp.mean(values, axis=axis, keepdims=True)
    spread = jnp.mean(jnp.square(values - centre), axis=axis, keepdims=True)
    return (values - centre) * lax.rsqrt(spread + 1e-05)


def swap_halves(values):
    flat = values.reshape(-1, LANES)
    return pltpu.roll(flat, LANES // 2, 1).reshape(values.shape)


def pack(low, high):
    lane = lax.broadcasted_iota(jnp.int32, low.shape, low.ndim - 1)
    return jnp.where(lane < LANES // 2, low, swap_halves(high))


def window_start(windowed):
    if not windowed:
        return 0
    return jnp.where(lax.axis_index("wide") * SUB < 3 * BLOCK, 0, BLOCK)


def chunks_of(rows):
    return ((0, LANES), (LANES, rows - LANES))


def project_kernel(mask_hbm, x_hbm, wl_hbm, wr_hbm, *refs):
    whole_ref, window_ref, normed_ref, cut_ref, mask_ref, x_ref, w_ref, edge, sems = refs
    group_size = whole_ref.shape[0]
    tokens = x_hbm.shape[0] // SUB
    copies = [
        pltpu.make_async_copy(mask_hbm, mask_ref, sems.at[0]),
        pltpu.make_async_copy(wl_hbm, w_ref.at[0], sems.at[1]),
        pltpu.make_async_copy(wr_hbm, w_ref.at[1], sems.at[2]),
    ]
    for index in range(2):
        part = pl.ds(index * LANES * SUB, LANES * SUB)
        copies.append(pltpu.make_async_copy(x_hbm.at[part], x_ref.at[part], sems.at[3 + index]))
    for copy in reversed(copies):
        copy.start()
    copies[0].wait()
    cut = mask_ref[0, 3] == 0
    cut_ref[0] = cut.astype(jnp.int32)
    column_block = lax.axis_index("wide") * SUB // BLOCK
    kept = [mask_ref[block, column_block].astype(jnp.float32) for block in range(mask_hbm.shape[0])]
    copies[1].wait()
    copies[2].wait()
    weights = jnp.concatenate([w_ref[0].T, w_ref[1].T], axis=0)

    def project(windowed, send_ref):
        first = window_start(windowed)
        row_block = (first + lax.broadcasted_iota(jnp.int32, (1, 2 * LANES), 1)) // BLOCK
        mask = jnp.zeros((1, 2 * LANES), jnp.float32)
        for block, value in enumerate(kept):
            mask = jnp.where(row_block == block, value, mask)
        if windowed:
            copies[3].wait()
            copies[4].wait()
        chunks = chunks_of(3 * BLOCK if windowed else tokens)
        for index, (low, count) in enumerate(chunks):
            if not windowed:
                copies[3 + index].wait()
            group = 2 * LANES // count
            chunk_mask = jnp.concatenate([mask[:, low : low + count]] * group, axis=1)
            base = pl.multiple_of((first + low) * SUB, SUB)
            for start in range(0, SUB, group):
                x = [x_ref[pl.ds(base + start + k, count, stride=SUB), :] for k in range(group)]
                normed = layer_norm(jnp.concatenate(x, axis=0), 1).astype(jnp.bfloat16)
                for k in range(group):
                    normed_ref[start + k, low : low + count, :] = normed[k * count : (k + 1) * count]
                mixed = lax.dot_general(
                    weights, normed, (((1,), (1,)), ((), ())), preferred_element_type=jnp.float32
                )
                for side in range(2):
                    gate = mixed[2 * side * C : (2 * side + 1) * C]
                    value = mixed[(2 * side + 1) * C : (2 * side + 2) * C]
                    proj = jax.nn.sigmoid(gate) * value * chunk_mask
                    parts = [proj[:, at : at + LANES] for at in (0, LANES)]
                    if windowed:
                        pair = [p.reshape(group_size, SUB, LANES) for p in parts]
                        pair = jnp.concatenate(pair, axis=1).astype(jnp.bfloat16)
                        place = side * send_ref.shape[1] // 2 + index * SUB * SUB + start // group * 2 * SUB
                        send_ref[:, place : place + 2 * SUB, :] = pair
                    else:
                        for k in range(2):
                            edge[side, index, pl.ds(start + k, C, stride=SUB), :] = parts[k]
        if windowed:
            return
        part = C // group_size * SUB
        for side in range(2):
            for index in range(2):
                values = edge[side, index, : C * SUB, :].reshape(group_size, part, LANES)
                low = (side * 2 + index) * part
                send_ref[:, low : low + part, :] = values.astype(jnp.bfloat16)

    pl.when(cut)(lambda: project(True, window_ref))
    pl.when(jnp.logical_not(cut))(lambda: project(False, whole_ref))


def whole_triangle_kernel(windowed, recv_ref, send_ref):
    group_size = recv_ref.shape[0]
    wide = send_ref.shape[0]
    per_device = C // group_size
    part = per_device * SUB
    columns = group_size * SUB
    half = per_device // 2

    def load(side, channel):
        parts = []
        for index in range(2):
            start = side * send_ref.shape[1] + index * part
            swap = windowed and index == 1 and channel >= half
            at = start + (channel - half if swap else channel) * SUB
            pair = recv_ref[:, at : at + 2 * SUB, :].astype(jnp.float32)
            if swap:
                pair = swap_halves(pair)
            parts.append([
                pair[:, low : low + SUB].reshape(columns, LANES).astype(jnp.bfloat16)
                for low in (0, SUB)
            ])
        return [jnp.concatenate([p[n] for p in parts], axis=1) for n in range(2)]

    def product(right, left):
        return lax.dot_general(
            right, left, (((0,), (0,)), ((), ())), preferred_element_type=jnp.float32
        )

    cut = 3 * BLOCK
    columns_first = lax.axis_index("wide") // group_size * columns
    column = columns_first + lax.broadcasted_iota(jnp.int32, (columns, 1), 0)
    sums = []
    for channel in range(0, per_device, 2):
        for left, right in zip(load(0, channel), load(1, channel)):
            if windowed:
                above = product(right, jnp.where(column < cut, left, 0))[:cut]
                below = product(right[:, LANES:], jnp.where(column < cut, 0, left))
                sums.append(jnp.concatenate([above, below[: wide * SUB - cut]], axis=0))
            else:
                sums.append(product(right, left))
    first = [s[:, :LANES] for s in sums]
    second = [s[:, LANES:] for s in sums]
    if windowed:
        second = [pack(second[c], second[c + half]) for c in range(half)]
    start = 0
    for channels in (first, second):
        for channel in range(0, len(channels), 2):
            pair = [channels[channel + n].reshape(wide, SUB, LANES) for n in range(2)]
            pair = jnp.concatenate(pair, axis=1).astype(jnp.bfloat16)
            send_ref[:, start : start + 2 * SUB, :] = pair
            start += 2 * SUB


def window_triangle_kernel(windowed, recv_ref, send_ref, edge):
    group_size = recv_ref.shape[0]
    wide = send_ref.shape[0]
    per_device = C // group_size
    part = per_device * SUB
    columns = group_size * SUB
    half = per_device // 2
    side_rows = send_ref.shape[1]
    for side in range(2):
        for index in range(2):
            height = min(part, side_rows - index * part)
            start = side * side_rows + index * part
            values = recv_ref[:, start : start + height, :].astype(jnp.float32)
            edge[side, index, : group_size * height, :] = values.reshape(group_size * height, LANES)

    def load(side, channel):
        parts = []
        for parity in range(2):
            rows = pl.ds(parity * SUB + channel, columns // 2, stride=2 * SUB)
            first = edge[side, 0, rows, :]
            if windowed:
                second = edge[side, 1, pl.ds(channel, columns // 2, stride=SUB), :]
                if parity:
                    second = swap_halves(second)
            else:
                second = edge[side, 1, rows, :]
            parts.append(jnp.concatenate([first, second], axis=1))
        return jnp.concatenate(parts, axis=0).astype(jnp.bfloat16)

    def product(right, left):
        return lax.dot_general(
            right, left, (((0,), (0,)), ((), ())), preferred_element_type=jnp.float32
        )

    cut = 3 * BLOCK
    columns_first = lax.axis_index("wide") // group_size * columns
    place = lax.broadcasted_iota(jnp.int32, (columns, 1), 0) % (columns // 2)
    column = columns_first + 2 * place
    sums = []
    for channel in range(per_device):
        left, right = load(0, channel), load(1, channel)
        if windowed:
            above = product(right, jnp.where(column < cut, left, 0))[:cut]
            below = product(right[:, LANES:], jnp.where(column < cut, 0, left))
            sums.append(jnp.concatenate([above, below[: wide * SUB - cut]], axis=0))
        else:
            sums.append(product(right, left))
    first = [s[:, :LANES] for s in sums]
    second = [s[:, LANES:] for s in sums]
    if windowed:
        second = [pack(second[c], second[c + half]) for c in range(half)]
    start = 0
    for channels in (first, second):
        for channel in range(0, len(channels), 2):
            pair = [channels[channel + n].reshape(wide, SUB, LANES) for n in range(2)]
            pair = jnp.concatenate(pair, axis=1).astype(jnp.bfloat16)
            send_ref[:, start : start + 2 * SUB, :] = pair
            start += 2 * SUB


def update_kernel(windowed, recv_ref, normed_ref, wg_ref, wo_ref, out_hbm, tri, out_ref, sems):
    group_size = recv_ref.shape[0] // PARTS
    part = C // group_size * SUB
    rows = 3 * BLOCK if windowed else normed_ref.shape[1]
    chunks = chunks_of(rows)
    first = window_start(windowed)
    copies = []
    if windowed:
        rest = out_hbm.shape[0] - rows * SUB
        to = pl.multiple_of(jnp.where(first == 0, rows, 0) * SUB, SUB)
        out_ref[pl.ds(rows * SUB, rest), :] = jnp.zeros((rest, C), jnp.float32)
        copies.append(
            pltpu.make_async_copy(
                out_ref.at[pl.ds(rows * SUB, rest)], out_hbm.at[pl.ds(to, rest)], sems.at[2]
            )
        )
        copies[0].start()
    for index, (low, count) in enumerate(chunks):
        height = part * count // LANES
        sums = [
            recv_ref[n * group_size : (n + 1) * group_size, index * part : index * part + height, :]
            for n in range(PARTS)
        ]
        sums = sum(values.astype(jnp.float32) for values in sums)
        if count < LANES:
            sums = jnp.concatenate([sums, swap_halves(sums)], axis=1)
        tri[index, : C * SUB, :] = layer_norm(sums.reshape(C, SUB, LANES), 0).reshape(C * SUB, LANES)
        for j in range(SUB):
            tri_normed = tri[index, pl.ds(j, C, stride=SUB), :].astype(jnp.bfloat16)
            mixed = lax.dot_general(
                tri_normed, wo_ref[...], (((0,), (0,)), ((), ())), preferred_element_type=jnp.float32
            )
            normed = normed_ref[j, low : low + count, :]
            gate = jax.nn.sigmoid(
                jnp.dot(normed, wg_ref[...], preferred_element_type=jnp.float32)
            )
            out_ref[pl.ds(low * SUB + j, count, stride=SUB), :] = gate * mixed[:count]
        to = pl.multiple_of((first + low) * SUB, SUB)
        copies.append(
            pltpu.make_async_copy(
                out_ref.at[pl.ds(low * SUB, count * SUB)],
                out_hbm.at[pl.ds(to, count * SUB)],
                sems.at[index],
            )
        )
        copies[-1].start()
    for copy in copies:
        copy.wait()


HBM = pl.BlockSpec(memory_space=pltpu.HBM)
VMEM = pl.BlockSpec(memory_space=pltpu.VMEM)
PARAMS = pltpu.CompilerParams(vmem_limit_bytes=48 * 1024 * 1024)


def in_hbm(array):
    return pltpu.with_memory_space_constraint(array, pltpu.HBM)


def exchange(array):
    wide, size = lax.axis_size("wide"), array.shape[0]
    groups = [list(range(first, first + size)) for first in range(0, wide, size)]
    return lax.all_to_all(
        array, "wide", split_axis=0, concat_axis=0, axis_index_groups=groups, tiled=True
    )


def after_projection(windowed, whole, window, normed, gate_weight, out_weight):
    send = window if windowed else whole
    group_size, both, _ = send.shape
    wide = group_size * PARTS
    tokens = normed.shape[1]
    back = pl.pallas_call(
        functools.partial(window_triangle_kernel if windowed else whole_triangle_kernel, windowed),
        out_shape=jax.ShapeDtypeStruct((wide, both // 2, LANES), jnp.bfloat16),
        in_specs=[VMEM],
        out_specs=VMEM,
        scratch_shapes=[pltpu.VMEM((2, 2, C * SUB + 2 * SUB, LANES), jnp.float32)] * windowed,
        compiler_params=PARAMS,
        name="triangle",
    )(exchange(send))
    return pl.pallas_call(
        functools.partial(update_kernel, windowed),
        out_shape=pltpu.HBM((tokens * SUB, C), jnp.float32),
        in_specs=[VMEM] * 4,
        out_specs=HBM,
        scratch_shapes=[
            pltpu.VMEM((2, C * SUB + SUB, LANES), jnp.float32),
            pltpu.VMEM((tokens * SUB + SUB, C), jnp.float32),
            pltpu.SemaphoreType.DMA((3,)),
        ],
        compiler_params=PARAMS,
        name="update",
    )(exchange(back), normed, gate_weight, out_weight)


def kernels_on_device(pair_act, block_mask, left_weight, right_weight, gate_weight, out_weight):
    tokens = pair_act.shape[0]
    wide = lax.axis_size("wide")
    group_size = wide // PARTS
    both = lambda rows: 2 * rows * (C // group_size) * SUB // LANES
    whole, window, normed, cut = pl.pallas_call(
        project_kernel,
        out_shape=(
            jax.ShapeDtypeStruct((group_size, both(tokens), LANES), jnp.bfloat16),
            jax.ShapeDtypeStruct((group_size, both(3 * BLOCK), LANES), jnp.bfloat16),
            jax.ShapeDtypeStruct((SUB, tokens, C), jnp.bfloat16),
            pltpu.SMEM((1,), jnp.int32),
        ),
        in_specs=[HBM] * 4,
        out_specs=(VMEM, VMEM, VMEM, pl.BlockSpec(memory_space=pltpu.SMEM)),
        scratch_shapes=[
            pltpu.SMEM(block_mask.shape, jnp.int32),
            pltpu.VMEM((tokens * SUB + SUB, C), jnp.float32),
            pltpu.VMEM((2, C, 2 * C), jnp.bfloat16),
            pltpu.VMEM((2, 2, C * SUB + SUB, LANES), jnp.float32),
            pltpu.SemaphoreType.DMA((5,)),
        ],
        compiler_params=PARAMS,
        name="project",
    )(
        in_hbm(block_mask),
        in_hbm(pair_act.reshape(tokens * SUB, C)),
        in_hbm(left_weight),
        in_hbm(right_weight),
    )
    update = lax.switch(
        cut[0],
        [functools.partial(after_projection, windowed) for windowed in (False, True)],
        whole,
        window,
        normed,
        gate_weight,
        out_weight,
    )
    return update.reshape(tokens, SUB, C)


def plain_on_device(pair_act, block_mask, left_weight, right_weight, gate_weight, out_weight):
    tile_rows = pair_act.shape[0]
    tile_cols = pair_act.shape[1]
    wide = lax.axis_size("wide")
    narrow = lax.axis_size("narrow")
    per_device = C // wide
    row_ids = lax.axis_index("narrow") * tile_rows + jnp.arange(tile_rows, dtype=jnp.int32)
    col_ids = lax.axis_index("wide") * tile_cols + jnp.arange(tile_cols, dtype=jnp.int32)
    block_ids = jnp.arange(block_mask.shape[0], dtype=jnp.int32)
    row_hot = (row_ids[:, None] // BLOCK == block_ids[None, :]).astype(jnp.float32)
    col_hot = (col_ids[:, None] // BLOCK == block_ids[None, :]).astype(jnp.float32)
    tile_mask = jnp.dot(jnp.dot(row_hot, block_mask.astype(jnp.float32)), col_hot.T).T
    normed = layer_norm(pair_act, -1).astype(jnp.bfloat16)

    def edges(weight):
        mixed = jnp.einsum("cd,ikc->dki", weight, normed, preferred_element_type=jnp.float32)
        proj = jax.nn.sigmoid(mixed[:C]) * mixed[C:] * tile_mask[None]
        return proj.astype(jnp.bfloat16).reshape(wide, per_device, tile_cols, tile_rows)

    send = jnp.stack([edges(left_weight), edges(right_weight)], axis=1)
    recv = lax.all_to_all(send, "wide", split_axis=0, concat_axis=0, tiled=True)
    left, right = recv[:, 0], recv[:, 1]
    if narrow > 1:
        right = lax.all_gather(right, "narrow", axis=3, tiled=True)
    tri = jnp.einsum("sckj,scki->cji", right, left, preferred_element_type=jnp.float32)
    back = tri.astype(jnp.bfloat16).reshape(per_device, wide, tile_cols, tile_rows)
    back = jnp.transpose(back, (1, 0, 2, 3))
    tri = lax.all_to_all(back, "wide", split_axis=0, concat_axis=0, tiled=True)
    tri = tri.reshape(C, tile_cols, tile_rows).astype(jnp.float32)
    tri_normed = layer_norm(tri, 0).astype(jnp.bfloat16)
    gate = jax.nn.sigmoid(
        jnp.einsum("ikc,cd->ikd", normed, gate_weight, preferred_element_type=jnp.float32)
    )
    return gate * jnp.einsum(
        "cji,cd->ijd", tri_normed, out_weight, preferred_element_type=jnp.float32
    )


def on_device(pair_act, block_mask, *weights):
    rows, cols = pair_act.shape[:2]
    blocks = block_mask.shape[0]
    fits = rows == 2 * LANES and cols == SUB and C // lax.axis_size("wide") == 4 and blocks == 4
    if lax.axis_size("narrow") > 1 or not fits:
        return plain_on_device(pair_act, block_mask, *weights)
    return kernels_on_device(pair_act, block_mask, *weights)


def solution(mesh):
    return jax.shard_map(
        on_device,
        mesh=mesh,
        in_specs=(P("narrow", "wide", None), P(), P(), P(), P(), P()),
        out_specs=P("narrow", "wide", None),
        check_vma=False,
    )
```
